32 devices in a mesh: dp: 4 (over y, core), ctx: 2 (over x), expert: 4 (over z).
Axes of the slice: x: 2, y: 2, z: 4, core: 2. Of those that a mesh axis runs over, the one named last changes fastest.
Arguments:
- tokens: bfloat16 [16, 1024, 512], P(('dp', 'expert'), 'ctx'), may hold values from -6 to 6
- cotangent: bfloat16 [16, 1024, 512], P(('dp', 'expert'), 'ctx'), may hold values from -6 to 6
- pad_mask: int32 [16, 1024], P(('dp', 'expert'), 'ctx'), may hold values from 0 to 1, as said below
- expert_ids: int32 [16, 1024, 2], P(('dp', 'expert'), 'ctx'), may hold values from 0 to 15, all different within a row
- slot_priority: int32 [16, 1024], P(('dp', 'expert'), 'ctx'), may hold values from 0 to 65535
- shared_slots: bfloat16 [4160, 512], P(('dp', 'ctx', 'expert')), may hold values from -1.5 to 1.5
- shared_first: float32 [4160, 512], P(('dp', 'ctx', 'expert')), may hold values from -1000 to 1000
- shared_second: float32 [4160, 512], P(('dp', 'ctx', 'expert')), may hold values from 0.1 to 200000
- shared_owner: int32 [2066], replicated, may hold values from 0 to 4159, as said below
- expert_slots: bfloat16 [4, 16384, 512], P('expert', ('dp', 'ctx')), may hold values from -5 to 5
- expert_first: float32 [4, 16384, 512], P('expert', ('dp', 'ctx')), may hold values from -1000 to 1000
- expert_second: float32 [4, 16384, 512], P('expert', ('dp', 'ctx')), may hold values from 0.01 to 200000
- expert_owner: int32 [4, 16384], P('expert'), may hold values from 0 to 16383, as said below
Outputs:
- block_out: bfloat16 [16, 1024, 512], P(('dp', 'expert'), 'ctx')
- tokens_grad: float32 [16, 1024, 512], P(('dp', 'expert'), 'ctx')
- shared_grad: float32 [4160, 512], P(('dp', 'ctx', 'expert'))
- shared_first_new: float32 [4160, 512], P(('dp', 'ctx', 'expert'))
- shared_second_new: float32 [4160, 512], P(('dp', 'ctx', 'expert'))
- shared_weight_new: float32 [4160, 512], P(('dp', 'ctx', 'expert'))
- expert_grad: float32 [4, 16384, 512], P('expert', ('dp', 'ctx'))
- expert_first_new: float32 [4, 16384, 512], P('expert', ('dp', 'ctx'))
- expert_second_new: float32 [4, 16384, 512], P('expert', ('dp', 'ctx'))
- expert_weight_new: float32 [4, 16384, 512], P('expert', ('dp', 'ctx'))
The draws below stay inside these ranges and needn't reach their ends.
Inputs may be any that keep to these rules, and one draw needn't show every extreme that they name: `pad_mask`: in each image the zeros are its last positions, 1 to 64 of them; some image has exactly 64 and some exactly one. `shared_owner`: distinct slots; the rows owned by a device lie in its own 130 slots, and some device has all 130 of them filled. Unnamed slots are not read. `expert_owner`: each row is a permutation of the 16384 slots: every device of an expert index owns exactly 2048 of its rows, in any order.
All inputs are finite; a program needn't handle non-finite values.
Results may differ from the reference program's by a relative error of at most 0.014.
Values may be sent and summed in bfloat16 or wider, within the bound.
No kernel may reach another device: no remote copies, remote signals or barrier semaphores. Data moves between devices by JAX's collectives and lax.ppermute only.
A program may use at most 192 MiB of HBM per device.

```python
import math
import jax
import jax.numpy as jnp
from jax import lax

D = 512
HEADS = 8
HEAD_DIM = 64
FF = 2048
TOP = 2
IMG_GRP = 1
SEQ_LEN = 1024
PART_LEN = 512
IMAGES = 16
EXPERTS = 16
EXP_SHARDS = 4
CAP = 80
PAD_MAX = 64
PIECES_A = 2066
HOLDERS_A = 32
OWN_A = 130
SLOTS_A = 4160
PIECES_B = 16384
HOLDERS_B = 8
OWN_B = 2048
SLOTS_B = 16384
N_CTX = 2


def owner_map(seed_key, pieces, holders, own_count):
    full_key, rest_key, pick_key = jax.random.split(seed_key, 3)
    full_holder = jax.random.randint(full_key, (), 0, holders).astype(jnp.int32)
    others = jax.random.permutation(rest_key, holders * own_count - own_count).astype(jnp.int32)
    others = jnp.where(others >= full_holder * own_count, others + own_count, others)
    filled_slots = full_holder * own_count + jnp.arange(own_count, dtype=jnp.int32)
    chosen_slots = jnp.concatenate([filled_slots, others])[:pieces]
    return chosen_slots[jax.random.permutation(pick_key, pieces)].astype(jnp.int32)


def shared_map(key):
    return owner_map(jax.random.fold_in(key, 11), PIECES_A, HOLDERS_A, OWN_A)


def expert_map(key, number):
    return owner_map(jax.random.fold_in(jax.random.fold_in(key, 22), number), PIECES_B, HOLDERS_B, OWN_B)


def shared_grad_scale(key):
    owner_rows = shared_map(key)
    rows = jnp.arange(PIECES_A)
    total_rows = float(IMAGES * SEQ_LEN) ** 0.5
    attn_scale = 1.4 * float(IMAGES) ** 0.5
    piece_scale = jnp.where(rows < 4 * D, attn_scale, jnp.where(rows < 4 * D + EXPERTS, 0.1 * total_rows, 0.3 * total_rows))
    return jnp.ones((SLOTS_A,), jnp.float32).at[owner_rows].set(piece_scale.astype(jnp.float32))


def expert_grad_scale():
    return 0.05 * float(2 * IMAGES * SEQ_LEN // EXPERTS) ** 0.5


def draw_shared_owner(key, part):
    return shared_map(key)


def draw_expert_owner(key, part):
    return jax.vmap(lambda number: expert_map(key, number))(jnp.arange(EXP_SHARDS))


def draw_shared_first(key, part):
    scale = shared_grad_scale(key)
    noise_key = jax.random.fold_in(key, 66)
    noise = jnp.clip(jax.random.normal(noise_key, (SLOTS_A, D), jnp.float32), -3.0, 3.0)
    return (noise * scale[:, None]).astype(jnp.float32)


def draw_shared_second(key, part):
    scale = shared_grad_scale(key)
    level_key, factor_key = jax.random.split(jax.random.fold_in(key, 77), 2)
    level = jnp.exp(jax.random.uniform(level_key, (SLOTS_A, 1), jnp.float32, minval=0.0, maxval=1.3863))
    factor = jnp.exp(jax.random.uniform(factor_key, (SLOTS_A, D), jnp.float32, minval=-0.6931, maxval=0.6931))
    return (level * factor * (scale * scale)[:, None]).astype(jnp.float32)


def draw_expert_first(key, part):
    noise_key = jax.random.fold_in(key, 88)
    noise = jnp.clip(jax.random.normal(noise_key, (EXP_SHARDS, SLOTS_B, D), jnp.float32), -3.0, 3.0)
    return (noise * expert_grad_scale()).astype(jnp.float32)


def draw_expert_second(key, part):
    level_key, factor_key = jax.random.split(jax.random.fold_in(key, 99), 2)
    level = jnp.exp(jax.random.uniform(level_key, (EXP_SHARDS, SLOTS_B, 1), jnp.float32, minval=0.0, maxval=1.3863))
    factor = jnp.exp(jax.random.uniform(factor_key, (EXP_SHARDS, SLOTS_B, D), jnp.float32, minval=-0.6931, maxval=0.6931))
    scale = expert_grad_scale()
    return (level * factor * (scale * scale)).astype(jnp.float32)


def draw_shared_slots(key, part):
    owner_rows = shared_map(key)
    normal_key, gain_key, empty_key = jax.random.split(jax.random.fold_in(key, 33), 3)
    rows = jnp.arange(PIECES_A)
    row_scale = jnp.where((rows >= 4 * D) & (rows < 4 * D + EXPERTS), 0.75 / D ** 0.5, (2.0 / D) ** 0.5)[:, None]
    matrix_vals = jnp.clip(jax.random.normal(normal_key, (PIECES_A, D), jnp.float32), -6.0, 6.0) * row_scale
    gain_vals = jax.random.uniform(gain_key, (PIECES_A, D), jnp.float32, minval=0.6, maxval=1.4)
    is_gain = (rows >= 4 * D + EXPERTS)[:, None]
    piece_vals = jnp.where(is_gain, gain_vals, matrix_vals)
    empty_vals = jnp.clip(jax.random.normal(empty_key, (SLOTS_A, D), jnp.float32), -6.0, 6.0) * (2.0 / D) ** 0.5
    return empty_vals.at[owner_rows].set(piece_vals).astype(jnp.bfloat16)


def expert_shard(key, number):
    owner_rows = expert_map(key, number)
    normal_key, empty_key = jax.random.split(jax.random.fold_in(jax.random.fold_in(key, 44), number), 2)
    second_rows = (jnp.arange(PIECES_B) // FF % 2 == 1)[:, None]
    row_scale = jnp.where(second_rows, 4.0 / FF ** 0.5, 1.0 / D ** 0.5)
    piece_vals = jnp.clip(jax.random.normal(normal_key, (PIECES_B, D), jnp.float32), -6.0, 6.0) * row_scale
    empty_vals = jnp.clip(jax.random.normal(empty_key, (SLOTS_B, D), jnp.float32), -6.0, 6.0) / D ** 0.5
    return empty_vals.at[owner_rows].set(piece_vals)


def draw_expert_slots(key, part):
    return jax.vmap(lambda number: expert_shard(key, number))(jnp.arange(EXP_SHARDS)).astype(jnp.bfloat16)


def draw_pad_mask(key, part):
    count_key, pick_key = jax.random.split(jax.random.fold_in(key, 55), 2)
    pads = jax.random.randint(count_key, (IMAGES,), 1, PAD_MAX + 1)
    picked = jax.random.randint(pick_key, (), 0, IMAGES)
    image_ids = jnp.arange(IMAGES)
    pads = jnp.where(image_ids == picked, PAD_MAX, pads)
    pads = jnp.where(image_ids == (picked + 1) % IMAGES, 1, pads)
    positions = jnp.arange(SEQ_LEN)
    return (positions[None, :] < SEQ_LEN - pads[:, None]).astype(jnp.int32)


def set_ends(array, rng, least, high):
    place = [jax.random.randint(jax.random.fold_in(rng, axis), (), 0, length) for axis, length in enumerate(array.shape)]
    main_axis = array.shape.index(max(array.shape))
    next_to = place[:main_axis] + [(place[main_axis] + 1) % array.shape[main_axis]] + place[main_axis + 1:]
    return array.at[tuple(place)].set(least).at[tuple(next_to)].set(high)


def block_scale(stream_key, extent, shards, smallest, largest):
    def one(axis_at, parts):
        steps = jax.random.uniform(jax.random.fold_in(jax.random.fold_in(stream_key, 6), axis_at), (parts,), jnp.float32, smallest / len(shards), largest / len(shards))
        return jnp.repeat(jnp.exp(steps), extent[axis_at] // parts).reshape((-1,) + (1,) * (len(extent) - axis_at - 1))

    level = one(*shards[0])
    for cut in shards[1:]:
        level = level * one(*cut)
    return level


def picks_of(rng, rows, number_of, top, lift):
    order = jax.random.permutation(jax.random.fold_in(rng, 1), number_of)
    pull = order
    for power in range(3):
        pull = pull * pull // number_of
    pull = pull * lift // number_of
    lots = jax.random.randint(jax.random.fold_in(rng, 2), (rows, number_of), 0, 4096) + pull
    fixed_rows = jax.random.permutation(jax.random.fold_in(rng, 3), rows)[jnp.arange(number_of) % rows]
    lots = jnp.where(jnp.arange(rows)[:, None] == fixed_rows[None, :], 1 << 14, lots)
    score = lots * number_of + jnp.arange(number_of)
    return lax.top_k(score.astype(jnp.int32), top)[1].astype(jnp.int32)


def normal_values(key, dims, width, reach, cuts=(), kind=jnp.bfloat16):
    entries = width * jax.random.normal(key, dims, jnp.float32)
    if cuts:
        entries = entries * block_scale(key, dims, cuts, -0.22, 0.18)
    return jnp.clip(entries, -reach, reach).astype(kind)


def setup_inputs(seed: int = 0) -> dict:
    seeds = jax.random.split(jax.random.key(seed), 14)
    return {
        "tokens": normal_values(seeds[0], (IMAGES, SEQ_LEN, D), 1.0, 6.0, ((0, 16), (1, 2))),
        "cotangent": normal_values(seeds[1], (IMAGES, SEQ_LEN, D), 1.0, 6.0, ((0, 16), (1, 2))),
        "pad_mask": draw_pad_mask(jax.random.fold_in(seeds[13], 71), 0),
        "expert_ids": picks_of(seeds[3], IMAGES * SEQ_LEN, EXPERTS, TOP, 1024).reshape((IMAGES, SEQ_LEN, TOP)),
        "slot_priority": set_ends(jax.random.randint(seeds[4], (IMAGES, SEQ_LEN), 0, 65536), jax.random.fold_in(seeds[4], 1), 0, 65535).astype(jnp.int32),
        "shared_slots": draw_shared_slots(jax.random.fold_in(seeds[13], 71), 0),
        "shared_first": draw_shared_first(jax.random.fold_in(seeds[13], 71), 0),
        "shared_second": draw_shared_second(jax.random.fold_in(seeds[13], 71), 0),
        "shared_owner": draw_shared_owner(jax.random.fold_in(seeds[13], 71), 0),
        "expert_slots": draw_expert_slots(jax.random.fold_in(seeds[13], 71), 0),
        "expert_first": draw_expert_first(jax.random.fold_in(seeds[13], 71), 0),
        "expert_second": draw_expert_second(jax.random.fold_in(seeds[13], 71), 0),
        "expert_owner": draw_expert_owner(jax.random.fold_in(seeds[13], 71), 0),
    }


PRECISE = lax.Precision.HIGHEST
MASKED_SCORE = -1e+30
MOMENT_DECAY = 0.5
LEARN_RATE = 0.05
WEIGHT_DECAY = 0.1
EPSILON = 1e-08
NORM_EPSILON = 1e-06

@jax.custom_vjp
def low(v):
    return lax.optimization_barrier(v.astype(jnp.bfloat16)).astype(jnp.float32)

@jax.custom_vjp
def low_back(v):
    return v

def low_keep(v):
    return (low(v), None)

def low_pass(kept, grad):
    return (grad,)

def back_keep(v):
    return (v, None)

def back_low(kept, grad):
    return (low(grad),)
low.defvjp(low_keep, low_pass)
low_back.defvjp(back_keep, back_low)

def layer_norm(values, gain_rows):
    center = values - lax.optimization_barrier(jnp.mean(values, axis=-1, keepdims=True))
    spread = lax.optimization_barrier(jnp.mean(center * center, axis=-1, keepdims=True))
    return center * lax.rsqrt(spread + NORM_EPSILON) * gain_rows

def to_devices(member):
    groups = IMAGES // IMG_GRP
    tail = member.shape[2:]
    shaped = member.reshape((groups, IMG_GRP, N_CTX, PART_LEN) + tail)
    shaped = jnp.moveaxis(shaped, 2, 1)
    return shaped.reshape((groups * N_CTX, IMG_GRP * PART_LEN) + tail)

def from_devices(member):
    groups = IMAGES // IMG_GRP
    tail = member.shape[2:]
    shaped = member.reshape((groups, N_CTX, IMG_GRP, PART_LEN) + tail)
    shaped = jnp.moveaxis(shaped, 1, 2)
    return shaped.reshape((IMAGES, SEQ_LEN) + tail)

def routing(chosen, priority, live_rows, expert_count, capacity):
    tok_count = chosen.shape[0]
    token_ids = jnp.arange(tok_count, dtype=jnp.int32)
    ranking = jnp.argsort(priority * tok_count + token_ids).astype(jnp.int32)
    labels = jnp.arange(expert_count, dtype=jnp.int32)
    wanted = jnp.any(chosen[:, :, None] == labels[None, None, :], axis=1) & (live_rows[:, None] == 1)
    wanted = wanted.astype(jnp.int32)
    ranked = wanted[ranking]
    before = (jnp.cumsum(ranked, axis=0) - ranked).astype(jnp.int32)
    position = jnp.zeros_like(before).at[ranking].set(before)
    slot_taken = jnp.take_along_axis(position, chosen, axis=1)
    kept_pair = (slot_taken < capacity) & (live_rows[:, None] == 1)
    target = jnp.where(kept_pair, chosen * capacity + slot_taken, expert_count * capacity).astype(jnp.int32)
    owners = jnp.broadcast_to(token_ids[:, None], chosen.shape)
    source = jnp.zeros((expert_count * capacity,), jnp.int32).at[target.reshape(-1)].set(owners.reshape(-1), mode='drop')
    filled = jnp.zeros((expert_count * capacity,), jnp.int32).at[target.reshape(-1)].set(1, mode='drop')
    slot_index = jnp.where(kept_pair, chosen * capacity + slot_taken, 0).astype(jnp.int32)
    return (slot_index, kept_pair.astype(jnp.int32), source, filled)

def attend_rows(query_rows, key_rows, value_rows, keep_mask):
    score = jnp.einsum('qhd,khd->hqk', query_rows, key_rows, precision=PRECISE) * HEAD_DIM ** (-0.5)
    score = low_back(score)
    score = jnp.where(keep_mask[None, None, :] > 0, score, MASKED_SCORE)
    row_max = lax.optimization_barrier(jnp.max(score, axis=-1, keepdims=True))
    row_sum = lax.optimization_barrier(jnp.sum(jnp.exp(score - row_max) * keep_mask, axis=-1, keepdims=True))
    attn_prob = jnp.exp(score - (row_max + jnp.log(row_sum))) * keep_mask
    return jnp.einsum('hqk,khd->qhd', low(attn_prob), value_rows, precision=PRECISE)

def attend_image(inputs):
    qkv_rows, keep_mask = inputs
    split_heads = qkv_rows.reshape(SEQ_LEN, 3, HEADS, HEAD_DIM)
    queries = split_heads[:, 0]
    key_rows = split_heads[:, 1]
    value_rows = split_heads[:, 2]
    row_block = math.gcd(SEQ_LEN, 1024)
    query_blocks = queries.reshape(SEQ_LEN // row_block, row_block, HEADS, HEAD_DIM)
    attend_step = jax.checkpoint(lambda block_rows: attend_rows(block_rows, key_rows, value_rows, keep_mask))
    return lax.map(attend_step, query_blocks).reshape(SEQ_LEN, HEADS * HEAD_DIM)

def expert_device(inputs, w_in, w_out):
    normed, router_prob, slot_index, kept_pair, source, filled, chosen = inputs
    dispatched = low_back(normed[source] * filled[:, None].astype(jnp.float32)).reshape(EXPERTS, CAP, D)
    hidden = low_back(jnp.einsum('ecd,efd->ecf', dispatched, w_in, precision=PRECISE))
    active = low(jax.nn.gelu(hidden, approximate=False))
    result = low_back(low(jnp.einsum('ecf,efd->ecd', active, w_out, precision=PRECISE))).reshape(EXPERTS * CAP, D)
    gate_value = jnp.take_along_axis(router_prob, chosen, axis=1) * kept_pair.astype(jnp.float32)
    return lax.optimization_barrier(jnp.sum(gate_value[:, :, None] * result[slot_index], axis=1))

def forward(shared, experts, tokens, keep_mask, routes):
    w_qkv = shared[:3 * D]
    w_attn_out = shared[3 * D:4 * D]
    w_router = shared[4 * D:4 * D + EXPERTS]
    gain_one = shared[4 * D + EXPERTS]
    gain_two = shared[4 * D + EXPERTS + 1]
    normed_one = low(layer_norm(tokens, gain_one))
    qkv_rows = low_back(low(jnp.einsum('std,ed->ste', normed_one, w_qkv, precision=PRECISE)))
    attended = lax.map(attend_image, (qkv_rows, keep_mask))
    attended = low_back(low(attended))
    branch = low_back(jnp.einsum('std,de->ste', attended, w_attn_out, precision=PRECISE))
    residual = tokens + branch
    normed_two = low(layer_norm(residual, gain_two))
    logits = low_back(jnp.einsum('std,ed->ste', normed_two, w_router, precision=PRECISE))
    router_prob = jax.nn.softmax(logits, axis=-1)
    weights = experts.reshape(EXPERTS, 2, FF, D)
    moe_step = jax.checkpoint(lambda inputs: expert_device(inputs, weights[:, 0], weights[:, 1]))
    mixture = lax.map(moe_step, (to_devices(normed_two), to_devices(router_prob)) + routes)
    return residual + from_devices(mixture)

def adam_update(gradient, first_old, second_old, weight):
    first_new = MOMENT_DECAY * first_old + (1.0 - MOMENT_DECAY) * gradient
    second_new = MOMENT_DECAY * second_old + (1.0 - MOMENT_DECAY) * gradient * gradient
    weight_new = weight - LEARN_RATE * (first_new / (jnp.sqrt(second_new) + EPSILON) + WEIGHT_DECAY * weight)
    return (first_new, second_new, weight_new)

def reference(tokens, cotangent, pad_mask, expert_ids, slot_priority, shared_slots, shared_first, shared_second, shared_owner, expert_slots, expert_first, expert_second, expert_owner):
    keep_mask = pad_mask.astype(jnp.float32)
    routed = jax.vmap(lambda chosen, priority, live_rows: routing(chosen, priority, live_rows, EXPERTS, CAP))(to_devices(expert_ids), to_devices(slot_priority), to_devices(pad_mask))
    routes = tuple(routed) + (to_devices(expert_ids),)
    shared = shared_slots[shared_owner].astype(jnp.float32)
    experts = jax.vmap(lambda slot_rows, owner_rows: slot_rows[owner_rows])(expert_slots, expert_owner).astype(jnp.float32)
    inputs = tokens.astype(jnp.float32)
    output, pull_back = jax.vjp(lambda shared_in, expert_in, token_in: forward(shared_in, expert_in, token_in, keep_mask, routes), shared, experts, inputs)
    grad_shared, grad_experts, grad_tokens = pull_back(cotangent.astype(jnp.float32) * keep_mask[:, :, None])
    slot_shared = jnp.zeros(shared_slots.shape, jnp.float32).at[shared_owner].set(grad_shared)
    slot_experts = jax.vmap(lambda owner_rows, values: jnp.zeros(expert_slots.shape[1:], jnp.float32).at[owner_rows].set(values))(expert_owner, grad_experts)
    first_shared, second_shared, weight_shared = adam_update(slot_shared, shared_first, shared_second, shared_slots.astype(jnp.float32))
    first_experts, second_experts, weight_experts = adam_update(slot_experts, expert_first, expert_second, expert_slots.astype(jnp.float32))
    return (output.astype(jnp.bfloat16), grad_tokens, slot_shared, first_shared, second_shared, weight_shared, slot_experts, first_experts, second_experts, weight_experts)
```

```python
import functools
import math

import jax
import jax.numpy as jnp
from jax import lax
from jax.experimental import pallas as pl
from jax.experimental.pallas import tpu as pltpu
from jax.sharding import PartitionSpec as P

HEADS = 8
HEAD_DIM = 64
FF = 2048
EXP_DEV = 4


MASKED_SCORE = -1e30
MOMENT_DECAY = 0.5
LEARN_RATE = 0.05
WEIGHT_DECAY = 0.1
EPSILON = 1e-08
NORM_EPSILON = 1e-06


def layer_norm(values, gain_rows):
    center = values - jnp.mean(values, axis=-1, keepdims=True)
    spread = jnp.mean(center * center, axis=-1, keepdims=True)
    return center * lax.rsqrt(spread + NORM_EPSILON) * gain_rows


def routing(chosen, priority, live_rows, expert_count, capacity):
    tok_count = chosen.shape[0]
    token_ids = jnp.arange(tok_count, dtype=jnp.int32)
    ranking = jnp.argsort(priority * tok_count + token_ids)
    labels = jnp.arange(expert_count, dtype=jnp.int32)
    wanted = jnp.any(chosen[:, :, None] == labels[None, None, :], axis=1) & (
        live_rows[:, None] == 1
    )
    wanted = wanted.astype(jnp.int32)
    ranked = wanted[ranking]
    before = jnp.cumsum(ranked, axis=0) - ranked
    position = jnp.zeros_like(before).at[ranking].set(before)
    slot_taken = jnp.take_along_axis(position, chosen, axis=1)
    kept_pair = (slot_taken < capacity) & (live_rows[:, None] == 1)
    target = jnp.where(kept_pair, chosen * capacity + slot_taken, expert_count * capacity)
    owners = jnp.broadcast_to(token_ids[:, None], chosen.shape)
    source = (
        jnp.zeros((expert_count * capacity,), jnp.int32)
        .at[target.reshape(-1)]
        .set(owners.reshape(-1), mode="drop")
    )
    filled = (
        jnp.zeros((expert_count * capacity,), jnp.int32).at[target.reshape(-1)].set(1, mode="drop")
    )
    slot_index = jnp.where(kept_pair, chosen * capacity + slot_taken, 0)
    return (slot_index, kept_pair.astype(jnp.int32), source, filled)


def head_view(values):
    return values.reshape(values.shape[0], values.shape[1], HEADS, HEAD_DIM)


def score_block(queries, key_rows, keep_mask):
    score = jnp.einsum(
        "iqhe,ikhe->ihqk", queries, head_view(key_rows), preferred_element_type=jnp.float32
    ) * HEAD_DIM ** (-0.5)
    return jnp.where(keep_mask[:, None, None, :] > 0, score, MASKED_SCORE)


def stats_step(running, portion, queries):
    row_max, row_sum = running
    key_rows, keep_mask = portion
    score = score_block(queries, key_rows, keep_mask)
    keep_wide = keep_mask.astype(jnp.float32)[:, None, None, :]
    new_max = jnp.maximum(row_max, jnp.max(score, axis=-1))
    row_sum = row_sum * jnp.exp(row_max - new_max) + jnp.sum(
        jnp.exp(score - new_max[..., None]) * keep_wide, axis=-1
    )
    return (new_max, row_sum)


def value_step(running, portion, queries, log_sum):
    key_rows, value_rows, keep_mask = portion
    score = score_block(queries, key_rows, keep_mask)
    keep_wide = keep_mask.astype(jnp.float32)[:, None, None, :]
    attn_prob = (jnp.exp(score - log_sum[..., None]) * keep_wide).astype(jnp.bfloat16)
    return running + jnp.einsum(
        "ihqk,ikhe->iqhe", attn_prob, head_view(value_rows), preferred_element_type=jnp.float32
    )


def grad_step(grad_query, portion, queries, log_sum, grad_out, row_delta):
    key_rows, value_rows, keep_mask = portion
    score = score_block(queries, key_rows, keep_mask)
    keep_wide = keep_mask.astype(jnp.float32)[:, None, None, :]
    attn_prob = jnp.exp(score - log_sum[..., None]) * keep_wide
    prob_low = attn_prob.astype(jnp.bfloat16)
    grad_value = jnp.einsum(
        "ihqk,iqhe->ikhe", prob_low, grad_out, preferred_element_type=jnp.float32
    )
    grad_prob = jnp.einsum(
        "iqhe,ikhe->ihqk", grad_out, head_view(value_rows), preferred_element_type=jnp.float32
    )
    grad_score = (attn_prob * (grad_prob - row_delta[..., None])).astype(jnp.bfloat16)
    score_scale = HEAD_DIM ** (-0.5)
    grad_query = (
        grad_query
        + jnp.einsum(
            "ihqk,ikhe->iqhe", grad_score, head_view(key_rows), preferred_element_type=jnp.float32
        )
        * score_scale
    )
    grad_key = (
        jnp.einsum("ihqk,iqhe->ikhe", grad_score, queries, preferred_element_type=jnp.float32)
        * score_scale
    )
    return (grad_query, jnp.stack([grad_key, grad_value]))


def each_block(step_fn, running, arrays, block_len):
    total_len = arrays[0].shape[1]
    size_rows = math.gcd(total_len, block_len)

    def one_turn(number, current):
        offset = number * size_rows
        portion = tuple(
            (lax.dynamic_slice_in_dim(member, offset, size_rows, 1) for member in arrays)
        )
        return step_fn(current, portion)

    return lax.fori_loop(0, total_len // size_rows, one_turn, running)


def adam_update(gradient, first_old, second_old, weight):
    first_new = MOMENT_DECAY * first_old + (1.0 - MOMENT_DECAY) * gradient
    second_new = MOMENT_DECAY * second_old + (1.0 - MOMENT_DECAY) * gradient * gradient
    weight_new = weight - LEARN_RATE * (
        first_new / (jnp.sqrt(second_new) + EPSILON) + WEIGHT_DECAY * weight
    )
    return (first_new, second_new, weight_new)


def on_device(
    tokens,
    cotangent,
    pad_mask,
    expert_ids,
    slot_priority,
    shared_slots,
    shared_first,
    shared_second,
    shared_owner,
    expert_slots,
    expert_first,
    expert_second,
    expert_owner,
):
    img_count, part_len, features = tokens.shape
    tok_count = img_count * part_len
    expert_count = EXP_DEV * lax.axis_size("expert")
    capacity = (10 * tok_count + 4 * expert_count - 1) // (4 * expert_count)
    all_shared = lax.all_gather(shared_slots, ("dp", "ctx", "expert"), axis=0, tiled=True)
    all_expert = lax.all_gather(expert_slots, ("dp", "ctx"), axis=1, tiled=True)
    pieces = all_shared[shared_owner]
    w_qkv = pieces[: 3 * features]
    w_attn_out = pieces[3 * features : 4 * features]
    w_router = pieces[4 * features : 4 * features + expert_count]
    gain_one = pieces[4 * features + expert_count].astype(jnp.float32)
    gain_two = pieces[4 * features + expert_count + 1].astype(jnp.float32)
    expert_rows = all_expert[0][expert_owner[0]].reshape(EXP_DEV, 2, FF, features)
    w_in = expert_rows[:, 0]
    w_out = expert_rows[:, 1]
    inputs = tokens.reshape(tok_count, features).astype(jnp.float32)
    keep_mask = pad_mask.astype(jnp.bfloat16)
    keep_rows = pad_mask.reshape(tok_count).astype(jnp.float32)
    normed_one, norm_one_back = jax.vjp(layer_norm, inputs, gain_one)
    normed_low = normed_one.astype(jnp.bfloat16)
    qkv_rows = lax.dot_general(
        normed_low, w_qkv, (((1,), (1,)), ((), ())), preferred_element_type=jnp.float32
    ).astype(jnp.bfloat16)
    query_rows = qkv_rows[:, :features].reshape(img_count, part_len, features)
    key_rows = qkv_rows[:, features : 2 * features].reshape(img_count, part_len, features)
    value_rows = qkv_rows[:, 2 * features :].reshape(img_count, part_len, features)
    queries = head_view(query_rows)
    start_max = jnp.full((img_count, HEADS, part_len), MASKED_SCORE, jnp.float32)
    start_sum = jnp.zeros((img_count, HEADS, part_len), jnp.float32)
    start_out = jnp.zeros((img_count, part_len, HEADS, HEAD_DIM), jnp.float32)
    whole_keys, whole_values, whole_keep = (
        lax.all_gather(key_rows, "ctx", axis=1, tiled=True),
        lax.all_gather(value_rows, "ctx", axis=1, tiled=True),
        lax.all_gather(keep_mask, "ctx", axis=1, tiled=True),
    )
    row_max, row_sum = each_block(
        lambda running, portion: stats_step(running, portion, queries),
        (start_max, start_sum),
        (whole_keys, whole_keep),
        part_len,
    )
    log_sum = row_max + jnp.log(row_sum)
    attended = each_block(
        lambda running, portion: value_step(running, portion, queries, log_sum),
        start_out,
        (whole_keys, whole_values, whole_keep),
        part_len,
    )
    attended_low = attended.reshape(tok_count, features).astype(jnp.bfloat16)
    branch = jnp.dot(attended_low, w_attn_out, preferred_element_type=jnp.float32)
    residual = inputs + branch
    normed_two, norm_two_back = jax.vjp(layer_norm, residual, gain_two)
    mixed_low = normed_two.astype(jnp.bfloat16)
    logits = lax.dot_general(
        mixed_low, w_router, (((1,), (1,)), ((), ())), preferred_element_type=jnp.float32
    )
    router_prob = jax.nn.softmax(logits, axis=-1)
    chosen = expert_ids.reshape(tok_count, 2)
    slot_index, kept_pair, source, filled = routing(
        chosen,
        slot_priority.reshape(tok_count),
        pad_mask.reshape(tok_count),
        expert_count,
        capacity,
    )
    filled_low = filled.astype(jnp.bfloat16)
    dispatched = (mixed_low[source] * filled_low[:, None]).reshape(expert_count, capacity, features)
    received = lax.all_to_all(dispatched, "expert", split_axis=0, concat_axis=1, tiled=True)
    hidden = jnp.einsum("ecd,efd->ecf", received, w_in, preferred_element_type=jnp.float32)
    active, gelu_back = jax.vjp(lambda pre_act: jax.nn.gelu(pre_act, approximate=False), hidden)
    active_low = active.astype(jnp.bfloat16)
    result = jnp.einsum(
        "ecf,efd->ecd", active_low, w_out, preferred_element_type=jnp.float32
    ).astype(jnp.bfloat16)
    returned = lax.all_to_all(result, "expert", split_axis=1, concat_axis=0, tiled=True).reshape(
        expert_count * capacity, features
    )
    kept_float = kept_pair.astype(jnp.float32)
    gate_value = jnp.take_along_axis(router_prob, chosen, axis=1) * kept_float
    picked = returned[slot_index].astype(jnp.float32)
    mixture = jnp.sum(gate_value[:, :, None] * picked, axis=1)
    output = (residual + mixture).astype(jnp.bfloat16).reshape(tokens.shape)
    grad_rows = cotangent.reshape(tok_count, features).astype(jnp.float32) * keep_rows[:, None]
    grad_gate = jnp.sum(grad_rows[:, None, :] * picked, axis=-1) * kept_float
    labels = jnp.arange(expert_count, dtype=jnp.int32)
    grad_prob = jnp.sum(
        (chosen[:, :, None] == labels[None, None, :]).astype(jnp.float32) * grad_gate[:, :, None],
        axis=1,
    )
    grad_logits = router_prob * (
        grad_prob - jnp.sum(grad_prob * router_prob, axis=-1, keepdims=True)
    )
    grad_logits_low = grad_logits.astype(jnp.bfloat16)
    slot_expert = jnp.arange(expert_count * capacity, dtype=jnp.int32) // capacity
    slot_gate = jnp.take_along_axis(router_prob[source], slot_expert[:, None], axis=1)[
        :, 0
    ] * filled.astype(jnp.float32)
    grad_result = (
        (grad_rows[source] * slot_gate[:, None])
        .astype(jnp.bfloat16)
        .reshape(expert_count, capacity, features)
    )
    grad_received = lax.all_to_all(grad_result, "expert", split_axis=0, concat_axis=1, tiled=True)
    grad_active = jnp.einsum(
        "ecd,efd->ecf", grad_received, w_out, preferred_element_type=jnp.float32
    )
    grad_hidden = gelu_back(grad_active)[0].astype(jnp.bfloat16)
    grad_w_out = jnp.einsum(
        "ecf,ecd->efd", active_low, grad_received, preferred_element_type=jnp.float32
    )
    grad_w_in = jnp.einsum(
        "ecf,ecd->efd", grad_hidden, received, preferred_element_type=jnp.float32
    )
    grad_sent = jnp.einsum(
        "ecf,efd->ecd", grad_hidden, w_in, preferred_element_type=jnp.float32
    ).astype(jnp.bfloat16)
    grad_back = lax.all_to_all(
        grad_sent, "expert", split_axis=1, concat_axis=0, tiled=True
    ).reshape(expert_count * capacity, features)
    grad_mixed = jnp.sum(grad_back[slot_index].astype(jnp.float32) * kept_float[:, :, None], axis=1)
    grad_mixed = grad_mixed + jnp.dot(grad_logits_low, w_router, preferred_element_type=jnp.float32)
    grad_router = lax.dot_general(
        grad_logits_low, mixed_low, (((0,), (0,)), ((), ())), preferred_element_type=jnp.float32
    )
    grad_residual_part, grad_gain_two = norm_two_back(grad_mixed)
    grad_residual = grad_rows + grad_residual_part
    grad_branch = grad_residual.astype(jnp.bfloat16)
    grad_w_attn_out = lax.dot_general(
        attended_low, grad_branch, (((0,), (0,)), ((), ())), preferred_element_type=jnp.float32
    )
    grad_attended = lax.dot_general(
        grad_branch, w_attn_out, (((1,), (1,)), ((), ())), preferred_element_type=jnp.float32
    ).astype(jnp.bfloat16)
    grad_out = head_view(grad_attended.reshape(img_count, part_len, features))
    row_delta = jnp.transpose(jnp.sum(grad_out.astype(jnp.float32) * attended, axis=-1), (0, 2, 1))
    start_grad = jnp.zeros((img_count, part_len, HEADS, HEAD_DIM), jnp.float32)
    whole_grads = jnp.zeros((2, img_count, whole_keys.shape[1], HEADS, HEAD_DIM), jnp.float32)

    def grad_turn(number, current):
        grad_query, grads_all = current
        offset = number * part_len
        portion = tuple(
            (
                lax.dynamic_slice_in_dim(member, offset, part_len, 1)
                for member in (whole_keys, whole_values, whole_keep)
            )
        )
        grad_query, grad_block = grad_step(
            grad_query, portion, queries, log_sum, grad_out, row_delta
        )
        grads_all = lax.dynamic_update_slice_in_dim(grads_all, grad_block, offset, 2)
        return (grad_query, grads_all)

    grad_query, whole_grads = lax.fori_loop(
        0, whole_keys.shape[1] // part_len, grad_turn, (start_grad, whole_grads)
    )
    grad_pair = lax.psum_scatter(whole_grads, "ctx", scatter_dimension=2, tiled=True)
    grad_qkv = jnp.concatenate(
        [
            grad_query.reshape(tok_count, features),
            grad_pair[0].reshape(tok_count, features),
            grad_pair[1].reshape(tok_count, features),
        ],
        axis=1,
    ).astype(jnp.bfloat16)
    grad_w_qkv = lax.dot_general(
        grad_qkv, normed_low, (((0,), (0,)), ((), ())), preferred_element_type=jnp.float32
    )
    grad_normed = jnp.dot(grad_qkv, w_qkv, preferred_element_type=jnp.float32)
    grad_input_part, grad_gain_one = norm_one_back(grad_normed)
    grad_tokens = (grad_residual + grad_input_part).reshape(tokens.shape)
    shared_pieces = jnp.concatenate(
        [grad_w_qkv, grad_w_attn_out, grad_router, grad_gain_one[None, :], grad_gain_two[None, :]],
        axis=0,
    )
    shared_layout = jnp.zeros(all_shared.shape, jnp.float32).at[shared_owner].set(shared_pieces)
    shared_grad = lax.psum_scatter(
        shared_layout, ("dp", "ctx", "expert"), scatter_dimension=0, tiled=True
    )
    expert_pieces = jnp.stack([grad_w_in, grad_w_out], axis=1).reshape(EXP_DEV * 2 * FF, features)
    expert_layout = (
        jnp.zeros(all_expert.shape, jnp.float32).at[0, expert_owner[0]].set(expert_pieces)
    )
    expert_grad = lax.psum_scatter(expert_layout, ("dp", "ctx"), scatter_dimension=1, tiled=True)
    shared_first_new, shared_second_new, shared_weight_new = adam_update(
        shared_grad, shared_first, shared_second, shared_slots.astype(jnp.float32)
    )
    expert_first_new, expert_second_new, expert_weight_new = adam_update(
        expert_grad, expert_first, expert_second, expert_slots.astype(jnp.float32)
    )
    return (
        output,
        grad_tokens,
        shared_grad,
        shared_first_new,
        shared_second_new,
        shared_weight_new,
        expert_grad,
        expert_first_new,
        expert_second_new,
        expert_weight_new,
    )


F32 = jnp.float32
BF16 = jnp.bfloat16
I32 = jnp.int32
LANES = 128
MASKED = -1e30
VMEM_LIMIT = 56 * 1024 * 1024


def dot_nn(left, right):
    return lax.dot_general(left, right, (((1,), (0,)), ((), ())), preferred_element_type=F32)


def dot_nt(left, right):
    return lax.dot_general(left, right, (((1,), (1,)), ((), ())), preferred_element_type=F32)


def dot_tn(left, right):
    return lax.dot_general(left, right, (((0,), (0,)), ((), ())), preferred_element_type=F32)


def iota(shape, dim):
    return lax.broadcasted_iota(I32, shape, dim)


def as_bf16(mask):
    return jnp.where(mask, 1.0, 0.0).astype(BF16)


def kernel_call(body, out_shape, scratch=(), grid=None, in_specs=None, out_specs=None, cost=None):
    extra = {}
    if grid is not None:
        extra = dict(grid=grid, in_specs=in_specs, out_specs=out_specs)
    flops, moved = cost if cost else (1e8, 1e6)
    return pl.pallas_call(
        body,
        out_shape=out_shape,
        scratch_shapes=list(scratch),
        compiler_params=pltpu.CompilerParams(vmem_limit_bytes=VMEM_LIMIT),
        cost_estimate=pl.CostEstimate(flops=int(flops), bytes_accessed=int(moved), transcendentals=0),
        **extra,
    )


def sds(shape, dtype):
    return jax.ShapeDtypeStruct(shape, dtype)


def route_body(n_exp, capacity, ids_ref, prio_ref, live_ref, cot_ref, row_ref, col_ref, sent_ref):
    toks = ids_ref.shape[1]
    half = capacity // 2
    prio_row = prio_ref[...]
    prio_col = jnp.transpose(jnp.broadcast_to(prio_row, (8, toks)))[:, :1]
    earlier = (prio_col < prio_row) | (
        (prio_col == prio_row) & (iota((toks, toks), 0) < iota((toks, toks), 1))
    )
    live = live_ref[...] > 0.0
    labels = iota((n_exp, toks), 0)
    first, second = ids_ref[0:1, :], ids_ref[1:2, :]
    wanted = ((labels == first) | (labels == second)) & live
    taken = dot_nn(as_bf16(wanted), as_bf16(earlier))
    places = []
    for chosen in (first, second):
        slot = jnp.sum(jnp.where(labels == chosen, taken, 0.0), axis=0, keepdims=True).astype(I32)
        kept = live & (slot < capacity)
        shard = chosen >> 2
        local = chosen & 3
        core = (slot >= half).astype(I32)
        target = ((((local >> 1) * 2 + core) * 2 + (local & 1)) * (n_exp // 4)) + shard
        places.append(jnp.where(kept, target * half + slot - core * half, -1))
    row_id = iota((8, toks), 0)
    rows = jnp.where(row_id == 0, places[0], jnp.where(row_id == 1, places[1], -1))
    row_ref[...] = rows
    col_ref[...] = jnp.transpose(rows.astype(F32)).astype(I32)
    slots = sent_ref.shape[0]
    spots = iota((slots, toks), 0)
    picks = as_bf16((spots == places[0]) | (spots == places[1]))
    sent_ref[...] = dot_nn(picks, cot_ref[...]).astype(BF16)


def unpack_body(base, n_pieces, pos_ref, *refs):
    pieces, rest = refs[:n_pieces], refs[n_pieces:]
    earlier = rest[0] if len(rest) == 3 else None
    out_ref, held = rest[-2], rest[-1]
    size = pieces[0].shape[0]
    for number, piece in enumerate(pieces):
        held[number * size : (number + 1) * size, :] = piece[...]
    total = size * n_pieces
    rows = out_ref.shape[0]

    def tile(start, count):
        spots = pos_ref[pl.ds(start, count), :] - base
        picks = as_bf16(spots == iota((count, total), 1))
        value = dot_nn(picks, held[...])
        if earlier is not None:
            value = value + earlier[pl.ds(start, count), :].astype(F32)
        out_ref[pl.ds(start, count), :] = value.astype(BF16)

    whole = rows // 256

    @pl.loop(0, whole)
    def _(number):
        tile(pl.multiple_of(number * 256, 256), 256)

    if rows % 256:
        tile(whole * 256, rows % 256)


def normalize(values):
    center = values - jnp.mean(values, axis=-1, keepdims=True)
    spread = jnp.mean(center * center, axis=-1, keepdims=True)
    scale = lax.rsqrt(spread + NORM_EPSILON)
    return center * scale, scale


def head_lanes(head, rows):
    return (iota((rows, LANES), 1) // HEAD_DIM) == head


def column_of(ref, start, count, lane):
    block = ref[pl.ds(start, count), :]
    return jnp.sum(jnp.where(iota(block.shape, 1) == lane, block, 0.0), axis=1, keepdims=True)


def row_of(ref, line):
    return ref[pl.ds(line, 1), :]


def forward_body(
    n_exp, own_ref, other_ref, keep_ref, w_ref, pos_ref,
    qkv_ref, normed_ref, attended_ref, residual_ref, prob_ref, sent_ref, lse_col_ref, lse_row_ref,
    mixed_ref,
):
    toks, width = own_ref.shape
    router = 4 * width
    gain_one = w_ref[router + n_exp : router + n_exp + 16, :].astype(F32)
    gain_two = gain_one[1:2, :]
    gain_one = gain_one[0:1, :]
    for part, ref in enumerate((own_ref, other_ref)):
        normed = normalize(ref[...].astype(F32))[0] * gain_one
        low = normed.astype(BF16)
        if part == 0:
            normed_ref[...] = low
        rows = pl.ds(part * toks, toks)
        for third in range(3):
            made = dot_nt(low, w_ref[third * width : (third + 1) * width, :]).astype(BF16)
            if third == 0:
                made = made * jnp.asarray(HEAD_DIM ** (-0.5), BF16)
            qkv_ref[rows, third * width : (third + 1) * width] = made
    keep = keep_ref[...] > 0.0
    step = 128
    lse_col_ref[...] = jnp.zeros_like(lse_col_ref)

    @pl.loop(0, HEADS // 2)
    def _(pair):
        at = pl.multiple_of(pair * LANES, LANES)
        keys = qkv_ref[:, pl.ds(pl.multiple_of(width + at, LANES), LANES)]
        values = qkv_ref[:, pl.ds(pl.multiple_of(2 * width + at, LANES), LANES)]

        @pl.loop(0, toks // step)
        def _(number):
            start = pl.multiple_of(number * step, step)
            queries = qkv_ref[pl.ds(start, step), pl.ds(at, LANES)]
            made = []
            logs = lse_col_ref[pl.ds(start, step), :]
            for head in range(2):
                mine = head_lanes(head, step)
                score = dot_nt(jnp.where(mine, queries, jnp.zeros_like(queries)), keys)
                score = jnp.where(keep, score, MASKED)
                top = jnp.max(score, axis=-1, keepdims=True)
                grown = jnp.exp(score - top)
                total = jnp.sum(grown, axis=-1, keepdims=True)
                log_sum = top + jnp.log(total)
                prob = (grown * (1.0 / total)).astype(BF16)
                made.append(dot_nn(prob, values))
                logs = jnp.where(iota(logs.shape, 1) == pair * 2 + head, log_sum, logs)
            lse_col_ref[pl.ds(start, step), :] = logs
            attended_ref[pl.ds(start, step), pl.ds(at, LANES)] = jnp.where(
                head_lanes(0, step), made[0], made[1]
            )

    lse_row_ref[...] = jnp.transpose(lse_col_ref[...])[:8, :]
    branch = dot_nn(attended_ref[...].astype(BF16), w_ref[3 * width : 4 * width, :])
    residual = own_ref[...].astype(F32) + branch
    residual_ref[...] = residual
    mixed = (normalize(residual)[0] * gain_two).astype(BF16)
    mixed_ref[...] = mixed
    logits = dot_nt(mixed, w_ref[router : router + n_exp, :])
    prob_ref[...] = jax.nn.softmax(logits, axis=-1)
    slots = sent_ref.shape[0]
    spots = iota((slots, toks), 0)
    picks = as_bf16((spots == pos_ref[0:1, :]) | (spots == pos_ref[1:2, :]))
    sent_ref[...] = dot_nn(picks, mixed).astype(BF16)


def gelu_parts(value):
    size = jnp.abs(value)
    share = 1.0 / (1.0 + (0.3275911 * 0.7071067811865476) * size)
    series = share * (
        0.254829592
        + share * (-0.284496736 + share * (1.421413741 + share * (-1.453152027 + share * 1.061405429)))
    )
    bell = jnp.exp(-0.5 * value * value)
    tail = 0.5 * series * bell
    below = jnp.where(value >= 0.0, 1.0 - tail, tail)
    return value * below, below + value * bell * 0.3989422804014327


def expert_body(
    n_exp, expert_ref, got_ref, cot_ref, w_in_ref, w_out_ref, router_ref,
    active_ref, hidden_ref, scaled_ref, result_ref, back_ref, router_grad_ref,
    prob, total, total_back,
):
    step = pl.program_id(0)
    expert = expert_ref[0]
    rows = got_ref.shape[0]
    labels = iota((rows, n_exp), 1)

    @pl.when(step == 0)
    def _():
        logits = dot_nt(got_ref[...], router_ref[...])
        share = jax.nn.softmax(logits, axis=-1)
        prob[...] = share
        gate = jnp.sum(jnp.where(labels == expert, share, 0.0), axis=-1, keepdims=True)
        scaled_ref[...] = (cot_ref[...].astype(F32) * gate).astype(BF16)
        total[...] = jnp.zeros_like(total)
        total_back[...] = jnp.zeros_like(total_back)

    tile = 256

    @pl.loop(0, rows // tile)
    def _(number):
        at = pl.ds(pl.multiple_of(number * tile, tile), tile)
        pre = dot_nt(got_ref[at, :], w_in_ref[...])
        active, slope = gelu_parts(pre)
        low = active.astype(BF16)
        active_ref[at, :] = low
        total[at, :] += dot_nn(low, w_out_ref[...])
        grad = (dot_nt(scaled_ref[at, :], w_out_ref[...]) * slope).astype(BF16)
        hidden_ref[at, :] = grad
        total_back[at, :] += dot_nn(grad, w_in_ref[...])

    @pl.when(step == pl.num_programs(0) - 1)
    def _():
        result = total[...].astype(BF16)
        result_ref[...] = result
        inner = jnp.sum(result.astype(F32) * cot_ref[...].astype(F32), axis=-1, keepdims=True)
        share = prob[...]
        mine = labels == expert
        gate = jnp.sum(jnp.where(mine, share, 0.0), axis=-1, keepdims=True)
        grad = share * (jnp.where(mine, inner, 0.0) - gate * inner)
        low = grad.astype(BF16)
        back_ref[...] = (total_back[...] + dot_nn(low, router_ref[...])).astype(BF16)
        router_grad_ref[...] = dot_tn(low, got_ref[...])


def norm_back(hat, scale, gain, grad):
    inner = grad * gain
    first = jnp.mean(inner, axis=-1, keepdims=True)
    second = jnp.mean(inner * hat, axis=-1, keepdims=True)
    return (inner - first - hat * second) * scale


def middle_body(
    n_exp, back_ref, pos_ref, residual_ref, cot_ref, keep_ref, attended_ref, w_ref,
    grad_ref, out_grad_ref, delta_col_ref, delta_row_ref, gain_ref,
):
    toks, width = residual_ref.shape
    router = 4 * width
    slots = back_ref.shape[0]
    gain_two = w_ref[router + n_exp : router + n_exp + 16, :].astype(F32)[1:2, :]
    spots = iota((toks, slots), 1)
    picks = as_bf16((spots == pos_ref[:, 0:1]) | (spots == pos_ref[:, 1:2]))
    grad_mixed = dot_nn(picks, back_ref[...])
    hat, scale = normalize(residual_ref[...])
    gain_ref[...] = jnp.broadcast_to(
        jnp.sum(grad_mixed * hat, axis=0, keepdims=True), gain_ref.shape
    )
    grad_rows = cot_ref[...].astype(F32) * keep_ref[...]
    grad = grad_rows + norm_back(hat, scale, gain_two, grad_mixed)
    grad_ref[...] = grad
    low = grad.astype(BF16)
    out_grad = dot_nt(low, w_ref[3 * width : 4 * width, :]).astype(BF16)
    out_grad_ref[...] = out_grad
    product = out_grad.astype(F32) * attended_ref[...]
    delta = jnp.zeros((toks, LANES), F32)
    lane = iota((toks, LANES), 1)
    for head in range(HEADS):
        at = (head // 2) * LANES
        part = jnp.where(head_lanes(head % 2, toks), product[:, at : at + LANES], 0.0)
        delta = jnp.where(lane == head, jnp.sum(part, axis=-1, keepdims=True), delta)
    delta_col_ref[...] = delta
    delta_row_ref[...] = jnp.transpose(delta)[:8, :]


def key_grads(qkv_ref, base, toks, width, out_grad_ref, lse_ref, delta_ref, keep_ref, store):
    step = 128

    @pl.loop(0, HEADS // 2)
    def _(pair):
        at = pl.multiple_of(pair * LANES, LANES)
        queries = qkv_ref[pl.ds(base, toks), pl.ds(at, LANES)]
        out_grad = out_grad_ref[:, pl.ds(at, LANES)]

        @pl.loop(0, toks // step)
        def _(number):
            start = pl.multiple_of(number * step, step)
            rows = pl.ds(start, step)
            keys = qkv_ref[rows, pl.ds(pl.multiple_of(width + at, LANES), LANES)]
            values = qkv_ref[rows, pl.ds(pl.multiple_of(2 * width + at, LANES), LANES)]
            live = keep_ref[rows, :] > 0.0
            made = []
            for head in range(2):
                mine = head_lanes(head, step)
                score = dot_nt(jnp.where(mine, keys, jnp.zeros_like(keys)), queries)
                score = jnp.where(live, score, MASKED)
                prob = jnp.exp(score - row_of(lse_ref, pair * 2 + head))
                slope = dot_nt(jnp.where(mine, values, jnp.zeros_like(values)), out_grad)
                grad = (prob * (slope - row_of(delta_ref, pair * 2 + head))).astype(BF16)
                made.append((dot_nn(grad, queries), dot_nn(prob.astype(BF16), out_grad)))
            first = head_lanes(0, step)
            store(rows, at, jnp.where(first, made[0][0], made[1][0]), jnp.where(first, made[0][1], made[1][1]))


def inner_body(
    n_exp, spread, qkv_ref, out_grad_ref, lse_col_ref, lse_row_ref, delta_col_ref, delta_row_ref,
    keep_row_ref, keep_col_ref, attended_ref, grad_ref, router_grad_ref, gain_ref, pos_ref,
    query_ref, kv_ref, early_ref, late,
):
    toks, width = out_grad_ref.shape
    step = 128
    keep = keep_row_ref[...] > 0.0

    @pl.loop(0, HEADS // 2)
    def _(pair):
        at = pl.multiple_of(pair * LANES, LANES)
        keys = qkv_ref[:, pl.ds(pl.multiple_of(width + at, LANES), LANES)]
        values = qkv_ref[:, pl.ds(pl.multiple_of(2 * width + at, LANES), LANES)]

        @pl.loop(0, toks // step)
        def _(number):
            start = pl.multiple_of(number * step, step)
            rows = pl.ds(start, step)
            queries = qkv_ref[rows, pl.ds(at, LANES)]
            out_grad = out_grad_ref[rows, pl.ds(at, LANES)]
            made = []
            for head in range(2):
                mine = head_lanes(head, step)
                score = dot_nt(jnp.where(mine, queries, jnp.zeros_like(queries)), keys)
                score = jnp.where(keep, score, MASKED)
                prob = jnp.exp(score - column_of(lse_col_ref, start, step, pair * 2 + head))
                slope = dot_nt(jnp.where(mine, out_grad, jnp.zeros_like(out_grad)), values)
                delta = column_of(delta_col_ref, start, step, pair * 2 + head)
                grad = (prob * (slope - delta)).astype(BF16)
                made.append(dot_nn(grad, keys))
            joined = jnp.where(head_lanes(0, step), made[0], made[1]) * HEAD_DIM ** (-0.5)
            query_ref[rows, pl.ds(at, LANES)] = joined.astype(BF16)

    def store(rows, at, key_grad, value_grad):
        kv_ref[0, rows, pl.ds(at, LANES)] = key_grad
        kv_ref[1, rows, pl.ds(at, LANES)] = value_grad

    key_grads(qkv_ref, 0, toks, width, out_grad_ref, lse_row_ref, delta_row_ref, keep_col_ref, store)
    late[0:width, :] = dot_tn(attended_ref[...].astype(BF16), grad_ref[...].astype(BF16)).astype(BF16)
    late[width : width + n_exp, :] = router_grad_ref[...].astype(BF16)
    row_id = iota((16, width), 0)
    late[width + n_exp : width + n_exp + 16, :] = jnp.where(
        row_id == 1, gain_ref[0:1, :], 0.0
    ).astype(BF16)
    count = late.shape[0]
    picks_at = pos_ref[:, 3 * width : 3 * width + count]
    tile = 272

    @pl.loop(0, early_ref.shape[0] // tile)
    def _(number):
        start = pl.multiple_of(number * tile, tile)
        picks = as_bf16(iota((tile, count), 0) + start == picks_at)
        early_ref[pl.ds(start, tile), :] = dot_nn(picks, late[...]).astype(BF16)


def outer_body(
    n_exp, qkv_ref, out_grad_ref, lse_ref, delta_ref, keep_col_ref, query_ref, kv_ref,
    normed_ref, own_ref, w_ref, grad_ref, pos_ref, early_ref,
    tokens_ref, pieces_ref, sent_ref, held,
):
    toks, width = query_ref.shape
    held[:, 0:width] = query_ref[...]

    def store(rows, at, key_grad, value_grad):
        key_grad = kv_ref[0, rows, pl.ds(at, LANES)] + key_grad
        value_grad = kv_ref[1, rows, pl.ds(at, LANES)] + value_grad
        held[rows, pl.ds(pl.multiple_of(width + at, LANES), LANES)] = key_grad.astype(BF16)
        held[rows, pl.ds(pl.multiple_of(2 * width + at, LANES), LANES)] = value_grad.astype(BF16)

    key_grads(qkv_ref, toks, toks, width, out_grad_ref, lse_ref, delta_ref, keep_col_ref, store)
    router = 4 * width
    gain_one = w_ref[router + n_exp : router + n_exp + 16, :].astype(F32)[0:1, :]
    grad_normed = dot_nn(held[...], w_ref[0 : 3 * width, :])
    hat, scale = normalize(own_ref[...].astype(F32))
    tokens_ref[...] = grad_ref[...] + norm_back(hat, scale, gain_one, grad_normed)
    gain_grad = jnp.sum(grad_normed * hat, axis=0, keepdims=True)
    for third in range(3):
        pieces_ref[third * width : (third + 1) * width, :] = dot_tn(
            held[:, third * width : (third + 1) * width], normed_ref[...]
        ).astype(BF16)
    row_id = iota((16, width), 0)
    pieces_ref[3 * width : 3 * width + 16, :] = jnp.where(row_id == 0, gain_grad, 0.0).astype(BF16)
    spread_rows(pos_ref, pieces_ref, early_ref, sent_ref, early_ref.shape[0] // 2, width, n_exp)


def spread_rows(pos_ref, pieces_ref, early_ref, out_ref, base, width, n_exp):
    count = pieces_ref.shape[0]
    tile = 272
    gain_at = 4 * width + n_exp
    main_at = pos_ref[:, 0 : 3 * width]
    one_at = pos_ref[:, gain_at : gain_at + 1]

    @pl.loop(0, out_ref.shape[0] // tile)
    def _(number):
        start = pl.multiple_of(number * tile, tile)
        spots = iota((tile, 3 * width), 0) + (start + base)
        made = dot_nn(as_bf16(spots == main_at), pieces_ref[0 : 3 * width, :])
        gain = pieces_ref[3 * width : 3 * width + 16, :].astype(F32)[0:1, :]
        made = made + jnp.where(iota((tile, width), 0) + (start + base) == one_at, gain, 0.0)
        early = early_ref[pl.ds(pl.multiple_of(start + base, 16), tile), :].astype(F32)
        out_ref[pl.ds(start, tile), :] = (made + early).astype(BF16)


def spread_body(width, n_exp, pos_ref, pieces_ref, early_ref, out_ref):
    spread_rows(pos_ref, pieces_ref, early_ref, out_ref, 0, width, n_exp)


def mixture_body(result_ref, pos_ref, ids_ref, prob_ref, residual_ref, out_ref):
    toks = residual_ref.shape[0]
    slots = result_ref.shape[0]
    share = prob_ref[...]
    total = residual_ref[...]
    for number in range(2):
        picks = as_bf16(iota((toks, slots), 1) == pos_ref[:, number : number + 1])
        mine = iota(share.shape, 1) == ids_ref[:, number : number + 1]
        gate = jnp.sum(jnp.where(mine, share, 0.0), axis=-1, keepdims=True)
        total = total + gate * dot_nn(picks, result_ref[...])
    out_ref[...] = total.astype(BF16)


SWAP = [(0, 1), (1, 0)]
SWAP_CORE = [(0, 1), (1, 0), (2, 3), (3, 2)]
SWAP_Y = [(0, 2), (2, 0), (1, 3), (3, 1)]


def swap_x(value):
    return lax.ppermute(value, "ctx", SWAP)


def swap_y(value):
    return lax.ppermute(value, "dp", SWAP_Y)


def swap_core(value):
    return lax.ppermute(value, "dp", SWAP_CORE)


def shift_z(value, by):
    count = lax.axis_size("expert")
    return lax.ppermute(value, "expert", [(i, (i + by) % count) for i in range(count)])


def total_f32(first, second):
    return first.astype(F32) + second.astype(F32)


def on_chip_experts(
    tokens, cotangent, pad_mask, expert_ids, slot_priority, shared_slots, shared_first, shared_second,
    shared_owner, expert_slots, expert_first, expert_second, expert_owner,
):
    toks, width = tokens.shape[1], tokens.shape[2]
    n_z = lax.axis_size("expert")
    n_exp = EXP_DEV * n_z
    capacity = (10 * toks + 4 * n_exp - 1) // (4 * n_exp)
    slots = n_exp * capacity
    everyone = ("dp", "ctx", "expert")
    dp, mx, mz = lax.axis_index("dp"), lax.axis_index("ctx"), lax.axis_index("expert")
    my, mc = dp // 2, dp % 2

    own_count = shared_slots.shape[0]
    stride = -(-own_count // 8) * 8
    padded = jnp.pad(shared_slots, ((0, stride - own_count), (0, 0)))
    line = [padded] + [shift_z(padded, by) for by in range(1, n_z)]
    part_a = jnp.concatenate(line[: n_z // 2], axis=0)
    part_b = jnp.concatenate(line[n_z // 2 :], axis=0)
    a_y, b_x = swap_y(part_a), swap_x(part_b)
    a_x, b_y = swap_x(part_a), swap_y(part_b)
    a_yx, b_xy = swap_x(a_y), swap_y(b_x)
    near = [part_a, a_y, a_x, a_yx, part_b, b_x, b_y, b_xy]
    far = [swap_core(piece) for piece in near]

    owner_dev, owner_row = shared_owner // own_count, shared_owner % own_count
    o_z, o_x, o_dp = owner_dev % n_z, owner_dev // n_z % 2, owner_dev // (n_z * 2)
    in_c, in_y, in_x = (o_dp % 2) ^ mc, (o_dp // 2) ^ my, o_x ^ mx
    in_z = (mz - o_z + n_z) % n_z
    late = in_z // (n_z // 2)
    cross = jnp.where(late == 0, in_y + 2 * in_x, in_x + 2 * in_y)
    place = (((in_c * 2 + late) * 4 + cross) * (n_z // 2) + in_z % (n_z // 2)) * stride + owner_row
    total_slots = 8 * n_z * stride
    row_count = -(-shared_owner.shape[0] // 16) * 16
    wide_count = -(-shared_owner.shape[0] // LANES) * LANES
    place_col = jnp.pad(place, (0, row_count - place.shape[0]), constant_values=-1)[:, None]
    place_row = jnp.pad(place, (0, wide_count - place.shape[0]), constant_values=-1)[None, :]

    own, other = tokens[0], swap_x(tokens[0])
    ids = expert_ids[0]
    live = pad_mask.astype(F32)
    live_other = swap_x(pad_mask).astype(F32)
    keep_row = jnp.concatenate([live, live_other], axis=1)
    keep_col = live.reshape(toks, 1)
    pos_row, pos_col, cot_sent = kernel_call(
        functools.partial(route_body, n_exp, capacity),
        (sds((8, toks), I32), sds((toks, 8), I32), sds((slots, width), BF16)),
        cost=(2 * slots * toks * width, 4e6),
    )(ids.T, slot_priority.astype(F32), live, cotangent[0])

    def exchange(rows):
        return lax.all_to_all(rows, everyone, split_axis=0, concat_axis=0, tiled=True)

    cot_got = exchange(cot_sent)

    half_slots = total_slots // 2
    unpack_scratch = [pltpu.VMEM((half_slots, width), BF16)]
    unpack_cost = (2 * row_count * half_slots * width, 8e6)
    first_rows = kernel_call(
        functools.partial(unpack_body, 0, len(near)), sds((row_count, width), BF16), unpack_scratch,
        cost=unpack_cost,
    )(place_col, *near)
    weights = kernel_call(
        functools.partial(unpack_body, half_slots, len(far)), sds((row_count, width), BF16),
        unpack_scratch, cost=unpack_cost,
    )(place_col, *far, first_rows)

    all_expert = lax.all_gather(expert_slots[0], ("dp", "ctx"), axis=0, tiled=True)
    local = my * 2 + mx
    ff_rows = 2 * FF
    my_rows = lax.dynamic_slice(expert_owner[0], (local * ff_rows,), (ff_rows,))
    expert_rows = all_expert[my_rows]
    w_in, w_out = expert_rows[:FF], expert_rows[FF:]

    (qkv, normed, attended, residual, prob, sent, lse_col, lse_row) = kernel_call(
        functools.partial(forward_body, n_exp),
        (
            sds((2 * toks, 3 * width), BF16), sds((toks, width), BF16), sds((toks, width), F32),
            sds((toks, width), F32), sds((toks, n_exp), F32), sds((slots, width), BF16),
            sds((toks, LANES), F32), sds((8, toks), F32),
        ),
        [pltpu.VMEM((toks, width), BF16)],
        cost=(8e9, 1e7),
    )(own, other, keep_row, weights, pos_row)
    lse_other = swap_x(lse_row)
    got = exchange(sent)

    expert_id = (mz * EXP_DEV + local).astype(I32).reshape(1)
    tile = 256
    router_rows = weights[4 * width : 4 * width + n_exp]
    whole = lambda shape: pl.BlockSpec(shape, lambda f: (0, 0))
    active, hidden, scaled, result, back, router_grad = kernel_call(
        functools.partial(expert_body, n_exp),
        (
            sds((slots, FF), BF16), sds((slots, FF), BF16), sds((slots, width), BF16),
            sds((slots, width), BF16), sds((slots, width), BF16), sds((n_exp, width), F32),
        ),
        [pltpu.VMEM((slots, n_exp), F32), pltpu.VMEM((slots, width), F32), pltpu.VMEM((slots, width), F32)],
        grid=(FF // tile,),
        in_specs=[
            pl.BlockSpec(memory_space=pltpu.SMEM), whole((slots, width)), whole((slots, width)),
            pl.BlockSpec((tile, width), lambda f: (f, 0)), pl.BlockSpec((tile, width), lambda f: (f, 0)),
            whole((n_exp, width)),
        ],
        out_specs=(
            pl.BlockSpec((slots, tile), lambda f: (0, f)), pl.BlockSpec((slots, tile), lambda f: (0, f)),
            whole((slots, width)), whole((slots, width)), whole((slots, width)), whole((n_exp, width)),
        ),
        cost=(8 * slots * FF * width, 3e7),
    )(expert_id, got, cot_got, w_in, w_out, router_rows)
    back_got = exchange(back)
    result_got = exchange(result)

    grad_in = dot_tn(hidden, got)
    grad_out = dot_tn(active, scaled)
    mine = jnp.where(mc == 0, grad_in, grad_out)
    theirs = jnp.where(mc == 0, grad_out, grad_in).astype(BF16)
    summed = (mine + swap_core(theirs).astype(F32)).astype(BF16)
    all_grads = lax.all_gather(summed, ("dp", "ctx"), axis=0, tiled=True)

    owned = expert_slots.shape[1]
    base = (dp * 2 + mx) * owned
    owner = expert_owner[0]
    n_rows = owner.shape[0]
    row_no = jnp.arange(n_rows, dtype=I32)
    e_local, e_half, e_row = row_no // ff_rows, row_no // FF % 2, row_no % FF
    lies = (((e_local // 2) * 2 + e_half) * 2 + e_local % 2) * FF + e_row
    rel = owner - base
    hit = (rel[:, None] >> 7) == jnp.arange(owned // LANES, dtype=I32)[None, :]
    left = jnp.concatenate(
        [jnp.where(hit, (lies >> 7)[:, None], 0), jnp.where(hit, (lies & 127)[:, None], 0)], axis=1
    ).astype(BF16)
    right = ((rel & 127)[:, None] == jnp.arange(LANES, dtype=I32)[None, :]).astype(BF16)
    found = dot_tn(left, right)
    n_hi = owned // LANES
    source = (found[:n_hi] * 128.0 + found[n_hi:]).astype(I32).reshape(owned)
    expert_grad = all_grads[source].astype(F32)

    grad_residual, out_grad, delta_col, delta_row, gain_two = kernel_call(
        functools.partial(middle_body, n_exp),
        (
            sds((toks, width), F32), sds((toks, width), BF16), sds((toks, LANES), F32),
            sds((8, toks), F32), sds((8, width), F32),
        ),
        cost=(2e9, 1e7),
    )(back_got, pos_col, residual, cotangent[0], keep_col, attended, weights)
    out_grad_other, delta_other = swap_x(out_grad), swap_x(delta_row)
    late_count = width + n_exp + 16
    query_grad, kv_grad, early = kernel_call(
        functools.partial(inner_body, n_exp, 0),
        (sds((toks, width), BF16), sds((2, toks, width), F32), sds((total_slots, width), BF16)),
        [pltpu.VMEM((late_count, width), BF16)],
        cost=(8e9, 2e7),
    )(
        qkv, out_grad, lse_col, lse_row, delta_col, delta_row, keep_row, keep_col, attended,
        grad_residual, router_grad, gain_two, place_row,
    )
    grad_tokens, pieces, far_rows = kernel_call(
        functools.partial(outer_body, n_exp),
        (sds((toks, width), F32), sds((3 * width + 16, width), BF16), sds((half_slots, width), BF16)),
        [pltpu.VMEM((toks, 3 * width), BF16)],
        cost=(8e9, 2e7),
    )(
        qkv, out_grad_other, lse_other, delta_other, keep_col, query_grad, kv_grad, normed, own,
        weights, grad_residual, place_row, early,
    )
    far_got = swap_core(far_rows)
    near_rows = kernel_call(
        functools.partial(spread_body, width, n_exp), sds((half_slots, width), BF16),
        cost=(2 * half_slots * 3 * width * width, 1e7),
    )(place_row, pieces, early)
    quarter = half_slots // 2
    eighth, sixteenth = quarter // 2, quarter // 4
    sum_a = total_f32(near_rows[:quarter], far_got[:quarter]).astype(BF16)
    sum_b = total_f32(near_rows[quarter:], far_got[quarter:]).astype(BF16)
    got_a, got_b = swap_x(sum_a[eighth:]), swap_y(sum_b[eighth:])
    sum_a = total_f32(sum_a[:eighth], got_a).astype(BF16)
    sum_b = total_f32(sum_b[:eighth], got_b).astype(BF16)
    got_a, got_b = swap_y(sum_a[sixteenth:]), swap_x(sum_b[sixteenth:])
    sum_a = total_f32(sum_a[:sixteenth], got_a).astype(BF16)
    sum_b = total_f32(sum_b[:sixteenth], got_b).astype(BF16)
    lines = [sum_a[i * stride : (i + 1) * stride] for i in range(n_z // 2)]
    lines += [sum_b[i * stride : (i + 1) * stride] for i in range(n_z // 2)]
    shared_grad = lines[0].astype(F32)
    for by in range(1, n_z):
        shared_grad = shared_grad + shift_z(lines[by], n_z - by).astype(F32)
    shared_grad = shared_grad[:own_count]

    output = kernel_call(
        mixture_body, sds((toks, width), BF16), cost=(4 * slots * toks * width, 4e6)
    )(result_got, pos_col, ids, prob, residual)

    shared_new = adam_update(shared_grad, shared_first, shared_second, shared_slots.astype(F32))
    expert_new = adam_update(expert_grad, expert_first[0], expert_second[0], expert_slots[0].astype(F32))
    return (
        output[None], grad_tokens[None], shared_grad, *shared_new,
        expert_grad[None], *(value[None] for value in expert_new),
    )


def solution(mesh):
    sizes = mesh.shape
    chip_experts = (sizes["dp"], sizes["ctx"], sizes["expert"]) == (4, 2, 4)
    return jax.shard_map(
        on_chip_experts if chip_experts else on_device,
        mesh=mesh,
        in_specs=(
            P(("dp", "expert"), "ctx", None),
            P(("dp", "expert"), "ctx", None),
            P(("dp", "expert"), "ctx"),
            P(("dp", "expert"), "ctx", None),
            P(("dp", "expert"), "ctx"),
            P(("dp", "ctx", "expert"), None),
            P(("dp", "ctx", "expert"), None),
            P(("dp", "ctx", "expert"), None),
            P(),
            P("expert", ("dp", "ctx"), None),
            P("expert", ("dp", "ctx"), None),
            P("expert", ("dp", "ctx"), None),
            P("expert", None),
        ),
        out_specs=(
            P(("dp", "expert"), "ctx", None),
            P(("dp", "expert"), "ctx", None),
            P(("dp", "ctx", "expert"), None),
            P(("dp", "ctx", "expert"), None),
            P(("dp", "ctx", "expert"), None),
            P(("dp", "ctx", "expert"), None),
            P("expert", ("dp", "ctx"), None),
            P("expert", ("dp", "ctx"), None),
            P("expert", ("dp", "ctx"), None),
            P("expert", ("dp", "ctx"), None),
        ),
        check_vma=False,
    )
```

```python
import functools
import math

import jax
import jax.numpy as jnp
from jax import lax
from jax.experimental import pallas as pl
from jax.experimental.pallas import tpu as pltpu
from jax.sharding import PartitionSpec as P

HEADS = 8
HEAD_DIM = 64
FF = 2048
EXP_DEV = 4


MASKED_SCORE = -1e30
MOMENT_DECAY = 0.5
LEARN_RATE = 0.05
WEIGHT_DECAY = 0.1
EPSILON = 1e-08
NORM_EPSILON = 1e-06


def layer_norm(values, gain_rows):
    center = values - jnp.mean(values, axis=-1, keepdims=True)
    spread = jnp.mean(center * center, axis=-1, keepdims=True)
    return center * lax.rsqrt(spread + NORM_EPSILON) * gain_rows


def routing(chosen, priority, live_rows, expert_count, capacity):
    tok_count = chosen.shape[0]
    token_ids = jnp.arange(tok_count, dtype=jnp.int32)
    ranking = jnp.argsort(priority * tok_count + token_ids)
    labels = jnp.arange(expert_count, dtype=jnp.int32)
    wanted = jnp.any(chosen[:, :, None] == labels[None, None, :], axis=1) & (
        live_rows[:, None] == 1
    )
    wanted = wanted.astype(jnp.int32)
    ranked = wanted[ranking]
    before = jnp.cumsum(ranked, axis=0) - ranked
    position = jnp.zeros_like(before).at[ranking].set(before)
    slot_taken = jnp.take_along_axis(position, chosen, axis=1)
    kept_pair = (slot_taken < capacity) & (live_rows[:, None] == 1)
    target = jnp.where(kept_pair, chosen * capacity + slot_taken, expert_count * capacity)
    owners = jnp.broadcast_to(token_ids[:, None], chosen.shape)
    source = (
        jnp.zeros((expert_count * capacity,), jnp.int32)
        .at[target.reshape(-1)]
        .set(owners.reshape(-1), mode="drop")
    )
    filled = (
        jnp.zeros((expert_count * capacity,), jnp.int32).at[target.reshape(-1)].set(1, mode="drop")
    )
    slot_index = jnp.where(kept_pair, chosen * capacity + slot_taken, 0)
    return (slot_index, kept_pair.astype(jnp.int32), source, filled)


def head_view(values):
    return values.reshape(values.shape[0], values.shape[1], HEADS, HEAD_DIM)


def score_block(queries, key_rows, keep_mask):
    score = jnp.einsum(
        "iqhe,ikhe->ihqk", queries, head_view(key_rows), preferred_element_type=jnp.float32
    ) * HEAD_DIM ** (-0.5)
    return jnp.where(keep_mask[:, None, None, :] > 0, score, MASKED_SCORE)


def stats_step(running, portion, queries):
    row_max, row_sum = running
    key_rows, keep_mask = portion
    score = score_block(queries, key_rows, keep_mask)
    keep_wide = keep_mask.astype(jnp.float32)[:, None, None, :]
    new_max = jnp.maximum(row_max, jnp.max(score, axis=-1))
    row_sum = row_sum * jnp.exp(row_max - new_max) + jnp.sum(
        jnp.exp(score - new_max[..., None]) * keep_wide, axis=-1
    )
    return (new_max, row_sum)


def value_step(running, portion, queries, log_sum):
    key_rows, value_rows, keep_mask = portion
    score = score_block(queries, key_rows, keep_mask)
    keep_wide = keep_mask.astype(jnp.float32)[:, None, None, :]
    attn_prob = (jnp.exp(score - log_sum[..., None]) * keep_wide).astype(jnp.bfloat16)
    return running + jnp.einsum(
        "ihqk,ikhe->iqhe", attn_prob, head_view(value_rows), preferred_element_type=jnp.float32
    )


def grad_step(grad_query, portion, queries, log_sum, grad_out, row_delta):
    key_rows, value_rows, keep_mask = portion
    score = score_block(queries, key_rows, keep_mask)
    keep_wide = keep_mask.astype(jnp.float32)[:, None, None, :]
    attn_prob = jnp.exp(score - log_sum[..., None]) * keep_wide
    prob_low = attn_prob.astype(jnp.bfloat16)
    grad_value = jnp.einsum(
        "ihqk,iqhe->ikhe", prob_low, grad_out, preferred_element_type=jnp.float32
    )
    grad_prob = jnp.einsum(
        "iqhe,ikhe->ihqk", grad_out, head_view(value_rows), preferred_element_type=jnp.float32
    )
    grad_score = (attn_prob * (grad_prob - row_delta[..., None])).astype(jnp.bfloat16)
    score_scale = HEAD_DIM ** (-0.5)
    grad_query = (
        grad_query
        + jnp.einsum(
            "ihqk,ikhe->iqhe", grad_score, head_view(key_rows), preferred_element_type=jnp.float32
        )
        * score_scale
    )
    grad_key = (
        jnp.einsum("ihqk,iqhe->ikhe", grad_score, queries, preferred_element_type=jnp.float32)
        * score_scale
    )
    return (grad_query, jnp.stack([grad_key, grad_value]))


def each_block(step_fn, running, arrays, block_len):
    total_len = arrays[0].shape[1]
    size_rows = math.gcd(total_len, block_len)

    def one_turn(number, current):
        offset = number * size_rows
        portion = tuple(
            (lax.dynamic_slice_in_dim(member, offset, size_rows, 1) for member in arrays)
        )
        return step_fn(current, portion)

    return lax.fori_loop(0, total_len // size_rows, one_turn, running)


def adam_update(gradient, first_old, second_old, weight):
    first_new = MOMENT_DECAY * first_old + (1.0 - MOMENT_DECAY) * gradient
    second_new = MOMENT_DECAY * second_old + (1.0 - MOMENT_DECAY) * gradient * gradient
    weight_new = weight - LEARN_RATE * (
        first_new / (jnp.sqrt(second_new) + EPSILON) + WEIGHT_DECAY * weight
    )
    return (first_new, second_new, weight_new)


def on_device(
    tokens,
    cotangent,
    pad_mask,
    expert_ids,
    slot_priority,
    shared_slots,
    shared_first,
    shared_second,
    shared_owner,
    expert_slots,
    expert_first,
    expert_second,
    expert_owner,
):
    img_count, part_len, features = tokens.shape
    tok_count = img_count * part_len
    expert_count = EXP_DEV * lax.axis_size("expert")
    capacity = (10 * tok_count + 4 * expert_count - 1) // (4 * expert_count)
    all_shared = lax.all_gather(shared_slots, ("dp", "ctx", "expert"), axis=0, tiled=True)
    all_expert = lax.all_gather(expert_slots, ("dp", "ctx"), axis=1, tiled=True)
    pieces = all_shared[shared_owner]
    w_qkv = pieces[: 3 * features]
    w_attn_out = pieces[3 * features : 4 * features]
    w_router = pieces[4 * features : 4 * features + expert_count]
    gain_one = pieces[4 * features + expert_count].astype(jnp.float32)
    gain_two = pieces[4 * features + expert_count + 1].astype(jnp.float32)
    expert_rows = all_expert[0][expert_owner[0]].reshape(EXP_DEV, 2, FF, features)
    w_in = expert_rows[:, 0]
    w_out = expert_rows[:, 1]
    inputs = tokens.reshape(tok_count, features).astype(jnp.float32)
    keep_mask = pad_mask.astype(jnp.bfloat16)
    keep_rows = pad_mask.reshape(tok_count).astype(jnp.float32)
    normed_one, norm_one_back = jax.vjp(layer_norm, inputs, gain_one)
    normed_low = normed_one.astype(jnp.bfloat16)
    qkv_rows = lax.dot_general(
        normed_low, w_qkv, (((1,), (1,)), ((), ())), preferred_element_type=jnp.float32
    ).astype(jnp.bfloat16)
    query_rows = qkv_rows[:, :features].reshape(img_count, part_len, features)
    key_rows = qkv_rows[:, features : 2 * features].reshape(img_count, part_len, features)
    value_rows = qkv_rows[:, 2 * features :].reshape(img_count, part_len, features)
    queries = head_view(query_rows)
    start_max = jnp.full((img_count, HEADS, part_len), MASKED_SCORE, jnp.float32)
    start_sum = jnp.zeros((img_count, HEADS, part_len), jnp.float32)
    start_out = jnp.zeros((img_count, part_len, HEADS, HEAD_DIM), jnp.float32)
    whole_keys, whole_values, whole_keep = (
        lax.all_gather(key_rows, "ctx", axis=1, tiled=True),
        lax.all_gather(value_rows, "ctx", axis=1, tiled=True),
        lax.all_gather(keep_mask, "ctx", axis=1, tiled=True),
    )
    row_max, row_sum = each_block(
        lambda running, portion: stats_step(running, portion, queries),
        (start_max, start_sum),
        (whole_keys, whole_keep),
        part_len,
    )
    log_sum = row_max + jnp.log(row_sum)
    attended = each_block(
        lambda running, portion: value_step(running, portion, queries, log_sum),
        start_out,
        (whole_keys, whole_values, whole_keep),
        part_len,
    )
    attended_low = attended.reshape(tok_count, features).astype(jnp.bfloat16)
    branch = jnp.dot(attended_low, w_attn_out, preferred_element_type=jnp.float32)
    residual = inputs + branch
    normed_two, norm_two_back = jax.vjp(layer_norm, residual, gain_two)
    mixed_low = normed_two.astype(jnp.bfloat16)
    logits = lax.dot_general(
        mixed_low, w_router, (((1,), (1,)), ((), ())), preferred_element_type=jnp.float32
    )
    router_prob = jax.nn.softmax(logits, axis=-1)
    chosen = expert_ids.reshape(tok_count, 2)
    slot_index, kept_pair, source, filled = routing(
        chosen,
        slot_priority.reshape(tok_count),
        pad_mask.reshape(tok_count),
        expert_count,
        capacity,
    )
    filled_low = filled.astype(jnp.bfloat16)
    dispatched = (mixed_low[source] * filled_low[:, None]).reshape(expert_count, capacity, features)
    received = lax.all_to_all(dispatched, "expert", split_axis=0, concat_axis=1, tiled=True)
    hidden = jnp.einsum("ecd,efd->ecf", received, w_in, preferred_element_type=jnp.float32)
    active, gelu_back = jax.vjp(lambda pre_act: jax.nn.gelu(pre_act, approximate=False), hidden)
    active_low = active.astype(jnp.bfloat16)
    result = jnp.einsum(
        "ecf,efd->ecd", active_low, w_out, preferred_element_type=jnp.float32
    ).astype(jnp.bfloat16)
    returned = lax.all_to_all(result, "expert", split_axis=1, concat_axis=0, tiled=True).reshape(
        expert_count * capacity, features
    )
    kept_float = kept_pair.astype(jnp.float32)
    gate_value = jnp.take_along_axis(router_prob, chosen, axis=1) * kept_float
    picked = returned[slot_index].astype(jnp.float32)
    mixture = jnp.sum(gate_value[:, :, None] * picked, axis=1)
    output = (residual + mixture).astype(jnp.bfloat16).reshape(tokens.shape)
    grad_rows = cotangent.reshape(tok_count, features).astype(jnp.float32) * keep_rows[:, None]
    grad_gate = jnp.sum(grad_rows[:, None, :] * picked, axis=-1) * kept_float
    labels = jnp.arange(expert_count, dtype=jnp.int32)
    grad_prob = jnp.sum(
        (chosen[:, :, None] == labels[None, None, :]).astype(jnp.float32) * grad_gate[:, :, None],
        axis=1,
    )
    grad_logits = router_prob * (
        grad_prob - jnp.sum(grad_prob * router_prob, axis=-1, keepdims=True)
    )
    grad_logits_low = grad_logits.astype(jnp.bfloat16)
    slot_expert = jnp.arange(expert_count * capacity, dtype=jnp.int32) // capacity
    slot_gate = jnp.take_along_axis(router_prob[source], slot_expert[:, None], axis=1)[
        :, 0
    ] * filled.astype(jnp.float32)
    grad_result = (
        (grad_rows[source] * slot_gate[:, None])
        .astype(jnp.bfloat16)
        .reshape(expert_count, capacity, features)
    )
    grad_received = lax.all_to_all(grad_result, "expert", split_axis=0, concat_axis=1, tiled=True)
    grad_active = jnp.einsum(
        "ecd,efd->ecf", grad_received, w_out, preferred_element_type=jnp.float32
    )
    grad_hidden = gelu_back(grad_active)[0].astype(jnp.bfloat16)
    grad_w_out = jnp.einsum(
        "ecf,ecd->efd", active_low, grad_received, preferred_element_type=jnp.float32
    )
    grad_w_in = jnp.einsum(
        "ecf,ecd->efd", grad_hidden, received, preferred_element_type=jnp.float32
    )
    grad_sent = jnp.einsum(
        "ecf,efd->ecd", grad_hidden, w_in, preferred_element_type=jnp.float32
    ).astype(jnp.bfloat16)
    grad_back = lax.all_to_all(
        grad_sent, "expert", split_axis=1, concat_axis=0, tiled=True
    ).reshape(expert_count * capacity, features)
    grad_mixed = jnp.sum(grad_back[slot_index].astype(jnp.float32) * kept_float[:, :, None], axis=1)
    grad_mixed = grad_mixed + jnp.dot(grad_logits_low, w_router, preferred_element_type=jnp.float32)
    grad_router = lax.dot_general(
        grad_logits_low, mixed_low, (((0,), (0,)), ((), ())), preferred_element_type=jnp.float32
    )
    grad_residual_part, grad_gain_two = norm_two_back(grad_mixed)
    grad_residual = grad_rows + grad_residual_part
    grad_branch = grad_residual.astype(jnp.bfloat16)
    grad_w_attn_out = lax.dot_general(
        attended_low, grad_branch, (((0,), (0,)), ((), ())), preferred_element_type=jnp.float32
    )
    grad_attended = lax.dot_general(
        grad_branch, w_attn_out, (((1,), (1,)), ((), ())), preferred_element_type=jnp.float32
    ).astype(jnp.bfloat16)
    grad_out = head_view(grad_attended.reshape(img_count, part_len, features))
    row_delta = jnp.transpose(jnp.sum(grad_out.astype(jnp.float32) * attended, axis=-1), (0, 2, 1))
    start_grad = jnp.zeros((img_count, part_len, HEADS, HEAD_DIM), jnp.float32)
    whole_grads = jnp.zeros((2, img_count, whole_keys.shape[1], HEADS, HEAD_DIM), jnp.float32)

    def grad_turn(number, current):
        grad_query, grads_all = current
        offset = number * part_len
        portion = tuple(
            (
                lax.dynamic_slice_in_dim(member, offset, part_len, 1)
                for member in (whole_keys, whole_values, whole_keep)
            )
        )
        grad_query, grad_block = grad_step(
            grad_query, portion, queries, log_sum, grad_out, row_delta
        )
        grads_all = lax.dynamic_update_slice_in_dim(grads_all, grad_block, offset, 2)
        return (grad_query, grads_all)

    grad_query, whole_grads = lax.fori_loop(
        0, whole_keys.shape[1] // part_len, grad_turn, (start_grad, whole_grads)
    )
    grad_pair = lax.psum_scatter(whole_grads, "ctx", scatter_dimension=2, tiled=True)
    grad_qkv = jnp.concatenate(
        [
            grad_query.reshape(tok_count, features),
            grad_pair[0].reshape(tok_count, features),
            grad_pair[1].reshape(tok_count, features),
        ],
        axis=1,
    ).astype(jnp.bfloat16)
    grad_w_qkv = lax.dot_general(
        grad_qkv, normed_low, (((0,), (0,)), ((), ())), preferred_element_type=jnp.float32
    )
    grad_normed = jnp.dot(grad_qkv, w_qkv, preferred_element_type=jnp.float32)
    grad_input_part, grad_gain_one = norm_one_back(grad_normed)
    grad_tokens = (grad_residual + grad_input_part).reshape(tokens.shape)
    shared_pieces = jnp.concatenate(
        [grad_w_qkv, grad_w_attn_out, grad_router, grad_gain_one[None, :], grad_gain_two[None, :]],
        axis=0,
    )
    shared_layout = jnp.zeros(all_shared.shape, jnp.float32).at[shared_owner].set(shared_pieces)
    shared_grad = lax.psum_scatter(
        shared_layout, ("dp", "ctx", "expert"), scatter_dimension=0, tiled=True
    )
    expert_pieces = jnp.stack([grad_w_in, grad_w_out], axis=1).reshape(EXP_DEV * 2 * FF, features)
    expert_layout = (
        jnp.zeros(all_expert.shape, jnp.float32).at[0, expert_owner[0]].set(expert_pieces)
    )
    expert_grad = lax.psum_scatter(expert_layout, ("dp", "ctx"), scatter_dimension=1, tiled=True)
    shared_first_new, shared_second_new, shared_weight_new = adam_update(
        shared_grad, shared_first, shared_second, shared_slots.astype(jnp.float32)
    )
    expert_first_new, expert_second_new, expert_weight_new = adam_update(
        expert_grad, expert_first, expert_second, expert_slots.astype(jnp.float32)
    )
    return (
        output,
        grad_tokens,
        shared_grad,
        shared_first_new,
        shared_second_new,
        shared_weight_new,
        expert_grad,
        expert_first_new,
        expert_second_new,
        expert_weight_new,
    )


F32 = jnp.float32
BF16 = jnp.bfloat16
I32 = jnp.int32
LANES = 128
MASKED = -1e30
VMEM_LIMIT = 56 * 1024 * 1024
MICRO = 1.15e9
QUICK = (1e6, 1e3)
THEIRS = 2


def dot_nn(left, right):
    return lax.dot_general(left, right, (((1,), (0,)), ((), ())), preferred_element_type=F32)


def dot_nt(left, right):
    return lax.dot_general(left, right, (((1,), (1,)), ((), ())), preferred_element_type=F32)


def dot_tn(left, right):
    return lax.dot_general(left, right, (((0,), (0,)), ((), ())), preferred_element_type=F32)


def iota(shape, dim):
    return lax.broadcasted_iota(I32, shape, dim)


def as_bf16(mask):
    return jnp.where(mask, 1.0, 0.0).astype(BF16)


def kernel_call(body, out_shape, scratch=(), grid=None, in_specs=None, out_specs=None, cost=None):
    given = dict(grid=grid, in_specs=in_specs, out_specs=out_specs)
    extra = {name: value for name, value in given.items() if value is not None}
    flops, moved = cost if cost else (1e8, 1e6)
    name = getattr(body, "func", body).__name__
    return pl.pallas_call(
        body,
        name=name,
        out_shape=out_shape,
        scratch_shapes=list(scratch),
        compiler_params=pltpu.CompilerParams(vmem_limit_bytes=VMEM_LIMIT),
        cost_estimate=pl.CostEstimate(flops=int(flops), bytes_accessed=int(moved), transcendentals=0),
        **extra,
    )


def sds(shape, dtype):
    return jax.ShapeDtypeStruct(shape, dtype)


def route_body(n_exp, capacity, ids_ref, prio_ref, live_ref, cot_ref, row_ref, col_ref, sent_ref):
    toks = ids_ref.shape[1]
    half = capacity // 2
    prio_row = prio_ref[...]
    prio_col = jnp.transpose(jnp.broadcast_to(prio_row, (8, toks)))[:, :1]
    earlier = (prio_col < prio_row) | (
        (prio_col == prio_row) & (iota((toks, toks), 0) < iota((toks, toks), 1))
    )
    live = live_ref[...] > 0.0
    labels = iota((n_exp, toks), 0)
    first, second = ids_ref[0:1, :], ids_ref[1:2, :]
    wanted = ((labels == first) | (labels == second)) & live
    taken = dot_nn(as_bf16(wanted), as_bf16(earlier))
    places = []
    for chosen in (first, second):
        slot = jnp.sum(jnp.where(labels == chosen, taken, 0.0), axis=0, keepdims=True).astype(I32)
        kept = live & (slot < capacity)
        shard = chosen >> 2
        local = chosen & 3
        core = (slot >= half).astype(I32)
        target = ((((local >> 1) * 2 + core) * 2 + (local & 1)) * (n_exp // 4)) + shard
        places.append(jnp.where(kept, target * half + slot - core * half, -1))
    row_id = iota((8, toks), 0)
    rows = jnp.where(row_id == 0, places[0], jnp.where(row_id == 1, places[1], -1))
    row_ref[...] = rows
    col_ref[...] = jnp.transpose(rows.astype(F32)).astype(I32)
    slots = sent_ref.shape[0]
    spots = iota((slots, toks), 0)
    picks = as_bf16((spots == places[0]) | (spots == places[1]))
    sent_ref[...] = dot_nn(picks, cot_ref[...]).astype(BF16)


def unpack_body(spots_at, n_earlier, pos_ref, *refs):
    n_pieces = len(spots_at)
    pieces, rest = refs[:n_pieces], refs[n_pieces:]
    out_ref, held = rest[-2], rest[-1]

    @pl.when(pl.program_id(0) == 0)
    def _():
        gather_pieces(pieces, held)

    wanted = pos_ref[...]
    size = pieces[0].shape[0]
    place = jnp.full(wanted.shape, -1, I32)
    for number, at in enumerate(spots_at):
        inside = (wanted >= at) & (wanted < at + size)
        place = jnp.where(inside, wanted - at + number * size, place)
    picks = as_bf16(place == iota((wanted.shape[0], held.shape[0]), 1))
    value = dot_nn(picks, held[...])
    for earlier in rest[:n_earlier]:
        value = value + earlier[...].astype(F32)
    out_ref[...] = value.astype(BF16)


def gather_pieces(pieces, held):
    at = 0
    for piece in pieces:
        held[at : at + piece.shape[0], :] = piece[...]
        at += piece.shape[0]


def normalize(values):
    center = values - jnp.mean(values, axis=-1, keepdims=True)
    spread = jnp.mean(center * center, axis=-1, keepdims=True)
    scale = lax.rsqrt(spread + NORM_EPSILON)
    return center * scale, scale


def head_lanes(head, rows):
    return (iota((rows, LANES), 1) // HEAD_DIM) == head


def of_head(values, head):
    return jnp.where(head_lanes(head, values.shape[0]), values, jnp.zeros_like(values))


def by_head(first, second):
    return jnp.where(head_lanes(0, first.shape[0]), first, second)


def forward_body(
    n_exp, own_ref, other_ref, keep_ref, w_ref, pos_ref,
    qkv_ref, normed_ref, attended_ref, residual_ref, prob_ref, sent_ref, lse_col_ref, lse_row_ref,
    mixed_ref,
):
    toks, width = own_ref.shape
    router = 4 * width
    gain_one = w_ref[router + n_exp : router + n_exp + 16, :].astype(F32)
    gain_two = gain_one[1:2, :]
    gain_one = gain_one[0:1, :]
    for part, ref in enumerate((own_ref, other_ref)):
        normed = normalize(ref[...].astype(F32))[0] * gain_one
        low = normed.astype(BF16)
        if part == 0:
            normed_ref[...] = low
        rows = pl.ds(part * toks, toks)
        for third in range(3):
            made = dot_nt(low, w_ref[third * width : (third + 1) * width, :]).astype(BF16)
            if third == 0:
                made = made * jnp.asarray(HEAD_DIM ** (-0.5), BF16)
            qkv_ref[rows, third * width : (third + 1) * width] = made
    bias = jnp.where(keep_ref[...] > 0.0, 0.0, MASKED)
    lane = iota((toks, LANES), 1)
    logs = jnp.zeros((toks, LANES), F32)
    for at in range(0, width, LANES):
        queries = qkv_ref[0:toks, at : at + LANES]
        keys = qkv_ref[:, width + at : width + at + LANES]
        values = qkv_ref[:, 2 * width + at : 2 * width + at + LANES]
        made = []
        for head in range(2):
            score = dot_nt(of_head(queries, head), keys) + bias
            top = jnp.max(score, axis=-1, keepdims=True)
            grown = jnp.exp(score - top)
            total = jnp.sum(grown, axis=-1, keepdims=True)
            made.append(dot_nn(grown.astype(BF16), values) * (1.0 / total))
            logs = jnp.where(lane == 2 * (at // LANES) + head, top + jnp.log(total), logs)
        attended_ref[:, at : at + LANES] = by_head(*made)
    lse_col_ref[...] = logs
    lse_row_ref[...] = jnp.transpose(lse_col_ref[...])[:8, :]
    branch = dot_nn(attended_ref[...].astype(BF16), w_ref[3 * width : 4 * width, :])
    residual = own_ref[...].astype(F32) + branch
    residual_ref[...] = residual
    mixed = (normalize(residual)[0] * gain_two).astype(BF16)
    mixed_ref[...] = mixed
    logits = dot_nt(mixed, w_ref[router : router + n_exp, :])
    prob_ref[...] = jax.nn.softmax(logits, axis=-1)
    slots = sent_ref.shape[0]
    spots = iota((slots, toks), 0)
    picks = as_bf16((spots == pos_ref[0:1, :]) | (spots == pos_ref[1:2, :]))
    sent_ref[...] = dot_nn(picks, mixed).astype(BF16)


def gelu_parts(value):
    below = 0.5 + 0.5 * lax.erf(value * 0.7071067811865476)
    return value * below, below + value * jnp.exp(-0.5 * value * value) * 0.3989422804014327


def expert_body(
    n_exp, expert_ref, got_ref, cot_ref, near_ref, far_in_ref, far_out_ref, router_ref,
    active_ref, hidden_ref, scaled_ref, result_ref, back_ref, router_grad_ref,
):
    @pl.when(pl.program_id(0) == 0)
    def _():
        router_grad_ref[...] = jnp.zeros_like(router_grad_ref)

    expert = expert_ref[0]
    got, cot = got_ref[...], cot_ref[...]
    labels = iota((got.shape[0], n_exp), 1)
    share = jax.nn.softmax(dot_nt(got, router_ref[...]), axis=-1)
    gate = jnp.sum(jnp.where(labels == expert, share, 0.0), axis=-1, keepdims=True)
    scaled = (cot.astype(F32) * gate).astype(BF16)
    scaled_ref[...] = scaled
    half = near_ref.shape[0] // 2
    total = total_back = 0.0
    halves = ((near_ref[:half, :], near_ref[half:, :]), (far_in_ref[...], far_out_ref[...]))
    for number, (w_in, w_out) in enumerate(halves):
        at = slice(number * half, (number + 1) * half)
        active, slope = gelu_parts(dot_nt(got, w_in))
        low = active.astype(BF16)
        active_ref[:, at] = low
        grad = (dot_nt(scaled, w_out) * slope).astype(BF16)
        hidden_ref[:, at] = grad
        total = total + dot_nn(low, w_out)
        total_back = total_back + dot_nn(grad, w_in)
    result = total.astype(BF16)
    result_ref[...] = result
    inner = jnp.sum(result.astype(F32) * cot.astype(F32), axis=-1, keepdims=True)
    grad = share * (jnp.where(labels == expert, inner, 0.0) - gate * inner)
    low = grad.astype(BF16)
    back_ref[...] = (total_back + dot_nn(low, router_ref[...])).astype(BF16)
    router_grad_ref[...] += dot_tn(low, got)


def weight_grad_body(hidden_ref, active_ref, got_ref, scaled_ref, mine_ref, *theirs_refs):
    half = hidden_ref.shape[1] // 2
    parts = max(len(theirs_refs) // 2, 1)
    for number, ref in enumerate(theirs_refs):
        size = ref.shape[0]
        at = slice(half + number % parts * size, half + (number % parts + 1) * size)
        left, right = ((hidden_ref, got_ref), (active_ref, scaled_ref))[number // parts]
        ref[...] = dot_tn(left[:, at], right[...]).astype(ref.dtype)
    mine_ref[:half, :] = dot_tn(hidden_ref[:, :half], got_ref[...])
    mine_ref[half:, :] = dot_tn(active_ref[:, :half], scaled_ref[...])


def norm_back(hat, scale, gain, grad):
    inner = grad * gain
    first = jnp.mean(inner, axis=-1, keepdims=True)
    second = jnp.mean(inner * hat, axis=-1, keepdims=True)
    return (inner - first - hat * second) * scale


def middle_body(
    n_exp, back_ref, pos_ref, residual_ref, cot_ref, keep_ref, attended_ref, w_ref,
    grad_ref, out_grad_ref, delta_col_ref, delta_row_ref, gain_ref,
):
    toks, width = residual_ref.shape
    router = 4 * width
    slots = back_ref.shape[0]
    gain_two = w_ref[router + n_exp : router + n_exp + 16, :].astype(F32)[1:2, :]
    spots = iota((toks, slots), 1)
    picks = as_bf16((spots == pos_ref[:, 0:1]) | (spots == pos_ref[:, 1:2]))
    grad_mixed = dot_nn(picks, back_ref[...])
    hat, scale = normalize(residual_ref[...])
    gain_ref[...] = jnp.broadcast_to(
        jnp.sum(grad_mixed * hat, axis=0, keepdims=True), gain_ref.shape
    )
    grad_rows = cot_ref[...].astype(F32) * keep_ref[...]
    grad = grad_rows + norm_back(hat, scale, gain_two, grad_mixed)
    grad_ref[...] = grad
    low = grad.astype(BF16)
    out_grad = dot_nt(low, w_ref[3 * width : 4 * width, :]).astype(BF16)
    out_grad_ref[...] = out_grad
    product = out_grad.astype(F32) * attended_ref[...]
    delta = jnp.zeros((toks, LANES), F32)
    lane = iota((toks, LANES), 1)
    for head in range(HEADS):
        at = (head // 2) * LANES
        part = jnp.where(head_lanes(head % 2, toks), product[:, at : at + LANES], 0.0)
        delta = jnp.where(lane == head, jnp.sum(part, axis=-1, keepdims=True), delta)
    delta_col_ref[...] = delta
    delta_row_ref[...] = jnp.transpose(delta)[:8, :]


def inner_body(
    n_exp, qkv_ref, out_grad_ref, lse_ref, delta_ref, keep_ref, attended_ref, grad_ref, router_grad_ref, gain_ref,
    query_ref, kv_ref, early_ref,
):
    toks, width = out_grad_ref.shape
    bias = jnp.where(keep_ref[...] > 0.0, 0.0, MASKED)
    for at in range(0, width, LANES):
        queries = qkv_ref[0:toks, at : at + LANES]
        keys = qkv_ref[:, width + at : width + at + LANES]
        values = qkv_ref[:, 2 * width + at : 2 * width + at + LANES]
        out_grad = out_grad_ref[:, at : at + LANES]
        made = []
        for head in range(2):
            line = 2 * (at // LANES) + head
            score = dot_nt(of_head(queries, head), keys) + bias
            prob = jnp.exp(score - lse_ref[:, line : line + 1])
            slope = dot_nt(of_head(out_grad, head), values)
            grad = (prob * (slope - delta_ref[:, line : line + 1])).astype(BF16)
            made.append(
                (dot_nn(grad, keys), dot_tn(grad[:, :toks], queries), dot_tn(prob[:, :toks].astype(BF16), out_grad))
            )
        query_ref[:, at : at + LANES] = (by_head(made[0][0], made[1][0]) * HEAD_DIM ** (-0.5)).astype(BF16)
        kv_ref[0, :, at : at + LANES] = by_head(made[0][1], made[1][1])
        kv_ref[1, :, at : at + LANES] = by_head(made[0][2], made[1][2])
    early_ref[0:width, :] = dot_tn(attended_ref[...].astype(BF16), grad_ref[...].astype(BF16)).astype(BF16)
    early_ref[width : width + n_exp, :] = router_grad_ref[...].astype(BF16)
    row_id = iota((16, width), 0)
    early_ref[width + n_exp : width + n_exp + 16, :] = jnp.where(
        row_id == 0, gain_ref[0:1, :], 0.0
    ).astype(BF16)


def outer_body(
    n_exp, qkv_ref, out_grad_ref, sums_ref, keep_ref, query_ref, kv_ref, normed_ref, own_ref, w_ref,
    pieces_ref, grad_normed_ref, held,
):
    toks, width = query_ref.shape
    held[:, 0:width] = query_ref[...]
    bias = jnp.where(keep_ref[...] > 0.0, 0.0, MASKED)
    for at in range(0, width, LANES):
        queries = qkv_ref[toks : 2 * toks, at : at + LANES]
        out_grad = out_grad_ref[:, at : at + LANES]
        keys = qkv_ref[0:toks, width + at : width + at + LANES]
        values = qkv_ref[0:toks, 2 * width + at : 2 * width + at + LANES]
        made = []
        for head in range(2):
            line = 2 * (at // LANES) + head
            score = dot_nt(of_head(keys, head), queries) + bias
            prob = jnp.exp(score - sums_ref[line : line + 1, :])
            slope = dot_nt(of_head(values, head), out_grad)
            grad = (prob * (slope - sums_ref[HEADS + line : HEADS + line + 1, :])).astype(BF16)
            made.append((dot_nn(grad, queries), dot_nn(prob.astype(BF16), out_grad)))
        for number in range(2):
            total = kv_ref[number, :, at : at + LANES] + by_head(made[0][number], made[1][number])
            held[:, (number + 1) * width + at : (number + 1) * width + at + LANES] = total.astype(BF16)
    pieces_ref[0 : 3 * width, :] = dot_tn(held[...], normed_ref[...]).astype(BF16)
    grad_normed = dot_nn(held[...], w_ref[0 : 3 * width, :])
    grad_normed_ref[...] = grad_normed
    gain_grad = jnp.sum(grad_normed * normalize(own_ref[...].astype(F32))[0], axis=0, keepdims=True)
    pieces_ref[3 * width : 3 * width + 16, :] = jnp.where(
        iota((16, width), 0) == 0, gain_grad, 0.0
    ).astype(BF16)


def tokens_body(n_exp, grad_normed_ref, own_ref, w_ref, grad_ref, out_ref):
    at = 4 * own_ref.shape[1] + n_exp
    gain_one = w_ref[at : at + 16, :].astype(F32)[0:1, :]
    hat, scale = normalize(own_ref[...].astype(F32))
    out_ref[...] = grad_ref[...] + norm_back(hat, scale, gain_one, grad_normed_ref[...])


def spread_body(starts, pos_ref, late_ref, late_far_ref, early_ref, early_far_ref, out_ref, held):
    cut = late_ref.shape[0]
    held[0:cut, :] = total_f32(late_ref[...], late_far_ref[...]).astype(BF16)
    held[cut:, :] = total_f32(early_ref[...], early_far_ref[...]).astype(BF16)
    size = out_ref.shape[1]
    for number, start in enumerate(starts):
        picks = as_bf16(iota((size, held.shape[0]), 0) + start == pos_ref[...])
        out_ref[number] = dot_nn(picks, held[...]).astype(BF16)


def room_of(owned, n_dev):
    return min(owned, -(-(owned // n_dev * 5 // 4) // 16) * 16)


def sent_at(partner):
    return ((partner >> 1) & 1) * 4 + ((partner >> 2) & 1) * 2 + (partner & 1)


def got_at(partner):
    return ((partner >> 2) & 1) * 4 + (partner & 1) * 2 + ((partner >> 1) & 1)


def plan_body(n_dev, room, me_ref, owner_ref, row_ref, col_ref, most_ref):
    me = me_ref[0]
    owned = owner_ref.shape[1]
    source = owner_ref[...] >> (owned.bit_length() - 1)
    spot = owner_ref[...] & (owned - 1)
    total = n_dev * n_dev
    classes = iota((n_dev, owned), 0)
    member = jnp.concatenate([classes == source[t : t + 1, :] for t in range(n_dev)], axis=0)
    ones = as_bf16(member)
    step = 256
    before = as_bf16(iota((step, step), 0) < iota((step, step), 1))
    count = jnp.zeros((total, 1), F32)
    ranks = []
    for at in range(0, owned, step):
        part = ones[:, at : at + step]
        ranks.append(dot_nn(part, before) + count)
        count = count + jnp.sum(part.astype(F32), axis=1, keepdims=True)
    most_ref[...] = jnp.broadcast_to(jnp.max(count, axis=0, keepdims=True).astype(I32), most_ref.shape)
    line = iota((total, 1), 0)
    to, of = line // n_dev, line % n_dev
    rank = jnp.concatenate(ranks, axis=1)
    turn = ((rank + 0.5) * (1.0 / room)).astype(I32)
    inside = rank.astype(I32) + turn * ((n_dev - 1) * room)
    arrives = jnp.sum(
        jnp.where(member & (to == me), inside + got_at(of ^ to) * room, 0), axis=0, keepdims=True
    )
    leaves = inside + sent_at(of ^ to) * room
    half = owned // LANES
    found = jnp.zeros((2 * half, LANES), F32)
    high, lanes = iota((half, owned), 0), iota((LANES, owned), 0)
    for t in range(n_dev):
        mine = slice(t * n_dev, (t + 1) * n_dev)
        chosen = member[mine] & (of[mine] == me)
        place = jnp.sum(jnp.where(chosen, leaves[mine], 0), axis=0, keepdims=True)
        hit = (spot[t : t + 1, :] // LANES == high) & (source[t : t + 1, :] == me)
        left = jnp.concatenate(
            [jnp.where(hit, place // LANES, 0), jnp.where(hit, place % LANES, 0)], axis=0
        ).astype(F32).astype(BF16)
        found = found + dot_nt(left, as_bf16((spot[t : t + 1, :] % LANES) == lanes))
    found = found[:half] * float(LANES) + found[half:]
    leave_row = jnp.concatenate([found[a : a + 1, :] for a in range(half)], axis=1)
    rows = jnp.concatenate([leave_row, arrives.astype(F32), jnp.zeros((6, owned), F32)], axis=0)
    row_ref[...] = rows.astype(I32)
    col_ref[...] = jnp.transpose(rows).astype(I32)


LEAVES, ARRIVES = 0, 1


def put_rows(line, base_ref, pos_ref, held, outs, tile):
    wanted = pos_ref[line : line + 1, :] - base_ref[0]
    base = 0
    for out in outs:
        for at in range(0, out.shape[0], tile):
            picks = as_bf16(iota((tile, held.shape[0]), 0) + (base + at) == wanted)
            out[at : at + tile, :] = dot_nn(picks, held[...]).astype(BF16)
        base += out.shape[0]


def put_body(line, tile, base_ref, pos_ref, rows_ref, *outs):
    put_rows(line, base_ref, pos_ref, rows_ref, outs, tile)


def sum_put_body(line, tile, n_in, base_ref, pos_ref, mine_ref, *refs):
    others, outs, held = refs[:n_in], refs[n_in:-1], refs[-1]
    gather_pieces(others, held)
    held[...] = total_f32(mine_ref[...], held[...]).astype(BF16)
    put_rows(line, base_ref, pos_ref, held, outs, tile)


def take_body(line, tile, base_ref, pos_ref, *refs):
    pieces, out, held = refs[:-2], refs[-2], refs[-1]
    gather_pieces(pieces, held)
    for at in range(0, out.shape[0], tile):
        wanted = pos_ref[at : at + tile, line : line + 1] - base_ref[0]
        picks = as_bf16(iota((tile, held.shape[0]), 1) == wanted)
        out[at : at + tile, :] = dot_nn(picks, held[...]).astype(BF16)


def take_more_body(line, tile, base_ref, pos_ref, *refs):
    pieces, more, out, held = refs[:-3], refs[-3], refs[-2], refs[-1]
    gather_pieces(pieces, held)
    for at in range(0, out.shape[0], tile):
        wanted = pos_ref[at : at + tile, line : line + 1] - base_ref[0]
        picks = as_bf16(iota((tile, held.shape[0]), 1) == wanted)
        out[at : at + tile, :] = (dot_nn(picks, held[...]) + more[at : at + tile, :].astype(F32)).astype(BF16)


def adam_body(n_in, pos_ref, *refs):
    pieces = refs[:n_in]
    more_ref, first_ref, second_ref, weight_ref, grad_ref, first_new, second_new, weight_new, held = refs[n_in:]

    @pl.when(pl.program_id(0) == 0)
    def _():
        gather_pieces(pieces, held)

    picks = as_bf16(iota((grad_ref.shape[0], held.shape[0]), 1) == pos_ref[:, LEAVES : LEAVES + 1])
    grad = dot_nn(picks, held[...]) + more_ref[...].astype(F32)
    grad_ref[...] = grad
    made = adam_update(grad, first_ref[...], second_ref[...], weight_ref[...].astype(F32))
    first_new[...], second_new[...], weight_new[...] = made


def mixture_body(result_ref, pos_ref, ids_ref, prob_ref, residual_ref, out_ref):
    toks = residual_ref.shape[0]
    slots = result_ref.shape[0]
    share = prob_ref[...]
    total = residual_ref[...]
    for number in range(2):
        picks = as_bf16(iota((toks, slots), 1) == pos_ref[:, number : number + 1])
        mine = iota(share.shape, 1) == ids_ref[:, number : number + 1]
        gate = jnp.sum(jnp.where(mine, share, 0.0), axis=-1, keepdims=True)
        total = total + gate * dot_nn(picks, result_ref[...])
    out_ref[...] = total.astype(BF16)


SWAP = [(0, 1), (1, 0)]
SWAP_CORE = [(0, 1), (1, 0), (2, 3), (3, 2)]
SWAP_Y = [(0, 2), (2, 0), (1, 3), (3, 1)]


def swap_x(value):
    return lax.ppermute(value, "ctx", SWAP)


def swap_y(value):
    return lax.ppermute(value, "dp", SWAP_Y)


def swap_x_y(value):
    return lax.ppermute(value, ("dp", "ctx"), [(i, i ^ 5) for i in range(8)])


def swap_core(value):
    return lax.ppermute(value, "dp", SWAP_CORE)


def shift_z(value, by):
    count = lax.axis_size("expert")
    return lax.ppermute(value, "expert", [(i, (i + by) % count) for i in range(count)])


def after(values, *others):
    values = list(values)
    return lax.optimization_barrier((*values, *others))[: len(values)]


def total_f32(first, second):
    return first.astype(F32) + second.astype(F32)


def on_chip_experts(
    tokens, cotangent, pad_mask, expert_ids, slot_priority, shared_slots, shared_first, shared_second,
    shared_owner, expert_slots, expert_first, expert_second, expert_owner,
):
    toks, width = tokens.shape[1], tokens.shape[2]
    n_z = lax.axis_size("expert")
    n_exp = EXP_DEV * n_z
    capacity = (10 * toks + 4 * n_exp - 1) // (4 * n_exp)
    slots = n_exp * capacity
    everyone = ("dp", "ctx", "expert")
    dp, mx, mz = lax.axis_index("dp"), lax.axis_index("ctx"), lax.axis_index("expert")
    my, mc = dp // 2, dp % 2

    own_count = shared_slots.shape[0]
    stride = -(-own_count // 8) * 8
    padded = jnp.pad(shared_slots, ((0, stride - own_count), (0, 0)))
    line = [padded] + [shift_z(padded, by) for by in range(1, n_z)]
    part_a = jnp.concatenate(line[: n_z // 2], axis=0)
    part_b = jnp.concatenate(line[n_z // 2 :], axis=0)
    a_y, b_x = swap_y(part_a), swap_x(part_b)
    pair_a, pair_b = jnp.concatenate([part_a, a_y], axis=0), jnp.concatenate([part_b, b_x], axis=0)
    first_near, last_near = [pair_a, pair_b], [swap_x(pair_a), swap_y(pair_b)]
    first_far = [swap_core(piece) for piece in first_near]
    last_far = [swap_core(piece) for piece in last_near]

    owner_dev, owner_row = shared_owner // own_count, shared_owner % own_count
    o_z, o_x, o_dp = owner_dev % n_z, owner_dev // n_z % 2, owner_dev // (n_z * 2)
    in_c, in_y, in_x = (o_dp % 2) ^ mc, (o_dp // 2) ^ my, o_x ^ mx
    in_z = (mz - o_z + n_z) % n_z
    late = in_z // (n_z // 2)
    cross = jnp.where(late == 0, in_y + 2 * in_x, in_x + 2 * in_y)
    place = (((in_c * 2 + late) * 4 + cross) * (n_z // 2) + in_z % (n_z // 2)) * stride + owner_row
    total_slots = 8 * n_z * stride
    row_count = -(-shared_owner.shape[0] // 16) * 16
    place_col = jnp.pad(place, (0, row_count - place.shape[0]), constant_values=-1)[:, None]
    gain_at = 4 * width + n_exp
    none = jnp.full((15,), -1, I32)
    place_row = jnp.concatenate(
        [place[: 3 * width], place[gain_at : gain_at + 1], none, place[3 * width : gain_at], place[gain_at + 1 :], none]
    )[None, :]

    own, other = tokens[0], swap_x(after([tokens[0]], *last_near)[0])
    ids = expert_ids[0]
    live = pad_mask.astype(F32)
    live_other = swap_x(pad_mask).astype(F32)
    keep_row = jnp.concatenate([live, live_other], axis=1)
    keep_col = live.reshape(toks, 1)
    pos_row, pos_col, cot_sent = kernel_call(
        functools.partial(route_body, n_exp, capacity),
        (sds((8, toks), I32), sds((toks, 8), I32), sds((slots, width), BF16)),
        cost=(4 * MICRO, 1e6),
    )(ids.T, slot_priority.astype(F32), live, cotangent[0])

    def exchange(rows):
        return lax.all_to_all(rows, everyone, split_axis=0, concat_axis=0, tiled=True)

    cot_got = exchange(after([cot_sent], part_a, part_b)[0])

    local = my * 2 + mx
    group, n_dev = dp * 2 + mx, 8
    owned = expert_slots.shape[1]
    room = room_of(owned, n_dev)
    owner = jnp.transpose(
        expert_owner[0].reshape(2, 2, 2, 2, FF // 2), (0, 3, 1, 2, 4)
    ).reshape(n_dev, owned)
    held = [pltpu.VMEM((n_dev * room, width), BF16)]
    sent_shapes, got_shapes = [sds((4 * room, width), BF16)] * 2, [sds((2 * room, width), BF16)] * 4
    smem, vmem = pl.BlockSpec(memory_space=pltpu.SMEM), pl.BlockSpec(memory_space=pltpu.VMEM)
    plan_row, plan_col, most = kernel_call(
        functools.partial(plan_body, n_dev, room),
        (sds((8, owned), I32), sds((owned, 8), I32), sds((8, LANES), I32)), cost=(5 * MICRO, 1e6),
        in_specs=[smem, vmem],
    )(group.astype(I32).reshape(1), *after([owner], pos_row))
    rounds = (most[0, 0] + room - 1) // room
    swaps = (swap_x, swap_y, swap_x_y)

    def with_base(body, out_shape, scratch, arrays, number=0):
        base = jnp.full((1,), number * n_dev * room, I32)
        return kernel_call(
            body, out_shape, scratch, in_specs=[smem] + [vmem] * len(arrays), cost=(8 * MICRO, 1e6)
        )(base, *arrays)

    def send_pieces(near, far):
        got = [near[:room], far[:room]]
        for by, swap in enumerate(swaps, 1):
            rows = slice(by * room, (by + 1) * room)
            got.append(swap(jnp.concatenate([near[rows], far[rows]], axis=0)))
        return got

    def return_near(pieces, *others):
        x, y, x_y = after(pieces[1:], *others) if others else pieces[1:]
        return [pieces[0], swap_x(x), swap_y(pieces[2]), swap_x_y(x_y)]

    def return_far(got):
        near = [piece[:room] for piece in got]
        return [*near, swap_core(jnp.concatenate([piece[room:] for piece in got], axis=0))]

    put_leaving = functools.partial(put_body, LEAVES, room)
    take_tile = 256 if owned % 256 == 0 else owned
    take_more = functools.partial(take_body, ARRIVES, take_tile)

    def more_weights(number, total):
        near, far = with_base(put_leaving, sent_shapes, (), [plan_row, expert_slots[0]], number)
        moved = send_pieces(near, swap_core(far))
        part = with_base(take_more, sds((owned, width), BF16), held, [plan_col, *moved], number)
        return total + part

    more_rows = lax.fori_loop(1, rounds, more_weights, jnp.zeros((owned, width), BF16))
    near, far = with_base(put_leaving, sent_shapes, (), [*after([plan_row], part_a, part_b, more_rows), expert_slots[0]])
    near_sent, far_sent = after([near, far], *last_near)
    far_sent = swap_core(far_sent)
    moved = send_pieces(*after([near_sent, far_sent], other))

    half_slots = total_slots // 2
    piece = half_slots // 4
    row_tile = row_count // 5 if row_count % 80 == 0 else row_count

    def unpack(spots, pieces, earlier):
        rows_of = lambda columns: pl.BlockSpec((row_tile, columns), lambda i: (i, 0))
        return kernel_call(
            functools.partial(unpack_body, spots, len(earlier)), sds((row_count, width), BF16),
            [pltpu.VMEM((len(pieces) * piece, width), BF16)],
            grid=(row_count // row_tile,),
            in_specs=[rows_of(1)] + [pl.BlockSpec((piece, width), lambda i: (0, 0))] * len(pieces)
            + [rows_of(width)] * len(earlier),
            out_specs=rows_of(width),
            cost=(7 * MICRO, 1e6),
        )(place_col, *pieces, *earlier)

    first_rows = unpack(
        [0, 2 * piece, half_slots, half_slots + 2 * piece], [*after(first_near, near), *first_far], []
    )
    near_rows = unpack([piece, 3 * piece], last_near, [first_rows])
    weights = unpack([half_slots + piece, half_slots + 3 * piece], last_far, [near_rows])

    (qkv, normed, attended, residual, prob, sent, lse_col, lse_row) = kernel_call(
        functools.partial(forward_body, n_exp),
        (
            sds((2 * toks, 3 * width), BF16), sds((toks, width), BF16), sds((toks, width), F32),
            sds((toks, width), F32), sds((toks, n_exp), F32), sds((slots, width), BF16),
            sds((toks, LANES), F32), sds((8, toks), F32),
        ),
        [pltpu.VMEM((toks, width), BF16)],
        cost=(13 * MICRO, 1e6),
    )(own, other, keep_row, weights, pos_row)
    got = exchange(sent)
    near_weights = with_base(
        functools.partial(take_more_body, ARRIVES, take_tile), sds((owned, width), BF16), held,
        [*after([plan_col], sent), *moved, more_rows],
    )

    far_weights = [swap_core(near_weights[: FF // 2]), swap_core(near_weights[FF // 2 :])]

    expert_id = (mz * EXP_DEV + local).astype(I32).reshape(1)
    tile = 256 if slots % 256 == 0 else slots
    router_rows = weights[4 * width : 4 * width + n_exp]
    whole = lambda shape: pl.BlockSpec(shape, lambda i: (0, 0))
    rows_of = lambda columns: pl.BlockSpec((tile, columns), lambda i: (i, 0))
    active, hidden, scaled, result, back, router_grad = kernel_call(
        functools.partial(expert_body, n_exp),
        (
            sds((slots, FF), BF16), sds((slots, FF), BF16), sds((slots, width), BF16),
            sds((slots, width), BF16), sds((slots, width), BF16), sds((n_exp, width), F32),
        ),
        grid=(slots // tile,),
        in_specs=[
            pl.BlockSpec(memory_space=pltpu.SMEM), rows_of(width), rows_of(width),
            whole((FF, width)), whole((FF // 2, width)), whole((FF // 2, width)), whole((n_exp, width)),
        ],
        out_specs=(
            rows_of(FF), rows_of(FF), rows_of(width), rows_of(width), rows_of(width), whole((n_exp, width)),
        ),
        cost=(19 * MICRO, 1e6),
    )(expert_id, got, cot_got, near_weights, *far_weights, router_rows)
    back_got = exchange(back)

    mine, *theirs = kernel_call(
        weight_grad_body, [sds((FF, width), F32)] + [sds((FF // THEIRS, width), BF16)] * THEIRS, cost=(10 * MICRO, 1e7)
    )(hidden, active, got, scaled)
    theirs_got = [swap_core(part) for part in theirs]
    put_returning = functools.partial(sum_put_body, ARRIVES, room, THEIRS)
    held_owned = [pltpu.VMEM((owned, width), BF16)]
    moved = with_base(put_returning, got_shapes, held_owned, [plan_row, mine, *theirs_got])
    back_got, *moved = after([back_got, *moved])

    def more_grads(number, total):
        parts = with_base(put_returning, got_shapes, held_owned, [plan_row, mine, *theirs_got], number)
        parts = return_far(return_near(parts))
        take = functools.partial(take_body, LEAVES, take_tile)
        return total + with_base(take, sds((owned, width), BF16), held, [plan_col, *parts], number)

    more = lax.fori_loop(1, rounds, more_grads, after([jnp.zeros((owned, width), BF16)], back_got)[0])
    grad_residual, out_grad, delta_col, delta_row, gain_two = kernel_call(
        functools.partial(middle_body, n_exp),
        (
            sds((toks, width), F32), sds((toks, width), BF16), sds((toks, LANES), F32),
            sds((8, toks), F32), sds((8, width), F32),
        ),
        cost=(6 * MICRO, 1e6),
    )(back_got, pos_col, residual, cotangent[0], keep_col, attended, weights)
    out_grad_other = swap_x(out_grad)
    sums_other = swap_x(jnp.concatenate([lse_row, delta_row], axis=0))
    moved = return_near(moved, out_grad_other)
    result_got = exchange(after([result], out_grad_other, more)[0])
    query_grad, kv_grad, early = kernel_call(
        functools.partial(inner_body, n_exp),
        (sds((toks, width), BF16), sds((2, toks, width), F32), sds((width + n_exp + 16, width), BF16)),
        cost=(15 * MICRO, 1e6),
    )(qkv, out_grad, lse_col, delta_col, keep_row, attended, grad_residual, router_grad, gain_two)
    early_far = swap_core(early)
    late, grad_normed = kernel_call(
        functools.partial(outer_body, n_exp),
        (sds((3 * width + 16, width), BF16), sds((toks, width), F32)),
        [pltpu.VMEM((toks, 3 * width), BF16)],
        cost=(12 * MICRO, 1e6),
    )(
        qkv, *after([out_grad_other], moved[2]), sums_other, keep_col, query_grad, kv_grad, normed, own, weights,
    )
    late_far = swap_core(late)
    grad_tokens = kernel_call(
        functools.partial(tokens_body, n_exp), sds((toks, width), F32), cost=(2 * MICRO, 4e6)
    )(grad_normed, own, weights, grad_residual)
    quarter = half_slots // 2
    eighth, sixteenth = quarter // 2, quarter // 4
    count = place_row.shape[1]

    def spread(starts, *others):
        return kernel_call(
            functools.partial(spread_body, starts), sds((2, eighth, width), BF16),
            [pltpu.VMEM((count, width), BF16)], cost=(6 * MICRO, 1e6),
        )(*after([place_row], *others), late, late_far, early, early_far)

    sends = spread((eighth, quarter + eighth))
    got_a, got_b = swap_x(sends[0]), swap_y(sends[1])
    keeps = spread((0, quarter), sends)
    moved = return_far(after(moved, keeps))

    tile = 256 if owned % 256 == 0 else owned
    rows_of = lambda columns: pl.BlockSpec((tile, columns), lambda i: (i, 0))
    expert_new = kernel_call(
        functools.partial(adam_body, len(moved)), [sds((owned, width), F32)] * 4, held,
        grid=(owned // tile,),
        in_specs=[rows_of(8)] + [pl.BlockSpec(piece.shape, lambda i: (0, 0)) for piece in moved] + [rows_of(width)] * 4,
        out_specs=[rows_of(width)] * 4,
        cost=(14 * MICRO, 3e7),
    )(plan_col, *moved, more, expert_first[0], expert_second[0], expert_slots[0])

    sum_a = total_f32(keeps[0], got_a).astype(BF16)
    sum_b = total_f32(keeps[1], got_b).astype(BF16)
    got_a, got_b = swap_y(sum_a[sixteenth:]), swap_x(sum_b[sixteenth:])
    sum_a = total_f32(sum_a[:sixteenth], got_a).astype(BF16)
    sum_b = total_f32(sum_b[:sixteenth], got_b).astype(BF16)
    lines = [sum_a[i * stride : (i + 1) * stride] for i in range(n_z // 2)]
    lines += [sum_b[i * stride : (i + 1) * stride] for i in range(n_z // 2)]
    shared_grad = lines[0].astype(F32)
    for by in range(1, n_z):
        shared_grad = shared_grad + shift_z(lines[by], n_z - by).astype(F32)
    shared_grad = shared_grad[:own_count]

    output = kernel_call(
        mixture_body, sds((toks, width), BF16), cost=(4 * slots * toks * width, 4e6)
    )(result_got, pos_col, ids, prob, residual)

    shared_new = adam_update(shared_grad, shared_first, shared_second, shared_slots.astype(F32))
    return (
        output[None], grad_tokens[None], shared_grad, *shared_new,
        *(value[None] for value in expert_new),
    )


def solution(mesh):
    sizes = mesh.shape
    chip_experts = (sizes["dp"], sizes["ctx"], sizes["expert"]) == (4, 2, 4)
    return jax.shard_map(
        on_chip_experts if chip_experts else on_device,
        mesh=mesh,
        in_specs=(
            P(("dp", "expert"), "ctx", None),
            P(("dp", "expert"), "ctx", None),
            P(("dp", "expert"), "ctx"),
            P(("dp", "expert"), "ctx", None),
            P(("dp", "expert"), "ctx"),
            P(("dp", "ctx", "expert"), None),
            P(("dp", "ctx", "expert"), None),
            P(("dp", "ctx", "expert"), None),
            P(),
            P("expert", ("dp", "ctx"), None),
            P("expert", ("dp", "ctx"), None),
            P("expert", ("dp", "ctx"), None),
            P("expert", None),
        ),
        out_specs=(
            P(("dp", "expert"), "ctx", None),
            P(("dp", "expert"), "ctx", None),
            P(("dp", "ctx", "expert"), None),
            P(("dp", "ctx", "expert"), None),
            P(("dp", "ctx", "expert"), None),
            P(("dp", "ctx", "expert"), None),
            P("expert", ("dp", "ctx"), None),
            P("expert", ("dp", "ctx"), None),
            P("expert", ("dp", "ctx"), None),
            P("expert", ("dp", "ctx"), None),
        ),
        check_vma=False,
    )
```

```python
import functools
import math

import jax
import jax.numpy as jnp
from jax import lax
from jax.experimental import pallas as pl
from jax.experimental.pallas import tpu as pltpu
from jax.sharding import PartitionSpec as P

HEADS = 8
HEAD_DIM = 64
FF = 2048
EXP_DEV = 4


MASKED_SCORE = -1e30
MOMENT_DECAY = 0.5
LEARN_RATE = 0.05
WEIGHT_DECAY = 0.1
EPSILON = 1e-08
NORM_EPSILON = 1e-06


def layer_norm(values, gain_rows):
    center = values - jnp.mean(values, axis=-1, keepdims=True)
    spread = jnp.mean(center * center, axis=-1, keepdims=True)
    return center * lax.rsqrt(spread + NORM_EPSILON) * gain_rows


def routing(chosen, priority, live_rows, expert_count, capacity):
    tok_count = chosen.shape[0]
    token_ids = jnp.arange(tok_count, dtype=jnp.int32)
    ranking = jnp.argsort(priority * tok_count + token_ids)
    labels = jnp.arange(expert_count, dtype=jnp.int32)
    wanted = jnp.any(chosen[:, :, None] == labels[None, None, :], axis=1) & (
        live_rows[:, None] == 1
    )
    wanted = wanted.astype(jnp.int32)
    ranked = wanted[ranking]
    before = jnp.cumsum(ranked, axis=0) - ranked
    position = jnp.zeros_like(before).at[ranking].set(before)
    slot_taken = jnp.take_along_axis(position, chosen, axis=1)
    kept_pair = (slot_taken < capacity) & (live_rows[:, None] == 1)
    target = jnp.where(kept_pair, chosen * capacity + slot_taken, expert_count * capacity)
    owners = jnp.broadcast_to(token_ids[:, None], chosen.shape)
    source = (
        jnp.zeros((expert_count * capacity,), jnp.int32)
        .at[target.reshape(-1)]
        .set(owners.reshape(-1), mode="drop")
    )
    filled = (
        jnp.zeros((expert_count * capacity,), jnp.int32).at[target.reshape(-1)].set(1, mode="drop")
    )
    slot_index = jnp.where(kept_pair, chosen * capacity + slot_taken, 0)
    return (slot_index, kept_pair.astype(jnp.int32), source, filled)


def head_view(values):
    return values.reshape(values.shape[0], values.shape[1], HEADS, HEAD_DIM)


def score_block(queries, key_rows, keep_mask):
    score = jnp.einsum(
        "iqhe,ikhe->ihqk", queries, head_view(key_rows), preferred_element_type=jnp.float32
    ) * HEAD_DIM ** (-0.5)
    return jnp.where(keep_mask[:, None, None, :] > 0, score, MASKED_SCORE)


def stats_step(running, portion, queries):
    row_max, row_sum = running
    key_rows, keep_mask = portion
    score = score_block(queries, key_rows, keep_mask)
    keep_wide = keep_mask.astype(jnp.float32)[:, None, None, :]
    new_max = jnp.maximum(row_max, jnp.max(score, axis=-1))
    row_sum = row_sum * jnp.exp(row_max - new_max) + jnp.sum(
        jnp.exp(score - new_max[..., None]) * keep_wide, axis=-1
    )
    return (new_max, row_sum)


def value_step(running, portion, queries, log_sum):
    key_rows, value_rows, keep_mask = portion
    score = score_block(queries, key_rows, keep_mask)
    keep_wide = keep_mask.astype(jnp.float32)[:, None, None, :]
    attn_prob = (jnp.exp(score - log_sum[..., None]) * keep_wide).astype(jnp.bfloat16)
    return running + jnp.einsum(
        "ihqk,ikhe->iqhe", attn_prob, head_view(value_rows), preferred_element_type=jnp.float32
    )


def grad_step(grad_query, portion, queries, log_sum, grad_out, row_delta):
    key_rows, value_rows, keep_mask = portion
    score = score_block(queries, key_rows, keep_mask)
    keep_wide = keep_mask.astype(jnp.float32)[:, None, None, :]
    attn_prob = jnp.exp(score - log_sum[..., None]) * keep_wide
    prob_low = attn_prob.astype(jnp.bfloat16)
    grad_value = jnp.einsum(
        "ihqk,iqhe->ikhe", prob_low, grad_out, preferred_element_type=jnp.float32
    )
    grad_prob = jnp.einsum(
        "iqhe,ikhe->ihqk", grad_out, head_view(value_rows), preferred_element_type=jnp.float32
    )
    grad_score = (attn_prob * (grad_prob - row_delta[..., None])).astype(jnp.bfloat16)
    score_scale = HEAD_DIM ** (-0.5)
    grad_query = (
        grad_query
        + jnp.einsum(
            "ihqk,ikhe->iqhe", grad_score, head_view(key_rows), preferred_element_type=jnp.float32
        )
        * score_scale
    )
    grad_key = (
        jnp.einsum("ihqk,iqhe->ikhe", grad_score, queries, preferred_element_type=jnp.float32)
        * score_scale
    )
    return (grad_query, jnp.stack([grad_key, grad_value]))


def each_block(step_fn, running, arrays, block_len):
    total_len = arrays[0].shape[1]
    size_rows = math.gcd(total_len, block_len)

    def one_turn(number, current):
        offset = number * size_rows
        portion = tuple(
            (lax.dynamic_slice_in_dim(member, offset, size_rows, 1) for member in arrays)
        )
        return step_fn(current, portion)

    return lax.fori_loop(0, total_len // size_rows, one_turn, running)


def adam_update(gradient, first_old, second_old, weight):
    first_new = MOMENT_DECAY * first_old + (1.0 - MOMENT_DECAY) * gradient
    second_new = MOMENT_DECAY * second_old + (1.0 - MOMENT_DECAY) * gradient * gradient
    weight_new = weight - LEARN_RATE * (
        first_new / (jnp.sqrt(second_new) + EPSILON) + WEIGHT_DECAY * weight
    )
    return (first_new, second_new, weight_new)


def on_device(
    tokens,
    cotangent,
    pad_mask,
    expert_ids,
    slot_priority,
    shared_slots,
    shared_first,
    shared_second,
    shared_owner,
    expert_slots,
    expert_first,
    expert_second,
    expert_owner,
):
    img_count, part_len, features = tokens.shape
    tok_count = img_count * part_len
    expert_count = EXP_DEV * lax.axis_size("expert")
    capacity = (10 * tok_count + 4 * expert_count - 1) // (4 * expert_count)
    all_shared = lax.all_gather(shared_slots, ("dp", "ctx", "expert"), axis=0, tiled=True)
    all_expert = lax.all_gather(expert_slots, ("dp", "ctx"), axis=1, tiled=True)
    pieces = all_shared[shared_owner]
    w_qkv = pieces[: 3 * features]
    w_attn_out = pieces[3 * features : 4 * features]
    w_router = pieces[4 * features : 4 * features + expert_count]
    gain_one = pieces[4 * features + expert_count].astype(jnp.float32)
    gain_two = pieces[4 * features + expert_count + 1].astype(jnp.float32)
    expert_rows = all_expert[0][expert_owner[0]].reshape(EXP_DEV, 2, FF, features)
    w_in = expert_rows[:, 0]
    w_out = expert_rows[:, 1]
    inputs = tokens.reshape(tok_count, features).astype(jnp.float32)
    keep_mask = pad_mask.astype(jnp.bfloat16)
    keep_rows = pad_mask.reshape(tok_count).astype(jnp.float32)
    normed_one, norm_one_back = jax.vjp(layer_norm, inputs, gain_one)
    normed_low = normed_one.astype(jnp.bfloat16)
    qkv_rows = lax.dot_general(
        normed_low, w_qkv, (((1,), (1,)), ((), ())), preferred_element_type=jnp.float32
    ).astype(jnp.bfloat16)
    query_rows = qkv_rows[:, :features].reshape(img_count, part_len, features)
    key_rows = qkv_rows[:, features : 2 * features].reshape(img_count, part_len, features)
    value_rows = qkv_rows[:, 2 * features :].reshape(img_count, part_len, features)
    queries = head_view(query_rows)
    start_max = jnp.full((img_count, HEADS, part_len), MASKED_SCORE, jnp.float32)
    start_sum = jnp.zeros((img_count, HEADS, part_len), jnp.float32)
    start_out = jnp.zeros((img_count, part_len, HEADS, HEAD_DIM), jnp.float32)
    whole_keys, whole_values, whole_keep = (
        lax.all_gather(key_rows, "ctx", axis=1, tiled=True),
        lax.all_gather(value_rows, "ctx", axis=1, tiled=True),
        lax.all_gather(keep_mask, "ctx", axis=1, tiled=True),
    )
    row_max, row_sum = each_block(
        lambda running, portion: stats_step(running, portion, queries),
        (start_max, start_sum),
        (whole_keys, whole_keep),
        part_len,
    )
    log_sum = row_max + jnp.log(row_sum)
    attended = each_block(
        lambda running, portion: value_step(running, portion, queries, log_sum),
        start_out,
        (whole_keys, whole_values, whole_keep),
        part_len,
    )
    attended_low = attended.reshape(tok_count, features).astype(jnp.bfloat16)
    branch = jnp.dot(attended_low, w_attn_out, preferred_element_type=jnp.float32)
    residual = inputs + branch
    normed_two, norm_two_back = jax.vjp(layer_norm, residual, gain_two)
    mixed_low = normed_two.astype(jnp.bfloat16)
    logits = lax.dot_general(
        mixed_low, w_router, (((1,), (1,)), ((), ())), preferred_element_type=jnp.float32
    )
    router_prob = jax.nn.softmax(logits, axis=-1)
    chosen = expert_ids.reshape(tok_count, 2)
    slot_index, kept_pair, source, filled = routing(
        chosen,
        slot_priority.reshape(tok_count),
        pad_mask.reshape(tok_count),
        expert_count,
        capacity,
    )
    filled_low = filled.astype(jnp.bfloat16)
    dispatched = (mixed_low[source] * filled_low[:, None]).reshape(expert_count, capacity, features)
    received = lax.all_to_all(dispatched, "expert", split_axis=0, concat_axis=1, tiled=True)
    hidden = jnp.einsum("ecd,efd->ecf", received, w_in, preferred_element_type=jnp.float32)
    active, gelu_back = jax.vjp(lambda pre_act: jax.nn.gelu(pre_act, approximate=False), hidden)
    active_low = active.astype(jnp.bfloat16)
    result = jnp.einsum(
        "ecf,efd->ecd", active_low, w_out, preferred_element_type=jnp.float32
    ).astype(jnp.bfloat16)
    returned = lax.all_to_all(result, "expert", split_axis=1, concat_axis=0, tiled=True).reshape(
        expert_count * capacity, features
    )
    kept_float = kept_pair.astype(jnp.float32)
    gate_value = jnp.take_along_axis(router_prob, chosen, axis=1) * kept_float
    picked = returned[slot_index].astype(jnp.float32)
    mixture = jnp.sum(gate_value[:, :, None] * picked, axis=1)
    output = (residual + mixture).astype(jnp.bfloat16).reshape(tokens.shape)
    grad_rows = cotangent.reshape(tok_count, features).astype(jnp.float32) * keep_rows[:, None]
    grad_gate = jnp.sum(grad_rows[:, None, :] * picked, axis=-1) * kept_float
    labels = jnp.arange(expert_count, dtype=jnp.int32)
    grad_prob = jnp.sum(
        (chosen[:, :, None] == labels[None, None, :]).astype(jnp.float32) * grad_gate[:, :, None],
        axis=1,
    )
    grad_logits = router_prob * (
        grad_prob - jnp.sum(grad_prob * router_prob, axis=-1, keepdims=True)
    )
    grad_logits_low = grad_logits.astype(jnp.bfloat16)
    slot_expert = jnp.arange(expert_count * capacity, dtype=jnp.int32) // capacity
    slot_gate = jnp.take_along_axis(router_prob[source], slot_expert[:, None], axis=1)[
        :, 0
    ] * filled.astype(jnp.float32)
    grad_result = (
        (grad_rows[source] * slot_gate[:, None])
        .astype(jnp.bfloat16)
        .reshape(expert_count, capacity, features)
    )
    grad_received = lax.all_to_all(grad_result, "expert", split_axis=0, concat_axis=1, tiled=True)
    grad_active = jnp.einsum(
        "ecd,efd->ecf", grad_received, w_out, preferred_element_type=jnp.float32
    )
    grad_hidden = gelu_back(grad_active)[0].astype(jnp.bfloat16)
    grad_w_out = jnp.einsum(
        "ecf,ecd->efd", active_low, grad_received, preferred_element_type=jnp.float32
    )
    grad_w_in = jnp.einsum(
        "ecf,ecd->efd", grad_hidden, received, preferred_element_type=jnp.float32
    )
    grad_sent = jnp.einsum(
        "ecf,efd->ecd", grad_hidden, w_in, preferred_element_type=jnp.float32
    ).astype(jnp.bfloat16)
    grad_back = lax.all_to_all(
        grad_sent, "expert", split_axis=1, concat_axis=0, tiled=True
    ).reshape(expert_count * capacity, features)
    grad_mixed = jnp.sum(grad_back[slot_index].astype(jnp.float32) * kept_float[:, :, None], axis=1)
    grad_mixed = grad_mixed + jnp.dot(grad_logits_low, w_router, preferred_element_type=jnp.float32)
    grad_router = lax.dot_general(
        grad_logits_low, mixed_low, (((0,), (0,)), ((), ())), preferred_element_type=jnp.float32
    )
    grad_residual_part, grad_gain_two = norm_two_back(grad_mixed)
    grad_residual = grad_rows + grad_residual_part
    grad_branch = grad_residual.astype(jnp.bfloat16)
    grad_w_attn_out = lax.dot_general(
        attended_low, grad_branch, (((0,), (0,)), ((), ())), preferred_element_type=jnp.float32
    )
    grad_attended = lax.dot_general(
        grad_branch, w_attn_out, (((1,), (1,)), ((), ())), preferred_element_type=jnp.float32
    ).astype(jnp.bfloat16)
    grad_out = head_view(grad_attended.reshape(img_count, part_len, features))
    row_delta = jnp.transpose(jnp.sum(grad_out.astype(jnp.float32) * attended, axis=-1), (0, 2, 1))
    start_grad = jnp.zeros((img_count, part_len, HEADS, HEAD_DIM), jnp.float32)
    whole_grads = jnp.zeros((2, img_count, whole_keys.shape[1], HEADS, HEAD_DIM), jnp.float32)

    def grad_turn(number, current):
        grad_query, grads_all = current
        offset = number * part_len
        portion = tuple(
            (
                lax.dynamic_slice_in_dim(member, offset, part_len, 1)
                for member in (whole_keys, whole_values, whole_keep)
            )
        )
        grad_query, grad_block = grad_step(
            grad_query, portion, queries, log_sum, grad_out, row_delta
        )
        grads_all = lax.dynamic_update_slice_in_dim(grads_all, grad_block, offset, 2)
        return (grad_query, grads_all)

    grad_query, whole_grads = lax.fori_loop(
        0, whole_keys.shape[1] // part_len, grad_turn, (start_grad, whole_grads)
    )
    grad_pair = lax.psum_scatter(whole_grads, "ctx", scatter_dimension=2, tiled=True)
    grad_qkv = jnp.concatenate(
        [
            grad_query.reshape(tok_count, features),
            grad_pair[0].reshape(tok_count, features),
            grad_pair[1].reshape(tok_count, features),
        ],
        axis=1,
    ).astype(jnp.bfloat16)
    grad_w_qkv = lax.dot_general(
        grad_qkv, normed_low, (((0,), (0,)), ((), ())), preferred_element_type=jnp.float32
    )
    grad_normed = jnp.dot(grad_qkv, w_qkv, preferred_element_type=jnp.float32)
    grad_input_part, grad_gain_one = norm_one_back(grad_normed)
    grad_tokens = (grad_residual + grad_input_part).reshape(tokens.shape)
    shared_pieces = jnp.concatenate(
        [grad_w_qkv, grad_w_attn_out, grad_router, grad_gain_one[None, :], grad_gain_two[None, :]],
        axis=0,
    )
    shared_layout = jnp.zeros(all_shared.shape, jnp.float32).at[shared_owner].set(shared_pieces)
    shared_grad = lax.psum_scatter(
        shared_layout, ("dp", "ctx", "expert"), scatter_dimension=0, tiled=True
    )
    expert_pieces = jnp.stack([grad_w_in, grad_w_out], axis=1).reshape(EXP_DEV * 2 * FF, features)
    expert_layout = (
        jnp.zeros(all_expert.shape, jnp.float32).at[0, expert_owner[0]].set(expert_pieces)
    )
    expert_grad = lax.psum_scatter(expert_layout, ("dp", "ctx"), scatter_dimension=1, tiled=True)
    shared_first_new, shared_second_new, shared_weight_new = adam_update(
        shared_grad, shared_first, shared_second, shared_slots.astype(jnp.float32)
    )
    expert_first_new, expert_second_new, expert_weight_new = adam_update(
        expert_grad, expert_first, expert_second, expert_slots.astype(jnp.float32)
    )
    return (
        output,
        grad_tokens,
        shared_grad,
        shared_first_new,
        shared_second_new,
        shared_weight_new,
        expert_grad,
        expert_first_new,
        expert_second_new,
        expert_weight_new,
    )


F32 = jnp.float32
BF16 = jnp.bfloat16
I32 = jnp.int32
LANES = 128
MASKED = -1e30
VMEM_LIMIT = 56 * 1024 * 1024
MICRO = 1.15e9
QUICK = (1e6, 1e3)
THEIRS = 2


def dot_nn(left, right):
    return lax.dot_general(left, right, (((1,), (0,)), ((), ())), preferred_element_type=F32)


def dot_nt(left, right):
    return lax.dot_general(left, right, (((1,), (1,)), ((), ())), preferred_element_type=F32)


def dot_tn(left, right):
    return lax.dot_general(left, right, (((0,), (0,)), ((), ())), preferred_element_type=F32)


def iota(shape, dim):
    return lax.broadcasted_iota(I32, shape, dim)


def as_bf16(mask):
    return jnp.where(mask, 1.0, 0.0).astype(BF16)


def kernel_call(
    body, out_shape, scratch=(), grid=None, in_specs=None, out_specs=None, cost=None, aliases=None
):
    given = dict(grid=grid, in_specs=in_specs, out_specs=out_specs)
    extra = {name: value for name, value in given.items() if value is not None}
    flops, moved = cost if cost else (1e8, 1e6)
    name = getattr(body, "func", body).__name__
    return pl.pallas_call(
        body,
        name=name,
        out_shape=out_shape,
        scratch_shapes=list(scratch),
        input_output_aliases=aliases or {},
        compiler_params=pltpu.CompilerParams(vmem_limit_bytes=VMEM_LIMIT),
        cost_estimate=pl.CostEstimate(flops=int(flops), bytes_accessed=int(moved), transcendentals=0),
        **extra,
    )


def sds(shape, dtype):
    return jax.ShapeDtypeStruct(shape, dtype)


def route_body(n_exp, capacity, ids_ref, prio_ref, live_ref, cot_ref, row_ref, col_ref, sent_ref):
    toks = ids_ref.shape[1]
    half = capacity // 2
    prio_row = prio_ref[...]
    prio_col = jnp.transpose(jnp.broadcast_to(prio_row, (8, toks)))[:, :1]
    earlier = (prio_col < prio_row) | (
        (prio_col == prio_row) & (iota((toks, toks), 0) < iota((toks, toks), 1))
    )
    live = live_ref[...] > 0.0
    labels = iota((n_exp, toks), 0)
    first, second = ids_ref[0:1, :], ids_ref[1:2, :]
    wanted = ((labels == first) | (labels == second)) & live
    taken = dot_nn(as_bf16(wanted), as_bf16(earlier))
    places = []
    for chosen in (first, second):
        slot = jnp.sum(jnp.where(labels == chosen, taken, 0.0), axis=0, keepdims=True).astype(I32)
        kept = live & (slot < capacity)
        shard = chosen >> 2
        local = chosen & 3
        core = (slot >= half).astype(I32)
        target = ((((local >> 1) * 2 + core) * 2 + (local & 1)) * (n_exp // 4)) + shard
        places.append(jnp.where(kept, target * half + slot - core * half, -1))
    row_id = iota((8, toks), 0)
    rows = jnp.where(row_id == 0, places[0], jnp.where(row_id == 1, places[1], -1))
    row_ref[...] = rows
    col_ref[...] = jnp.transpose(rows.astype(F32)).astype(I32)
    slots = sent_ref.shape[0]
    spots = iota((slots, toks), 0)
    picks = as_bf16((spots == places[0]) | (spots == places[1]))
    sent_ref[...] = dot_nn(picks, cot_ref[...]).astype(BF16)


def unpack_body(spots_at, n_earlier, pos_ref, *refs):
    n_pieces = len(spots_at)
    pieces, rest = refs[:n_pieces], refs[n_pieces:]
    out_ref, held = rest[-2], rest[-1]

    @pl.when(pl.program_id(0) == 0)
    def _():
        gather_pieces(pieces, held)

    wanted = pos_ref[...]
    size = pieces[0].shape[0]
    place = jnp.full(wanted.shape, -1, I32)
    for number, at in enumerate(spots_at):
        inside = (wanted >= at) & (wanted < at + size)
        place = jnp.where(inside, wanted - at + number * size, place)
    picks = as_bf16(place == iota((wanted.shape[0], held.shape[0]), 1))
    value = dot_nn(picks, held[...])
    for earlier in rest[:n_earlier]:
        value = value + earlier[...].astype(F32)
    out_ref[...] = value.astype(BF16)


def gather_pieces(pieces, held):
    at = 0
    for piece in pieces:
        held[at : at + piece.shape[0], :] = piece[...]
        at += piece.shape[0]


def gather_halves(pieces, held):
    size = pieces[0].shape[0] // 2
    for number, piece in enumerate(pieces[:4]):
        held[number * size : (number + 1) * size, :] = piece[:size, :]
    at = 4 * size
    for piece in pieces[4:]:
        held[at : at + piece.shape[0], :] = piece[...]
        at += piece.shape[0]


def normalize(values):
    center = values - jnp.mean(values, axis=-1, keepdims=True)
    spread = jnp.mean(center * center, axis=-1, keepdims=True)
    scale = lax.rsqrt(spread + NORM_EPSILON)
    return center * scale, scale


def head_lanes(head, rows):
    return (iota((rows, LANES), 1) // HEAD_DIM) == head


def of_head(values, head):
    return jnp.where(head_lanes(head, values.shape[0]), values, jnp.zeros_like(values))


def by_head(first, second):
    return jnp.where(head_lanes(0, first.shape[0]), first, second)


def forward_body(
    n_exp, own_ref, other_ref, keep_ref, w_ref, pos_ref,
    qkv_ref, normed_ref, attended_ref, residual_ref, prob_ref, sent_ref, lse_col_ref, lse_row_ref,
    mixed_ref,
):
    toks, width = own_ref.shape
    router = 4 * width
    gain_one = w_ref[router + n_exp : router + n_exp + 16, :].astype(F32)
    gain_two = gain_one[1:2, :]
    gain_one = gain_one[0:1, :]
    for part, ref in enumerate((own_ref, other_ref)):
        normed = normalize(ref[...].astype(F32))[0] * gain_one
        low = normed.astype(BF16)
        if part == 0:
            normed_ref[...] = low
        rows = pl.ds(part * toks, toks)
        for third in range(3):
            made = dot_nt(low, w_ref[third * width : (third + 1) * width, :]).astype(BF16)
            if third == 0:
                made = made * jnp.asarray(HEAD_DIM ** (-0.5), BF16)
            qkv_ref[rows, third * width : (third + 1) * width] = made
    bias = jnp.where(keep_ref[...] > 0.0, 0.0, MASKED)
    lane = iota((toks, LANES), 1)
    logs = jnp.zeros((toks, LANES), F32)
    for at in range(0, width, LANES):
        queries = qkv_ref[0:toks, at : at + LANES]
        keys = qkv_ref[:, width + at : width + at + LANES]
        values = qkv_ref[:, 2 * width + at : 2 * width + at + LANES]
        made = []
        for head in range(2):
            score = dot_nt(of_head(queries, head), keys) + bias
            top = jnp.max(score, axis=-1, keepdims=True)
            grown = jnp.exp(score - top)
            total = jnp.sum(grown, axis=-1, keepdims=True)
            made.append(dot_nn(grown.astype(BF16), values) * (1.0 / total))
            logs = jnp.where(lane == 2 * (at // LANES) + head, top + jnp.log(total), logs)
        attended_ref[:, at : at + LANES] = by_head(*made)
    lse_col_ref[...] = logs
    lse_row_ref[...] = jnp.transpose(lse_col_ref[...])[:8, :]
    branch = dot_nn(attended_ref[...].astype(BF16), w_ref[3 * width : 4 * width, :])
    residual = own_ref[...].astype(F32) + branch
    residual_ref[...] = residual
    mixed = (normalize(residual)[0] * gain_two).astype(BF16)
    mixed_ref[...] = mixed
    logits = dot_nt(mixed, w_ref[router : router + n_exp, :])
    prob_ref[...] = jax.nn.softmax(logits, axis=-1)
    slots = sent_ref.shape[0]
    spots = iota((slots, toks), 0)
    picks = as_bf16((spots == pos_ref[0:1, :]) | (spots == pos_ref[1:2, :]))
    sent_ref[...] = dot_nn(picks, mixed).astype(BF16)


def gelu_parts(value):
    below = 0.5 + 0.5 * lax.erf(value * 0.7071067811865476)
    return value * below, below + value * jnp.exp(-0.5 * value * value) * 0.3989422804014327


def expert_body(
    n_exp, expert_ref, got_ref, cot_ref, near_ref, far_in_ref, far_out_ref, router_ref,
    active_ref, hidden_ref, scaled_ref, result_ref, back_ref, router_grad_ref,
):
    @pl.when(pl.program_id(0) == 0)
    def _():
        router_grad_ref[...] = jnp.zeros_like(router_grad_ref)

    expert = expert_ref[0]
    got, cot = got_ref[...], cot_ref[...]
    labels = iota((got.shape[0], n_exp), 1)
    share = jax.nn.softmax(dot_nt(got, router_ref[...]), axis=-1)
    gate = jnp.sum(jnp.where(labels == expert, share, 0.0), axis=-1, keepdims=True)
    scaled = (cot.astype(F32) * gate).astype(BF16)
    scaled_ref[...] = scaled
    half = near_ref.shape[0] // 2
    total = total_back = 0.0
    halves = ((near_ref[:half, :], near_ref[half:, :]), (far_in_ref[...], far_out_ref[...]))
    for number, (w_in, w_out) in enumerate(halves):
        at = slice(number * half, (number + 1) * half)
        active, slope = gelu_parts(dot_nt(got, w_in))
        low = active.astype(BF16)
        active_ref[:, at] = low
        grad = (dot_nt(scaled, w_out) * slope).astype(BF16)
        hidden_ref[:, at] = grad
        total = total + dot_nn(low, w_out)
        total_back = total_back + dot_nn(grad, w_in)
    result = total.astype(BF16)
    result_ref[...] = result
    inner = jnp.sum(result.astype(F32) * cot.astype(F32), axis=-1, keepdims=True)
    grad = share * (jnp.where(labels == expert, inner, 0.0) - gate * inner)
    low = grad.astype(BF16)
    back_ref[...] = (total_back + dot_nn(low, router_ref[...])).astype(BF16)
    router_grad_ref[...] += dot_tn(low, got)


def weight_grad_body(hidden_ref, active_ref, got_ref, scaled_ref, *outs):
    size = outs[0].shape[0]
    for number, out in enumerate(outs):
        left, right = ((hidden_ref, got_ref), (active_ref, scaled_ref))[number % 2]
        at = slice((1 - number // 2) * size, (2 - number // 2) * size)
        out[...] = dot_tn(left[:, at], right[...]).astype(out.dtype)


def norm_back(hat, scale, gain, grad):
    inner = grad * gain
    first = jnp.mean(inner, axis=-1, keepdims=True)
    second = jnp.mean(inner * hat, axis=-1, keepdims=True)
    return (inner - first - hat * second) * scale


def middle_body(
    n_exp, back_ref, pos_ref, residual_ref, cot_ref, keep_ref, attended_ref, w_ref,
    grad_ref, out_grad_ref, delta_col_ref, delta_row_ref, gain_ref,
):
    toks, width = residual_ref.shape
    router = 4 * width
    slots = back_ref.shape[0]
    gain_two = w_ref[router + n_exp : router + n_exp + 16, :].astype(F32)[1:2, :]
    spots = iota((toks, slots), 1)
    picks = as_bf16((spots == pos_ref[:, 0:1]) | (spots == pos_ref[:, 1:2]))
    grad_mixed = dot_nn(picks, back_ref[...])
    hat, scale = normalize(residual_ref[...])
    gain_ref[...] = jnp.broadcast_to(
        jnp.sum(grad_mixed * hat, axis=0, keepdims=True), gain_ref.shape
    )
    grad_rows = cot_ref[...].astype(F32) * keep_ref[...]
    grad = grad_rows + norm_back(hat, scale, gain_two, grad_mixed)
    grad_ref[...] = grad
    low = grad.astype(BF16)
    out_grad = dot_nt(low, w_ref[3 * width : 4 * width, :]).astype(BF16)
    out_grad_ref[...] = out_grad
    product = out_grad.astype(F32) * attended_ref[...]
    delta = jnp.zeros((toks, LANES), F32)
    lane = iota((toks, LANES), 1)
    for head in range(HEADS):
        at = (head // 2) * LANES
        part = jnp.where(head_lanes(head % 2, toks), product[:, at : at + LANES], 0.0)
        delta = jnp.where(lane == head, jnp.sum(part, axis=-1, keepdims=True), delta)
    delta_col_ref[...] = delta
    delta_row_ref[...] = jnp.transpose(delta)[:8, :]


def inner_body(
    n_exp, qkv_ref, out_grad_ref, lse_ref, delta_ref, keep_ref, attended_ref, grad_ref, router_grad_ref, gain_ref,
    query_ref, kv_ref, early_ref,
):
    toks, width = out_grad_ref.shape
    bias = jnp.where(keep_ref[...] > 0.0, 0.0, MASKED)
    for at in range(0, width, LANES):
        queries = qkv_ref[0:toks, at : at + LANES]
        keys = qkv_ref[:, width + at : width + at + LANES]
        values = qkv_ref[:, 2 * width + at : 2 * width + at + LANES]
        out_grad = out_grad_ref[:, at : at + LANES]
        made = []
        for head in range(2):
            line = 2 * (at // LANES) + head
            score = dot_nt(of_head(queries, head), keys) + bias
            prob = jnp.exp(score - lse_ref[:, line : line + 1])
            slope = dot_nt(of_head(out_grad, head), values)
            grad = (prob * (slope - delta_ref[:, line : line + 1])).astype(BF16)
            made.append(
                (dot_nn(grad, keys), dot_tn(grad[:, :toks], queries), dot_tn(prob[:, :toks].astype(BF16), out_grad))
            )
        query_ref[:, at : at + LANES] = (by_head(made[0][0], made[1][0]) * HEAD_DIM ** (-0.5)).astype(BF16)
        kv_ref[0, :, at : at + LANES] = by_head(made[0][1], made[1][1])
        kv_ref[1, :, at : at + LANES] = by_head(made[0][2], made[1][2])
    early_ref[0:width, :] = dot_tn(attended_ref[...].astype(BF16), grad_ref[...].astype(BF16)).astype(BF16)
    early_ref[width : width + n_exp, :] = router_grad_ref[...].astype(BF16)
    row_id = iota((16, width), 0)
    early_ref[width + n_exp : width + n_exp + 16, :] = jnp.where(
        row_id == 0, gain_ref[0:1, :], 0.0
    ).astype(BF16)


def outer_body(
    n_exp, qkv_ref, out_grad_ref, sums_ref, keep_ref, query_ref, kv_ref, normed_ref, own_ref, w_ref, early_ref,
    pieces_ref, grad_normed_ref, held,
):
    toks, width = query_ref.shape
    held[:, 0:width] = query_ref[...]
    bias = jnp.where(keep_ref[...] > 0.0, 0.0, MASKED)
    for at in range(0, width, LANES):
        queries = qkv_ref[toks : 2 * toks, at : at + LANES]
        out_grad = out_grad_ref[:, at : at + LANES]
        keys = qkv_ref[0:toks, width + at : width + at + LANES]
        values = qkv_ref[0:toks, 2 * width + at : 2 * width + at + LANES]
        made = []
        for head in range(2):
            line = 2 * (at // LANES) + head
            score = dot_nt(of_head(keys, head), queries) + bias
            prob = jnp.exp(score - sums_ref[line : line + 1, :])
            slope = dot_nt(of_head(values, head), out_grad)
            grad = (prob * (slope - sums_ref[HEADS + line : HEADS + line + 1, :])).astype(BF16)
            made.append((dot_nn(grad, queries), dot_nn(prob.astype(BF16), out_grad)))
        for number in range(2):
            total = kv_ref[number, :, at : at + LANES] + by_head(made[0][number], made[1][number])
            held[:, (number + 1) * width + at : (number + 1) * width + at + LANES] = total.astype(BF16)
    pieces_ref[0 : 3 * width, :] = dot_tn(held[...], normed_ref[...]).astype(BF16)
    grad_normed = dot_nn(held[...], w_ref[0 : 3 * width, :])
    grad_normed_ref[...] = grad_normed
    gain_grad = jnp.sum(grad_normed * normalize(own_ref[...].astype(F32))[0], axis=0, keepdims=True)
    pieces_ref[3 * width : 3 * width + 16, :] = jnp.where(
        iota((16, width), 0) == 0, gain_grad, 0.0
    ).astype(BF16)
    pieces_ref[3 * width + 16 :, :] = early_ref[...]


def tokens_body(n_exp, grad_normed_ref, own_ref, w_ref, grad_ref, out_ref):
    at = 4 * own_ref.shape[1] + n_exp
    gain_one = w_ref[at : at + 16, :].astype(F32)[0:1, :]
    hat, scale = normalize(own_ref[...].astype(F32))
    out_ref[...] = grad_ref[...] + norm_back(hat, scale, gain_one, grad_normed_ref[...])


def spread_body(starts, pos_ref, mine_ref, far_ref, *outs):
    held, outs = outs[-1], outs[:-1]
    held[...] = total_f32(mine_ref[...], far_ref[...]).astype(BF16)
    size = outs[0].shape[0]
    for number, start in enumerate(starts):
        picks = as_bf16(iota((size, held.shape[0]), 0) + start == pos_ref[...])
        outs[number][...] = dot_nn(picks, held[...]).astype(BF16)


def room_of(owned, n_dev):
    return min(owned, -(-(owned // n_dev * 5 // 4) // 16) * 16)


def sent_at(partner):
    return ((partner >> 2) & 1) * 4 + (partner & 1) * 2 + ((partner >> 1) & 1)


def got_at(partner):
    return ((partner >> 1) & 1) * 4 + ((partner >> 2) & 1) * 2 + (partner & 1)


def sent_cell(cell):
    return (cell >> 2) * 4 + (cell & 1) * 2 + ((cell >> 1) & 1)


def plan_body(n_dev, room, me_ref, owner_ref, row_ref, col_ref, most_ref):
    me = me_ref[0]
    owned = owner_ref.shape[1]
    source = owner_ref[...] >> (owned.bit_length() - 1)
    spot = owner_ref[...] & (owned - 1)
    total = n_dev * n_dev
    classes = iota((n_dev, owned), 0)
    member = jnp.concatenate([classes == source[t : t + 1, :] for t in range(n_dev)], axis=0)
    ones = as_bf16(member)
    step = 256
    before = as_bf16(iota((step, step), 0) < iota((step, step), 1))
    count = jnp.zeros((total, 1), F32)
    ranks = []
    for at in range(0, owned, step):
        part = ones[:, at : at + step]
        ranks.append(dot_nn(part, before) + count)
        count = count + jnp.sum(part.astype(F32), axis=1, keepdims=True)
    most_ref[...] = jnp.broadcast_to(jnp.max(count, axis=0, keepdims=True).astype(I32), most_ref.shape)
    line = iota((total, 1), 0)
    to, of = line // n_dev, line % n_dev
    rank = jnp.concatenate(ranks, axis=1)
    turn = ((rank + 0.5) * (1.0 / room)).astype(I32)
    inside = rank.astype(I32) + turn * ((n_dev - 1) * room)
    wanted = member & (to == me)
    arrives = jnp.sum(jnp.where(wanted, inside + got_at(of ^ to) * room, 0), axis=0, keepdims=True)
    returns = jnp.sum(jnp.where(wanted, inside + sent_at(of ^ to) * room, 0), axis=0, keepdims=True)
    leaves = inside + sent_at(of ^ to) * room
    half = owned // LANES
    found = jnp.zeros((2 * half, LANES), F32)
    high, lanes = iota((half, owned), 0), iota((LANES, owned), 0)
    for t in range(n_dev):
        mine = slice(t * n_dev, (t + 1) * n_dev)
        chosen = member[mine] & (of[mine] == me)
        place = jnp.sum(jnp.where(chosen, leaves[mine], 0), axis=0, keepdims=True)
        hit = (spot[t : t + 1, :] // LANES == high) & (source[t : t + 1, :] == me)
        left = jnp.concatenate(
            [jnp.where(hit, place // LANES, 0), jnp.where(hit, place % LANES, 0)], axis=0
        ).astype(F32).astype(BF16)
        found = found + dot_nt(left, as_bf16((spot[t : t + 1, :] % LANES) == lanes))
    found = found[:half] * float(LANES) + found[half:]
    leave_row = jnp.concatenate([found[a : a + 1, :] for a in range(half)], axis=1)
    block = ((leave_row + 0.5) * (1.0 / room)).astype(I32)
    round_no, cell = block // n_dev, block % n_dev
    comes = leave_row.astype(I32) + (round_no * n_dev + got_at(sent_cell(cell)) - block) * room
    rows = jnp.concatenate(
        [leave_row, arrives.astype(F32), returns.astype(F32), comes.astype(F32), jnp.zeros((4, owned), F32)], axis=0
    )
    row_ref[...] = rows.astype(I32)
    col_ref[...] = jnp.transpose(rows).astype(I32)


LEAVES, ARRIVES, RETURNS, COMES = range(4)


def put_rows(line, base_ref, pos_ref, held, outs, tile):
    wanted = pos_ref[line : line + 1, :] - base_ref[0]
    base = 0
    for out in outs:
        for at in range(0, out.shape[0], tile):
            picks = as_bf16(iota((tile, held.shape[0]), 0) + (base + at) == wanted)
            out[at : at + tile, :] = dot_nn(picks, held[...]).astype(BF16)
        base += out.shape[0]


def put_body(line, tile, base_ref, pos_ref, rows_ref, *outs):
    put_rows(line, base_ref, pos_ref, rows_ref, outs, tile)


def sum_put_body(line, tile, cells, n_in, base_ref, pos_ref, *refs):
    mine, theirs, outs, held = refs[:n_in], refs[n_in : 2 * n_in], refs[2 * n_in : -1], refs[-1]
    size = mine[0].shape[0]
    for number in range(n_in):
        held[number * size : (number + 1) * size, :] = total_f32(mine[number][...], theirs[number][...]).astype(BF16)
    wanted = pos_ref[line : line + 1, :] - base_ref[0]
    for cell, out in zip(cells, outs):
        for at in range(0, out.shape[0], tile):
            picks = as_bf16(iota((tile, held.shape[0]), 0) + (cell * out.shape[0] + at) == wanted)
            out[at : at + tile, :] = dot_nn(picks, held[...]).astype(BF16)


def take_body(line, tile, base_ref, pos_ref, *refs):
    pieces, out, held = refs[:-2], refs[-2], refs[-1]
    gather_halves(pieces, held)
    for at in range(0, out.shape[0], tile):
        wanted = pos_ref[at : at + tile, line : line + 1] - base_ref[0]
        picks = as_bf16(iota((tile, held.shape[0]), 1) == wanted)
        out[at : at + tile, :] = dot_nn(picks, held[...]).astype(BF16)


def adam_body(n_in, n_made, pos_ref, *refs):
    pieces, (first_ref, second_ref, weight_ref) = refs[:n_in], refs[n_in : n_in + 3]
    grad_ref, first_new, second_new, weight_new, held = refs[n_in + 3 + n_made :]

    @pl.when(pl.program_id(0) == 0)
    def _():
        gather_halves(pieces, held)

    picks = as_bf16(iota((grad_ref.shape[0], held.shape[0]), 1) == pos_ref[:, COMES : COMES + 1])
    grad = dot_nn(picks, held[...])
    grad_ref[...] = grad
    made = adam_update(grad, first_ref[...], second_ref[...], weight_ref[...].astype(F32))
    first_new[...], second_new[...], weight_new[...] = made


def mixture_body(result_ref, pos_ref, ids_ref, prob_ref, residual_ref, out_ref):
    toks = residual_ref.shape[0]
    slots = result_ref.shape[0]
    share = prob_ref[...]
    total = residual_ref[...]
    for number in range(2):
        picks = as_bf16(iota((toks, slots), 1) == pos_ref[:, number : number + 1])
        mine = iota(share.shape, 1) == ids_ref[:, number : number + 1]
        gate = jnp.sum(jnp.where(mine, share, 0.0), axis=-1, keepdims=True)
        total = total + gate * dot_nn(picks, result_ref[...])
    out_ref[...] = total.astype(BF16)


SWAP = [(0, 1), (1, 0)]
SWAP_CORE = [(0, 1), (1, 0), (2, 3), (3, 2)]
SWAP_Y = [(0, 2), (2, 0), (1, 3), (3, 1)]


def swap_x(value):
    return lax.ppermute(value, "ctx", SWAP)


def swap_y(value):
    return lax.ppermute(value, "dp", SWAP_Y)


def swap_x_y(value):
    return lax.ppermute(value, ("dp", "ctx"), [(i, i ^ 5) for i in range(8)])


def swap_core(value):
    return lax.ppermute(value, "dp", SWAP_CORE)


def shift_z(value, by):
    count = lax.axis_size("expert")
    return lax.ppermute(value, "expert", [(i, (i + by) % count) for i in range(count)])


def after(values, *others):
    values = list(values)
    return lax.optimization_barrier((*values, *others))[: len(values)]


def total_f32(first, second):
    return first.astype(F32) + second.astype(F32)


def on_chip_experts(
    tokens, cotangent, pad_mask, expert_ids, slot_priority, shared_slots, shared_first, shared_second,
    shared_owner, expert_slots, expert_first, expert_second, expert_owner,
):
    toks, width = tokens.shape[1], tokens.shape[2]
    n_z = lax.axis_size("expert")
    n_exp = EXP_DEV * n_z
    capacity = (10 * toks + 4 * n_exp - 1) // (4 * n_exp)
    slots = n_exp * capacity
    everyone = ("dp", "ctx", "expert")
    dp, mx, mz = lax.axis_index("dp"), lax.axis_index("ctx"), lax.axis_index("expert")
    my, mc = dp // 2, dp % 2

    own_count = shared_slots.shape[0]
    stride = -(-own_count // 8) * 8
    padded = jnp.pad(shared_slots, ((0, stride - own_count), (0, 0)))
    line = [padded] + [shift_z(padded, by) for by in range(1, n_z)]
    part_a = jnp.concatenate(line[: n_z // 2], axis=0)
    part_b = jnp.concatenate(line[n_z // 2 :], axis=0)
    a_y, b_x = swap_y(part_a), swap_x(part_b)
    pair_a, pair_b = jnp.concatenate([part_a, a_y], axis=0), jnp.concatenate([part_b, b_x], axis=0)
    first_near, last_near = [pair_a, pair_b], [swap_x(pair_a), swap_y(pair_b)]
    first_far = [swap_core(piece) for piece in first_near]

    owner_dev, owner_row = shared_owner // own_count, shared_owner % own_count
    o_z, o_x, o_dp = owner_dev % n_z, owner_dev // n_z % 2, owner_dev // (n_z * 2)
    in_c, in_y, in_x = (o_dp % 2) ^ mc, (o_dp // 2) ^ my, o_x ^ mx
    in_z = (mz - o_z + n_z) % n_z
    late = in_z // (n_z // 2)
    cross = jnp.where(late == 0, in_y + 2 * in_x, in_x + 2 * in_y)
    place = (((in_c * 2 + late) * 4 + cross) * (n_z // 2) + in_z % (n_z // 2)) * stride + owner_row
    total_slots = 8 * n_z * stride
    row_count = -(-shared_owner.shape[0] // 16) * 16
    place_col = jnp.pad(place, (0, row_count - place.shape[0]), constant_values=-1)[:, None]
    gain_at = 4 * width + n_exp
    none = jnp.full((15,), -1, I32)
    place_row = jnp.concatenate(
        [place[: 3 * width], place[gain_at : gain_at + 1], none, place[3 * width : gain_at], place[gain_at + 1 :], none]
    )[None, :]

    half_slots = total_slots // 2
    piece = half_slots // 4
    row_tile = row_count // 5 if row_count % 80 == 0 else row_count

    def unpack(spots, pieces, earlier):
        rows_of = lambda columns: pl.BlockSpec((row_tile, columns), lambda i: (i, 0))
        return kernel_call(
            functools.partial(unpack_body, spots, len(earlier)), sds((row_count, width), BF16),
            [pltpu.VMEM((len(pieces) * piece, width), BF16)],
            grid=(row_count // row_tile,),
            in_specs=[rows_of(1)] + [pl.BlockSpec((piece, width), lambda i: (0, 0))] * len(pieces)
            + [rows_of(width)] * len(earlier),
            out_specs=rows_of(width),
            cost=(7 * MICRO, 1e6),
        )(place_col, *pieces, *earlier)

    first_rows = unpack(
        [0, 2 * piece, half_slots, half_slots + 2 * piece], [*first_near, *first_far], []
    )
    last_near = after(last_near, first_rows)
    last_far = [swap_core(piece) for piece in last_near]

    own, other = tokens[0], swap_x(tokens[0])
    ids = expert_ids[0]
    live = pad_mask.astype(F32)
    live_other = swap_x(pad_mask).astype(F32)
    keep_row = jnp.concatenate([live, live_other], axis=1)
    keep_col = live.reshape(toks, 1)
    pos_row, pos_col, cot_sent = kernel_call(
        functools.partial(route_body, n_exp, capacity),
        (sds((8, toks), I32), sds((toks, 8), I32), sds((slots, width), BF16)),
        cost=(4 * MICRO, 1e6),
    )(*after([ids.T], other), slot_priority.astype(F32), live, cotangent[0])

    def exchange(rows):
        return lax.all_to_all(rows, everyone, split_axis=0, concat_axis=0, tiled=True)

    cot_got = exchange(after([cot_sent], a_y, b_x)[0])

    local = my * 2 + mx
    group, n_dev = dp * 2 + mx, 8
    owned = expert_slots.shape[1]
    room = room_of(owned, n_dev)
    owner = jnp.transpose(
        expert_owner[0].reshape(2, 2, 2, 2, FF // 2), (0, 3, 1, 2, 4)
    ).reshape(n_dev, owned)
    held = [pltpu.VMEM((n_dev * room, width), BF16)]
    sent_shapes = [sds((2 * room, width), BF16)] * 4
    smem, vmem = pl.BlockSpec(memory_space=pltpu.SMEM), pl.BlockSpec(memory_space=pltpu.VMEM)
    plan_row, plan_col, most = kernel_call(
        functools.partial(plan_body, n_dev, room),
        (sds((8, owned), I32), sds((owned, 8), I32), sds((8, LANES), I32)), cost=(5 * MICRO, 1e6),
        in_specs=[smem, vmem],
    )(group.astype(I32).reshape(1), *after([owner], part_a, part_b, pos_row, other))
    rounds = (most[0, 0] + room - 1) // room
    def with_base(body, out_shape, scratch, arrays, number=0, cost=QUICK):
        base = jnp.full((1,), number * n_dev * room, I32)
        return kernel_call(
            body, out_shape, scratch, in_specs=[smem] + [vmem] * len(arrays), cost=cost
        )(base, *arrays)

    def over_links(pieces):
        return [pieces[0], swap_x(pieces[1]), swap_y(pieces[2]), swap_x_y(pieces[3])]

    def over_cores(got):
        far = [jnp.concatenate([got[at][room:], got[at + 1][room:]], axis=0) for at in (0, 2)]
        return [*got, swap_core(far[0]), swap_core(far[1])]

    put_leaving = functools.partial(put_body, LEAVES, room)
    take_tile = 256 if owned % 256 == 0 else owned
    take_arrived = functools.partial(take_body, ARRIVES, take_tile)
    leaving = with_base(
        put_leaving, sent_shapes, (), [*after([plan_row], a_y, b_x), expert_slots[0]], 0, (8 * MICRO, 1e6)
    )
    moved = over_links(after(leaving, *last_near))

    weights = unpack(
        [piece, 3 * piece, half_slots + piece, half_slots + 3 * piece], [*last_near, *last_far], [first_rows]
    )

    (qkv, normed, attended, residual, prob, sent, lse_col, lse_row) = kernel_call(
        functools.partial(forward_body, n_exp),
        (
            sds((2 * toks, 3 * width), BF16), sds((toks, width), BF16), sds((toks, width), F32),
            sds((toks, width), F32), sds((toks, n_exp), F32), sds((slots, width), BF16),
            sds((toks, LANES), F32), sds((8, toks), F32),
        ),
        [pltpu.VMEM((toks, width), BF16)],
        cost=(13 * MICRO, 1e6),
    )(*after([own], cot_got), other, keep_row, weights, pos_row)
    got = exchange(sent)
    moved = over_cores(after(moved, sent))
    near_weights = with_base(take_arrived, sds((owned, width), BF16), held, [plan_col, *moved])
    far_weights = [swap_core(near_weights[: FF // 2]), swap_core(near_weights[FF // 2 :])]

    def more_weights(number, totals):
        leaving = with_base(put_leaving, sent_shapes, (), [plan_row, expert_slots[0]], number)
        moved = over_cores(over_links(leaving))
        part = with_base(take_arrived, sds((owned, width), BF16), held, [plan_col, *moved], number)
        there = swap_core(part)
        return totals[0] + part, totals[1] + there[: FF // 2], totals[2] + there[FF // 2 :]

    got, *expert_weights = after([got, near_weights, *far_weights])
    near_weights, *far_weights = lax.fori_loop(1, rounds, more_weights, tuple(expert_weights))

    expert_id = (mz * EXP_DEV + local).astype(I32).reshape(1)
    tile = 256 if slots % 256 == 0 else slots
    router_rows = weights[4 * width : 4 * width + n_exp]
    whole = lambda shape: pl.BlockSpec(shape, lambda i: (0, 0))
    rows_of = lambda columns: pl.BlockSpec((tile, columns), lambda i: (i, 0))
    active, hidden, scaled, result, back, router_grad = kernel_call(
        functools.partial(expert_body, n_exp),
        (
            sds((slots, FF), BF16), sds((slots, FF), BF16), sds((slots, width), BF16),
            sds((slots, width), BF16), sds((slots, width), BF16), sds((n_exp, width), F32),
        ),
        grid=(slots // tile,),
        in_specs=[
            pl.BlockSpec(memory_space=pltpu.SMEM), rows_of(width), rows_of(width),
            whole((FF, width)), whole((FF // 2, width)), whole((FF // 2, width)), whole((n_exp, width)),
        ],
        out_specs=(
            rows_of(FF), rows_of(FF), rows_of(width), rows_of(width), rows_of(width), whole((n_exp, width)),
        ),
        cost=(19 * MICRO, 1e6),
    )(expert_id, got, cot_got, near_weights, *far_weights, router_rows)
    back_got = exchange(back)

    halves = [sds((FF // 2, width), BF16)] * 2 + [sds((FF // 2, width), F32)] * 2
    *theirs, mine_in, mine_out = kernel_call(weight_grad_body, halves, cost=(10 * MICRO, 1e6))(
        hidden, active, got, scaled
    )
    theirs_got, mine = [swap_core(part) for part in theirs], (mine_in, mine_out)
    held_owned = [pltpu.VMEM((owned, width), BF16)]

    def returning(cells, number=0):
        body = functools.partial(sum_put_body, RETURNS, room, cells, 2)
        return with_base(body, [sent_shapes[0]] * len(cells), held_owned, [plan_row, *mine, *theirs_got], number, (4 * MICRO, 1e6))

    moved_x, moved_xy = returning((1, 3))
    moved_0, moved_y = returning((0, 2))
    moved = [moved_0, moved_x, moved_y, moved_xy]
    back_got = after([back_got], moved[0])[0]

    grad_residual, out_grad, delta_col, delta_row, gain_two = kernel_call(
        functools.partial(middle_body, n_exp),
        (
            sds((toks, width), F32), sds((toks, width), BF16), sds((toks, LANES), F32),
            sds((8, toks), F32), sds((8, width), F32),
        ),
        cost=(6 * MICRO, 1e6),
    )(back_got, pos_col, residual, cotangent[0], keep_col, attended, weights)
    out_grad_other = swap_x(out_grad)
    sums_other = swap_x(jnp.concatenate([lse_row, delta_row], axis=0))
    moved = over_links(moved)
    query_grad, kv_grad, early = kernel_call(
        functools.partial(inner_body, n_exp),
        (sds((toks, width), BF16), sds((2, toks, width), F32), sds((width + n_exp + 16, width), BF16)),
        cost=(15 * MICRO, 1e6),
    )(qkv, out_grad, lse_col, delta_col, keep_row, attended, grad_residual, router_grad, gain_two)
    result_got = exchange(after([result], query_grad)[0])
    late, grad_normed = kernel_call(
        functools.partial(outer_body, n_exp),
        (sds((place_row.shape[1], width), BF16), sds((toks, width), F32)),
        [pltpu.VMEM((toks, 3 * width), BF16)],
        cost=QUICK,
    )(
        qkv, *after([out_grad_other], *moved), sums_other, keep_col, query_grad, kv_grad, normed, own, weights, early,
    )
    late_far = swap_core(late)
    quarter = half_slots // 2
    eighth, sixteenth = quarter // 2, quarter // 4
    count = place_row.shape[1]

    def spread(starts, *others):
        return kernel_call(
            functools.partial(spread_body, starts), [sds((eighth, width), BF16)] * 2,
            [pltpu.VMEM((count, width), BF16)], cost=QUICK,
        )(*after([place_row], *others), late, late_far)

    sends = spread((eighth, quarter + eighth))
    got_a, got_b = swap_x(sends[0]), swap_y(sends[1])
    keeps = spread((0, quarter), *sends)
    grad_tokens = kernel_call(
        functools.partial(tokens_body, n_exp), sds((toks, width), F32), cost=QUICK
    )(*after([grad_normed], *sends), own, weights, grad_residual)
    moved = over_cores(after(moved, *keeps))

    tile = 256 if owned % 512 == 0 else owned // 2
    steps = owned // tile // 2

    def adam_half(number, made, *others):
        rows_of = lambda columns: pl.BlockSpec((tile, columns), lambda i: (i + number * steps, 0))
        n_given = 1 + len(moved) + 3
        return kernel_call(
            functools.partial(adam_body, len(moved), len(made)), [sds((owned, width), F32)] * 4, held,
            grid=(steps,),
            in_specs=[rows_of(8)] + [pl.BlockSpec(piece.shape, lambda i: (0, 0)) for piece in moved]
            + [rows_of(width)] * 3 + [pl.BlockSpec(memory_space=pl.ANY)] * len(made),
            out_specs=[rows_of(width)] * 4,
            cost=QUICK,
            aliases={n_given + at: at for at in range(len(made))},
        )(*after([plan_col], *others), *moved, expert_first[0], expert_second[0], expert_slots[0], *made)

    got_a, got_b = after([got_a, got_b], grad_tokens)
    sum_a = total_f32(keeps[0], got_a).astype(BF16)
    sum_b = total_f32(keeps[1], got_b).astype(BF16)
    got_a, got_b = swap_y(sum_a[sixteenth:]), swap_x(sum_b[sixteenth:])
    half_new = adam_half(0, [], sum_a, sum_b)
    got_a, got_b = after([got_a, got_b], half_new[0])
    sum_a = total_f32(sum_a[:sixteenth], got_a).astype(BF16)
    sum_b = total_f32(sum_b[:sixteenth], got_b).astype(BF16)
    lines = [sum_a[i * stride : (i + 1) * stride] for i in range(n_z // 2)]
    lines += [sum_b[i * stride : (i + 1) * stride] for i in range(n_z // 2)]
    output = kernel_call(
        mixture_body, sds((toks, width), BF16), cost=QUICK
    )(*after([result_got], *lines), pos_col, ids, prob, residual)
    expert_new = adam_half(1, half_new, *lines)
    shared_grad = lines[0].astype(F32)
    for by in range(1, n_z):
        shared_grad = shared_grad + shift_z(lines[by], n_z - by).astype(F32)
    shared_grad = shared_grad[:own_count]


    def more_grads(number, made):
        parts = returning(range(4), number)
        parts = over_cores(over_links(parts))
        take = functools.partial(take_body, COMES, take_tile)
        part = with_base(take, sds((owned, width), BF16), held, [plan_col, *parts], number)
        grad = made[0] + part.astype(F32)
        return (grad, *adam_update(grad, expert_first[0], expert_second[0], expert_slots[0].astype(F32)))

    shared_grad, *expert_new = after([shared_grad, *expert_new], output)
    expert_new = lax.fori_loop(1, rounds, more_grads, tuple(expert_new))
    shared_new = adam_update(shared_grad, shared_first, shared_second, shared_slots.astype(F32))
    return (
        output[None], grad_tokens[None], shared_grad, *shared_new,
        *(value[None] for value in expert_new),
    )


def solution(mesh):
    sizes = mesh.shape
    chip_experts = (sizes["dp"], sizes["ctx"], sizes["expert"]) == (4, 2, 4)
    return jax.shard_map(
        on_chip_experts if chip_experts else on_device,
        mesh=mesh,
        in_specs=(
            P(("dp", "expert"), "ctx", None),
            P(("dp", "expert"), "ctx", None),
            P(("dp", "expert"), "ctx"),
            P(("dp", "expert"), "ctx", None),
            P(("dp", "expert"), "ctx"),
            P(("dp", "ctx", "expert"), None),
            P(("dp", "ctx", "expert"), None),
            P(("dp", "ctx", "expert"), None),
            P(),
            P("expert", ("dp", "ctx"), None),
            P("expert", ("dp", "ctx"), None),
            P("expert", ("dp", "ctx"), None),
            P("expert", None),
        ),
        out_specs=(
            P(("dp", "expert"), "ctx", None),
            P(("dp", "expert"), "ctx", None),
            P(("dp", "ctx", "expert"), None),
            P(("dp", "ctx", "expert"), None),
            P(("dp", "ctx", "expert"), None),
            P(("dp", "ctx", "expert"), None),
            P("expert", ("dp", "ctx"), None),
            P("expert", ("dp", "ctx"), None),
            P("expert", ("dp", "ctx"), None),
            P("expert", ("dp", "ctx"), None),
        ),
        check_vma=False,
    )
```

```python
import functools
import math

import jax
import jax.numpy as jnp
from jax import lax
from jax.experimental import pallas as pl
from jax.experimental.pallas import tpu as pltpu
from jax.sharding import PartitionSpec as P

HEADS = 8
HEAD_DIM = 64
FF = 2048
EXP_DEV = 4


MASKED_SCORE = -1e30
MOMENT_DECAY = 0.5
LEARN_RATE = 0.05
WEIGHT_DECAY = 0.1
EPSILON = 1e-08
NORM_EPSILON = 1e-06


def layer_norm(values, gain_rows):
    center = values - jnp.mean(values, axis=-1, keepdims=True)
    spread = jnp.mean(center * center, axis=-1, keepdims=True)
    return center * lax.rsqrt(spread + NORM_EPSILON) * gain_rows


def routing(chosen, priority, live_rows, expert_count, capacity):
    tok_count = chosen.shape[0]
    token_ids = jnp.arange(tok_count, dtype=jnp.int32)
    ranking = jnp.argsort(priority * tok_count + token_ids)
    labels = jnp.arange(expert_count, dtype=jnp.int32)
    wanted = jnp.any(chosen[:, :, None] == labels[None, None, :], axis=1) & (
        live_rows[:, None] == 1
    )
    wanted = wanted.astype(jnp.int32)
    ranked = wanted[ranking]
    before = jnp.cumsum(ranked, axis=0) - ranked
    position = jnp.zeros_like(before).at[ranking].set(before)
    slot_taken = jnp.take_along_axis(position, chosen, axis=1)
    kept_pair = (slot_taken < capacity) & (live_rows[:, None] == 1)
    target = jnp.where(kept_pair, chosen * capacity + slot_taken, expert_count * capacity)
    owners = jnp.broadcast_to(token_ids[:, None], chosen.shape)
    source = (
        jnp.zeros((expert_count * capacity,), jnp.int32)
        .at[target.reshape(-1)]
        .set(owners.reshape(-1), mode="drop")
    )
    filled = (
        jnp.zeros((expert_count * capacity,), jnp.int32).at[target.reshape(-1)].set(1, mode="drop")
    )
    slot_index = jnp.where(kept_pair, chosen * capacity + slot_taken, 0)
    return (slot_index, kept_pair.astype(jnp.int32), source, filled)


def head_view(values):
    return values.reshape(values.shape[0], values.shape[1], HEADS, HEAD_DIM)


def score_block(queries, key_rows, keep_mask):
    score = jnp.einsum(
        "iqhe,ikhe->ihqk", queries, head_view(key_rows), preferred_element_type=jnp.float32
    ) * HEAD_DIM ** (-0.5)
    return jnp.where(keep_mask[:, None, None, :] > 0, score, MASKED_SCORE)


def stats_step(running, portion, queries):
    row_max, row_sum = running
    key_rows, keep_mask = portion
    score = score_block(queries, key_rows, keep_mask)
    keep_wide = keep_mask.astype(jnp.float32)[:, None, None, :]
    new_max = jnp.maximum(row_max, jnp.max(score, axis=-1))
    row_sum = row_sum * jnp.exp(row_max - new_max) + jnp.sum(
        jnp.exp(score - new_max[..., None]) * keep_wide, axis=-1
    )
    return (new_max, row_sum)


def value_step(running, portion, queries, log_sum):
    key_rows, value_rows, keep_mask = portion
    score = score_block(queries, key_rows, keep_mask)
    keep_wide = keep_mask.astype(jnp.float32)[:, None, None, :]
    attn_prob = (jnp.exp(score - log_sum[..., None]) * keep_wide).astype(jnp.bfloat16)
    return running + jnp.einsum(
        "ihqk,ikhe->iqhe", attn_prob, head_view(value_rows), preferred_element_type=jnp.float32
    )


def grad_step(grad_query, portion, queries, log_sum, grad_out, row_delta):
    key_rows, value_rows, keep_mask = portion
    score = score_block(queries, key_rows, keep_mask)
    keep_wide = keep_mask.astype(jnp.float32)[:, None, None, :]
    attn_prob = jnp.exp(score - log_sum[..., None]) * keep_wide
    prob_low = attn_prob.astype(jnp.bfloat16)
    grad_value = jnp.einsum(
        "ihqk,iqhe->ikhe", prob_low, grad_out, preferred_element_type=jnp.float32
    )
    grad_prob = jnp.einsum(
        "iqhe,ikhe->ihqk", grad_out, head_view(value_rows), preferred_element_type=jnp.float32
    )
    grad_score = (attn_prob * (grad_prob - row_delta[..., None])).astype(jnp.bfloat16)
    score_scale = HEAD_DIM ** (-0.5)
    grad_query = (
        grad_query
        + jnp.einsum(
            "ihqk,ikhe->iqhe", grad_score, head_view(key_rows), preferred_element_type=jnp.float32
        )
        * score_scale
    )
    grad_key = (
        jnp.einsum("ihqk,iqhe->ikhe", grad_score, queries, preferred_element_type=jnp.float32)
        * score_scale
    )
    return (grad_query, jnp.stack([grad_key, grad_value]))


def each_block(step_fn, running, arrays, block_len):
    total_len = arrays[0].shape[1]
    size_rows = math.gcd(total_len, block_len)

    def one_turn(number, current):
        offset = number * size_rows
        portion = tuple(
            (lax.dynamic_slice_in_dim(member, offset, size_rows, 1) for member in arrays)
        )
        return step_fn(current, portion)

    return lax.fori_loop(0, total_len // size_rows, one_turn, running)


def adam_update(gradient, first_old, second_old, weight):
    first_new = MOMENT_DECAY * first_old + (1.0 - MOMENT_DECAY) * gradient
    second_new = MOMENT_DECAY * second_old + (1.0 - MOMENT_DECAY) * gradient * gradient
    weight_new = weight - LEARN_RATE * (
        first_new / (jnp.sqrt(second_new) + EPSILON) + WEIGHT_DECAY * weight
    )
    return (first_new, second_new, weight_new)


def on_device(
    tokens,
    cotangent,
    pad_mask,
    expert_ids,
    slot_priority,
    shared_slots,
    shared_first,
    shared_second,
    shared_owner,
    expert_slots,
    expert_first,
    expert_second,
    expert_owner,
):
    img_count, part_len, features = tokens.shape
    tok_count = img_count * part_len
    expert_count = EXP_DEV * lax.axis_size("expert")
    capacity = (10 * tok_count + 4 * expert_count - 1) // (4 * expert_count)
    all_shared = lax.all_gather(shared_slots, ("dp", "ctx", "expert"), axis=0, tiled=True)
    all_expert = lax.all_gather(expert_slots, ("dp", "ctx"), axis=1, tiled=True)
    pieces = all_shared[shared_owner]
    w_qkv = pieces[: 3 * features]
    w_attn_out = pieces[3 * features : 4 * features]
    w_router = pieces[4 * features : 4 * features + expert_count]
    gain_one = pieces[4 * features + expert_count].astype(jnp.float32)
    gain_two = pieces[4 * features + expert_count + 1].astype(jnp.float32)
    expert_rows = all_expert[0][expert_owner[0]].reshape(EXP_DEV, 2, FF, features)
    w_in = expert_rows[:, 0]
    w_out = expert_rows[:, 1]
    inputs = tokens.reshape(tok_count, features).astype(jnp.float32)
    keep_mask = pad_mask.astype(jnp.bfloat16)
    keep_rows = pad_mask.reshape(tok_count).astype(jnp.float32)
    normed_one, norm_one_back = jax.vjp(layer_norm, inputs, gain_one)
    normed_low = normed_one.astype(jnp.bfloat16)
    qkv_rows = lax.dot_general(
        normed_low, w_qkv, (((1,), (1,)), ((), ())), preferred_element_type=jnp.float32
    ).astype(jnp.bfloat16)
    query_rows = qkv_rows[:, :features].reshape(img_count, part_len, features)
    key_rows = qkv_rows[:, features : 2 * features].reshape(img_count, part_len, features)
    value_rows = qkv_rows[:, 2 * features :].reshape(img_count, part_len, features)
    queries = head_view(query_rows)
    start_max = jnp.full((img_count, HEADS, part_len), MASKED_SCORE, jnp.float32)
    start_sum = jnp.zeros((img_count, HEADS, part_len), jnp.float32)
    start_out = jnp.zeros((img_count, part_len, HEADS, HEAD_DIM), jnp.float32)
    whole_keys, whole_values, whole_keep = (
        lax.all_gather(key_rows, "ctx", axis=1, tiled=True),
        lax.all_gather(value_rows, "ctx", axis=1, tiled=True),
        lax.all_gather(keep_mask, "ctx", axis=1, tiled=True),
    )
    row_max, row_sum = each_block(
        lambda running, portion: stats_step(running, portion, queries),
        (start_max, start_sum),
        (whole_keys, whole_keep),
        part_len,
    )
    log_sum = row_max + jnp.log(row_sum)
    attended = each_block(
        lambda running, portion: value_step(running, portion, queries, log_sum),
        start_out,
        (whole_keys, whole_values, whole_keep),
        part_len,
    )
    attended_low = attended.reshape(tok_count, features).astype(jnp.bfloat16)
    branch = jnp.dot(attended_low, w_attn_out, preferred_element_type=jnp.float32)
    residual = inputs + branch
    normed_two, norm_two_back = jax.vjp(layer_norm, residual, gain_two)
    mixed_low = normed_two.astype(jnp.bfloat16)
    logits = lax.dot_general(
        mixed_low, w_router, (((1,), (1,)), ((), ())), preferred_element_type=jnp.float32
    )
    router_prob = jax.nn.softmax(logits, axis=-1)
    chosen = expert_ids.reshape(tok_count, 2)
    slot_index, kept_pair, source, filled = routing(
        chosen,
        slot_priority.reshape(tok_count),
        pad_mask.reshape(tok_count),
        expert_count,
        capacity,
    )
    filled_low = filled.astype(jnp.bfloat16)
    dispatched = (mixed_low[source] * filled_low[:, None]).reshape(expert_count, capacity, features)
    received = lax.all_to_all(dispatched, "expert", split_axis=0, concat_axis=1, tiled=True)
    hidden = jnp.einsum("ecd,efd->ecf", received, w_in, preferred_element_type=jnp.float32)
    active, gelu_back = jax.vjp(lambda pre_act: jax.nn.gelu(pre_act, approximate=False), hidden)
    active_low = active.astype(jnp.bfloat16)
    result = jnp.einsum(
        "ecf,efd->ecd", active_low, w_out, preferred_element_type=jnp.float32
    ).astype(jnp.bfloat16)
    returned = lax.all_to_all(result, "expert", split_axis=1, concat_axis=0, tiled=True).reshape(
        expert_count * capacity, features
    )
    kept_float = kept_pair.astype(jnp.float32)
    gate_value = jnp.take_along_axis(router_prob, chosen, axis=1) * kept_float
    picked = returned[slot_index].astype(jnp.float32)
    mixture = jnp.sum(gate_value[:, :, None] * picked, axis=1)
    output = (residual + mixture).astype(jnp.bfloat16).reshape(tokens.shape)
    grad_rows = cotangent.reshape(tok_count, features).astype(jnp.float32) * keep_rows[:, None]
    grad_gate = jnp.sum(grad_rows[:, None, :] * picked, axis=-1) * kept_float
    labels = jnp.arange(expert_count, dtype=jnp.int32)
    grad_prob = jnp.sum(
        (chosen[:, :, None] == labels[None, None, :]).astype(jnp.float32) * grad_gate[:, :, None],
        axis=1,
    )
    grad_logits = router_prob * (
        grad_prob - jnp.sum(grad_prob * router_prob, axis=-1, keepdims=True)
    )
    grad_logits_low = grad_logits.astype(jnp.bfloat16)
    slot_expert = jnp.arange(expert_count * capacity, dtype=jnp.int32) // capacity
    slot_gate = jnp.take_along_axis(router_prob[source], slot_expert[:, None], axis=1)[
        :, 0
    ] * filled.astype(jnp.float32)
    grad_result = (
        (grad_rows[source] * slot_gate[:, None])
        .astype(jnp.bfloat16)
        .reshape(expert_count, capacity, features)
    )
    grad_received = lax.all_to_all(grad_result, "expert", split_axis=0, concat_axis=1, tiled=True)
    grad_active = jnp.einsum(
        "ecd,efd->ecf", grad_received, w_out, preferred_element_type=jnp.float32
    )
    grad_hidden = gelu_back(grad_active)[0].astype(jnp.bfloat16)
    grad_w_out = jnp.einsum(
        "ecf,ecd->efd", active_low, grad_received, preferred_element_type=jnp.float32
    )
    grad_w_in = jnp.einsum(
        "ecf,ecd->efd", grad_hidden, received, preferred_element_type=jnp.float32
    )
    grad_sent = jnp.einsum(
        "ecf,efd->ecd", grad_hidden, w_in, preferred_element_type=jnp.float32
    ).astype(jnp.bfloat16)
    grad_back = lax.all_to_all(
        grad_sent, "expert", split_axis=1, concat_axis=0, tiled=True
    ).reshape(expert_count * capacity, features)
    grad_mixed = jnp.sum(grad_back[slot_index].astype(jnp.float32) * kept_float[:, :, None], axis=1)
    grad_mixed = grad_mixed + jnp.dot(grad_logits_low, w_router, preferred_element_type=jnp.float32)
    grad_router = lax.dot_general(
        grad_logits_low, mixed_low, (((0,), (0,)), ((), ())), preferred_element_type=jnp.float32
    )
    grad_residual_part, grad_gain_two = norm_two_back(grad_mixed)
    grad_residual = grad_rows + grad_residual_part
    grad_branch = grad_residual.astype(jnp.bfloat16)
    grad_w_attn_out = lax.dot_general(
        attended_low, grad_branch, (((0,), (0,)), ((), ())), preferred_element_type=jnp.float32
    )
    grad_attended = lax.dot_general(
        grad_branch, w_attn_out, (((1,), (1,)), ((), ())), preferred_element_type=jnp.float32
    ).astype(jnp.bfloat16)
    grad_out = head_view(grad_attended.reshape(img_count, part_len, features))
    row_delta = jnp.transpose(jnp.sum(grad_out.astype(jnp.float32) * attended, axis=-1), (0, 2, 1))
    start_grad = jnp.zeros((img_count, part_len, HEADS, HEAD_DIM), jnp.float32)
    whole_grads = jnp.zeros((2, img_count, whole_keys.shape[1], HEADS, HEAD_DIM), jnp.float32)

    def grad_turn(number, current):
        grad_query, grads_all = current
        offset = number * part_len
        portion = tuple(
            (
                lax.dynamic_slice_in_dim(member, offset, part_len, 1)
                for member in (whole_keys, whole_values, whole_keep)
            )
        )
        grad_query, grad_block = grad_step(
            grad_query, portion, queries, log_sum, grad_out, row_delta
        )
        grads_all = lax.dynamic_update_slice_in_dim(grads_all, grad_block, offset, 2)
        return (grad_query, grads_all)

    grad_query, whole_grads = lax.fori_loop(
        0, whole_keys.shape[1] // part_len, grad_turn, (start_grad, whole_grads)
    )
    grad_pair = lax.psum_scatter(whole_grads, "ctx", scatter_dimension=2, tiled=True)
    grad_qkv = jnp.concatenate(
        [
            grad_query.reshape(tok_count, features),
            grad_pair[0].reshape(tok_count, features),
            grad_pair[1].reshape(tok_count, features),
        ],
        axis=1,
    ).astype(jnp.bfloat16)
    grad_w_qkv = lax.dot_general(
        grad_qkv, normed_low, (((0,), (0,)), ((), ())), preferred_element_type=jnp.float32
    )
    grad_normed = jnp.dot(grad_qkv, w_qkv, preferred_element_type=jnp.float32)
    grad_input_part, grad_gain_one = norm_one_back(grad_normed)
    grad_tokens = (grad_residual + grad_input_part).reshape(tokens.shape)
    shared_pieces = jnp.concatenate(
        [grad_w_qkv, grad_w_attn_out, grad_router, grad_gain_one[None, :], grad_gain_two[None, :]],
        axis=0,
    )
    shared_layout = jnp.zeros(all_shared.shape, jnp.float32).at[shared_owner].set(shared_pieces)
    shared_grad = lax.psum_scatter(
        shared_layout, ("dp", "ctx", "expert"), scatter_dimension=0, tiled=True
    )
    expert_pieces = jnp.stack([grad_w_in, grad_w_out], axis=1).reshape(EXP_DEV * 2 * FF, features)
    expert_layout = (
        jnp.zeros(all_expert.shape, jnp.float32).at[0, expert_owner[0]].set(expert_pieces)
    )
    expert_grad = lax.psum_scatter(expert_layout, ("dp", "ctx"), scatter_dimension=1, tiled=True)
    shared_first_new, shared_second_new, shared_weight_new = adam_update(
        shared_grad, shared_first, shared_second, shared_slots.astype(jnp.float32)
    )
    expert_first_new, expert_second_new, expert_weight_new = adam_update(
        expert_grad, expert_first, expert_second, expert_slots.astype(jnp.float32)
    )
    return (
        output,
        grad_tokens,
        shared_grad,
        shared_first_new,
        shared_second_new,
        shared_weight_new,
        expert_grad,
        expert_first_new,
        expert_second_new,
        expert_weight_new,
    )


F32 = jnp.float32
BF16 = jnp.bfloat16
I32 = jnp.int32
LANES = 128
MASKED = -1e30
VMEM_LIMIT = 56 * 1024 * 1024
MICRO = 1.15e9
QUICK = (1e6, 1e3)
THEIRS = 2


def dot_nn(left, right):
    return lax.dot_general(left, right, (((1,), (0,)), ((), ())), preferred_element_type=F32)


def dot_nt(left, right):
    return lax.dot_general(left, right, (((1,), (1,)), ((), ())), preferred_element_type=F32)


def dot_tn(left, right):
    return lax.dot_general(left, right, (((0,), (0,)), ((), ())), preferred_element_type=F32)


def iota(shape, dim):
    return lax.broadcasted_iota(I32, shape, dim)


def as_bf16(mask):
    return jnp.where(mask, 1.0, 0.0).astype(BF16)


def kernel_call(
    body, out_shape, scratch=(), grid=None, in_specs=None, out_specs=None, cost=None
):
    given = dict(grid=grid, in_specs=in_specs, out_specs=out_specs)
    extra = {name: value for name, value in given.items() if value is not None}
    flops, moved = cost if cost else (1e8, 1e6)
    name = getattr(body, "func", body).__name__
    return pl.pallas_call(
        body,
        name=name,
        out_shape=out_shape,
        scratch_shapes=list(scratch),
        compiler_params=pltpu.CompilerParams(vmem_limit_bytes=VMEM_LIMIT),
        cost_estimate=pl.CostEstimate(flops=int(flops), bytes_accessed=int(moved), transcendentals=0),
        **extra,
    )


def sds(shape, dtype):
    return jax.ShapeDtypeStruct(shape, dtype)


def route_body(n_exp, capacity, ids_ref, prio_ref, live_ref, cot_ref, row_ref, col_ref, sent_ref):
    toks = ids_ref.shape[1]
    half = capacity // 2
    prio_row = prio_ref[...]
    prio_col = jnp.transpose(jnp.broadcast_to(prio_row, (8, toks)))[:, :1]
    earlier = (prio_col < prio_row) | (
        (prio_col == prio_row) & (iota((toks, toks), 0) < iota((toks, toks), 1))
    )
    live = live_ref[...] > 0.0
    labels = iota((n_exp, toks), 0)
    first, second = ids_ref[0:1, :], ids_ref[1:2, :]
    wanted = ((labels == first) | (labels == second)) & live
    taken = dot_nn(as_bf16(wanted), as_bf16(earlier))
    places = []
    for chosen in (first, second):
        slot = jnp.sum(jnp.where(labels == chosen, taken, 0.0), axis=0, keepdims=True).astype(I32)
        kept = live & (slot < capacity)
        shard = chosen >> 2
        local = chosen & 3
        core = (slot >= half).astype(I32)
        target = ((((local >> 1) * 2 + core) * 2 + (local & 1)) * (n_exp // 4)) + shard
        places.append(jnp.where(kept, target * half + slot - core * half, -1))
    row_id = iota((8, toks), 0)
    rows = jnp.where(row_id == 0, places[0], jnp.where(row_id == 1, places[1], -1))
    row_ref[...] = rows
    col_ref[...] = jnp.transpose(rows.astype(F32)).astype(I32)
    slots = sent_ref.shape[0]
    spots = iota((slots, toks), 0)
    picks = as_bf16((spots == places[0]) | (spots == places[1]))
    sent_ref[...] = dot_nn(picks, cot_ref[...]).astype(BF16)


def unpack_body(spots_at, n_earlier, pos_ref, *refs):
    n_pieces = len(spots_at)
    pieces, rest = refs[:n_pieces], refs[n_pieces:]
    out_ref, held = rest[-2], rest[-1]

    @pl.when(pl.program_id(0) == 0)
    def _():
        gather_pieces(pieces, held)

    wanted = pos_ref[...]
    size = pieces[0].shape[0]
    place = jnp.full(wanted.shape, -1, I32)
    for number, at in enumerate(spots_at):
        inside = (wanted >= at) & (wanted < at + size)
        place = jnp.where(inside, wanted - at + number * size, place)
    picks = as_bf16(place == iota((wanted.shape[0], held.shape[0]), 1))
    value = dot_nn(picks, held[...])
    for earlier in rest[:n_earlier]:
        value = value + earlier[...].astype(F32)
    out_ref[...] = value.astype(BF16)


def gather_pieces(pieces, held):
    at = 0
    for piece in pieces:
        held[at : at + piece.shape[0], :] = piece[...]
        at += piece.shape[0]


def gather_halves(pieces, held):
    size = pieces[0].shape[0] // 2
    for number, piece in enumerate(pieces[:4]):
        held[number * size : (number + 1) * size, :] = piece[:size, :]
    at = 4 * size
    for piece in pieces[4:]:
        held[at : at + piece.shape[0], :] = piece[...]
        at += piece.shape[0]


def normalize(values):
    center = values - jnp.mean(values, axis=-1, keepdims=True)
    spread = jnp.mean(center * center, axis=-1, keepdims=True)
    scale = lax.rsqrt(spread + NORM_EPSILON)
    return center * scale, scale


def head_lanes(head, rows):
    return (iota((rows, LANES), 1) // HEAD_DIM) == head


def of_head(values, head):
    return jnp.where(head_lanes(head, values.shape[0]), values, jnp.zeros_like(values))


def by_head(first, second):
    return jnp.where(head_lanes(0, first.shape[0]), first, second)


def forward_body(
    n_exp, own_ref, other_ref, keep_ref, w_ref, pos_ref,
    qkv_ref, normed_ref, attended_ref, residual_ref, prob_ref, sent_ref, lse_col_ref, lse_row_ref,
    mixed_ref,
):
    toks, width = own_ref.shape
    router = 4 * width
    gain_one = w_ref[router + n_exp : router + n_exp + 16, :].astype(F32)
    gain_two = gain_one[1:2, :]
    gain_one = gain_one[0:1, :]
    for part, ref in enumerate((own_ref, other_ref)):
        normed = normalize(ref[...].astype(F32))[0] * gain_one
        low = normed.astype(BF16)
        if part == 0:
            normed_ref[...] = low
        rows = pl.ds(part * toks, toks)
        for third in range(3):
            made = dot_nt(low, w_ref[third * width : (third + 1) * width, :]).astype(BF16)
            if third == 0:
                made = made * jnp.asarray(HEAD_DIM ** (-0.5), BF16)
            qkv_ref[rows, third * width : (third + 1) * width] = made
    bias = jnp.where(keep_ref[...] > 0.0, 0.0, MASKED)
    lane = iota((toks, LANES), 1)
    logs = jnp.zeros((toks, LANES), F32)
    for at in range(0, width, LANES):
        queries = qkv_ref[0:toks, at : at + LANES]
        keys = qkv_ref[:, width + at : width + at + LANES]
        values = qkv_ref[:, 2 * width + at : 2 * width + at + LANES]
        made = []
        for head in range(2):
            score = dot_nt(of_head(queries, head), keys) + bias
            top = jnp.max(score, axis=-1, keepdims=True)
            grown = jnp.exp(score - top)
            total = jnp.sum(grown, axis=-1, keepdims=True)
            made.append(dot_nn(grown.astype(BF16), values) * (1.0 / total))
            logs = jnp.where(lane == 2 * (at // LANES) + head, top + jnp.log(total), logs)
        attended_ref[:, at : at + LANES] = by_head(*made)
    lse_col_ref[...] = logs
    lse_row_ref[...] = jnp.transpose(lse_col_ref[...])[:8, :]
    branch = dot_nn(attended_ref[...].astype(BF16), w_ref[3 * width : 4 * width, :])
    residual = own_ref[...].astype(F32) + branch
    residual_ref[...] = residual
    mixed = (normalize(residual)[0] * gain_two).astype(BF16)
    mixed_ref[...] = mixed
    logits = dot_nt(mixed, w_ref[router : router + n_exp, :])
    prob_ref[...] = jax.nn.softmax(logits, axis=-1)
    slots = sent_ref.shape[0]
    spots = iota((slots, toks), 0)
    picks = as_bf16((spots == pos_ref[0:1, :]) | (spots == pos_ref[1:2, :]))
    sent_ref[...] = dot_nn(picks, mixed).astype(BF16)


def gelu_parts(value):
    below = 0.5 + 0.5 * lax.erf(value * 0.7071067811865476)
    return value * below, below + value * jnp.exp(-0.5 * value * value) * 0.3989422804014327


def expert_body(
    n_exp, expert_ref, got_ref, cot_ref, near_ref, far_in_ref, far_out_ref, router_ref,
    active_ref, hidden_ref, scaled_ref, result_ref, back_ref, router_grad_ref,
):
    @pl.when(pl.program_id(0) == 0)
    def _():
        router_grad_ref[...] = jnp.zeros_like(router_grad_ref)

    expert = expert_ref[0]
    got, cot = got_ref[...], cot_ref[...]
    labels = iota((got.shape[0], n_exp), 1)
    share = jax.nn.softmax(dot_nt(got, router_ref[...]), axis=-1)
    gate = jnp.sum(jnp.where(labels == expert, share, 0.0), axis=-1, keepdims=True)
    scaled = (cot.astype(F32) * gate).astype(BF16)
    scaled_ref[...] = scaled
    half = near_ref.shape[0] // 2
    total = total_back = 0.0
    halves = ((near_ref[:half, :], near_ref[half:, :]), (far_in_ref[...], far_out_ref[...]))
    for number, (w_in, w_out) in enumerate(halves):
        at = slice(number * half, (number + 1) * half)
        active, slope = gelu_parts(dot_nt(got, w_in))
        low = active.astype(BF16)
        active_ref[:, at] = low
        grad = (dot_nt(scaled, w_out) * slope).astype(BF16)
        hidden_ref[:, at] = grad
        total = total + dot_nn(low, w_out)
        total_back = total_back + dot_nn(grad, w_in)
    result = total.astype(BF16)
    result_ref[...] = result
    inner = jnp.sum(result.astype(F32) * cot.astype(F32), axis=-1, keepdims=True)
    grad = share * (jnp.where(labels == expert, inner, 0.0) - gate * inner)
    low = grad.astype(BF16)
    back_ref[...] = (total_back + dot_nn(low, router_ref[...])).astype(BF16)
    router_grad_ref[...] += dot_tn(low, got)


def weight_grad_body(hidden_ref, active_ref, got_ref, scaled_ref, *outs):
    size = outs[0].shape[0]
    for number, out in enumerate(outs):
        left, right = ((hidden_ref, got_ref), (active_ref, scaled_ref))[number % 2]
        at = slice((1 - number // 2) * size, (2 - number // 2) * size)
        out[...] = dot_tn(left[:, at], right[...]).astype(out.dtype)


def norm_back(hat, scale, gain, grad):
    inner = grad * gain
    first = jnp.mean(inner, axis=-1, keepdims=True)
    second = jnp.mean(inner * hat, axis=-1, keepdims=True)
    return (inner - first - hat * second) * scale


def middle_body(
    n_exp, back_ref, pos_ref, residual_ref, cot_ref, keep_ref, attended_ref, w_ref,
    grad_ref, out_grad_ref, delta_col_ref, delta_row_ref, gain_ref,
):
    toks, width = residual_ref.shape
    router = 4 * width
    slots = back_ref.shape[0]
    gain_two = w_ref[router + n_exp : router + n_exp + 16, :].astype(F32)[1:2, :]
    spots = iota((toks, slots), 1)
    picks = as_bf16((spots == pos_ref[:, 0:1]) | (spots == pos_ref[:, 1:2]))
    grad_mixed = dot_nn(picks, back_ref[...])
    hat, scale = normalize(residual_ref[...])
    gain_ref[...] = jnp.broadcast_to(
        jnp.sum(grad_mixed * hat, axis=0, keepdims=True), gain_ref.shape
    )
    grad_rows = cot_ref[...].astype(F32) * keep_ref[...]
    grad = grad_rows + norm_back(hat, scale, gain_two, grad_mixed)
    grad_ref[...] = grad
    low = grad.astype(BF16)
    out_grad = dot_nt(low, w_ref[3 * width : 4 * width, :]).astype(BF16)
    out_grad_ref[...] = out_grad
    product = out_grad.astype(F32) * attended_ref[...]
    delta = jnp.zeros((toks, LANES), F32)
    lane = iota((toks, LANES), 1)
    for head in range(HEADS):
        at = (head // 2) * LANES
        part = jnp.where(head_lanes(head % 2, toks), product[:, at : at + LANES], 0.0)
        delta = jnp.where(lane == head, jnp.sum(part, axis=-1, keepdims=True), delta)
    delta_col_ref[...] = delta
    delta_row_ref[...] = jnp.transpose(delta)[:8, :]


def inner_body(
    n_exp, qkv_ref, out_grad_ref, lse_ref, delta_ref, keep_ref, attended_ref, grad_ref, router_grad_ref, gain_ref,
    query_ref, kv_ref, early_ref,
):
    toks, width = out_grad_ref.shape
    bias = jnp.where(keep_ref[...] > 0.0, 0.0, MASKED)
    for at in range(0, width, LANES):
        queries = qkv_ref[0:toks, at : at + LANES]
        keys = qkv_ref[:, width + at : width + at + LANES]
        values = qkv_ref[:, 2 * width + at : 2 * width + at + LANES]
        out_grad = out_grad_ref[:, at : at + LANES]
        made = []
        for head in range(2):
            line = 2 * (at // LANES) + head
            score = dot_nt(of_head(queries, head), keys) + bias
            prob = jnp.exp(score - lse_ref[:, line : line + 1])
            slope = dot_nt(of_head(out_grad, head), values)
            grad = (prob * (slope - delta_ref[:, line : line + 1])).astype(BF16)
            made.append(
                (dot_nn(grad, keys), dot_tn(grad[:, :toks], queries), dot_tn(prob[:, :toks].astype(BF16), out_grad))
            )
        query_ref[:, at : at + LANES] = (by_head(made[0][0], made[1][0]) * HEAD_DIM ** (-0.5)).astype(BF16)
        kv_ref[0, :, at : at + LANES] = by_head(made[0][1], made[1][1])
        kv_ref[1, :, at : at + LANES] = by_head(made[0][2], made[1][2])
    early_ref[0:width, :] = dot_tn(attended_ref[...].astype(BF16), grad_ref[...].astype(BF16)).astype(BF16)
    early_ref[width : width + n_exp, :] = router_grad_ref[...].astype(BF16)
    row_id = iota((16, width), 0)
    early_ref[width + n_exp : width + n_exp + 16, :] = jnp.where(
        row_id == 0, gain_ref[0:1, :], 0.0
    ).astype(BF16)


def outer_body(
    n_exp, qkv_ref, out_grad_ref, sums_ref, keep_ref, query_ref, kv_ref, normed_ref, own_ref, w_ref, early_ref,
    query_rows_ref, key_rows_ref, value_rows_ref, rest_ref, grad_normed_ref, held,
):
    toks, width = query_ref.shape
    held[:, 0:width] = query_ref[...]
    bias = jnp.where(keep_ref[...] > 0.0, 0.0, MASKED)
    for at in range(0, width, LANES):
        queries = qkv_ref[toks : 2 * toks, at : at + LANES]
        out_grad = out_grad_ref[:, at : at + LANES]
        keys = qkv_ref[0:toks, width + at : width + at + LANES]
        values = qkv_ref[0:toks, 2 * width + at : 2 * width + at + LANES]
        made = []
        for head in range(2):
            line = 2 * (at // LANES) + head
            score = dot_nt(of_head(keys, head), queries) + bias
            prob = jnp.exp(score - sums_ref[line : line + 1, :])
            slope = dot_nt(of_head(values, head), out_grad)
            grad = (prob * (slope - sums_ref[HEADS + line : HEADS + line + 1, :])).astype(BF16)
            made.append((dot_nn(grad, queries), dot_nn(prob.astype(BF16), out_grad)))
        for number in range(2):
            total = kv_ref[number, :, at : at + LANES] + by_head(made[0][number], made[1][number])
            held[:, (number + 1) * width + at : (number + 1) * width + at + LANES] = total.astype(BF16)
    for third, ref in enumerate((query_rows_ref, key_rows_ref, value_rows_ref)):
        ref[...] = dot_tn(held[:, third * width : (third + 1) * width], normed_ref[...]).astype(BF16)
    grad_normed = dot_nn(held[...], w_ref[0 : 3 * width, :])
    grad_normed_ref[...] = grad_normed
    gain_grad = jnp.sum(grad_normed * normalize(own_ref[...].astype(F32))[0], axis=0, keepdims=True)
    rest_ref[0:16, :] = jnp.where(
        iota((16, width), 0) == 0, gain_grad, 0.0
    ).astype(BF16)
    rest_ref[16:, :] = early_ref[...]


def step_body(keep_a, got_a, keep_b, got_b, go_a, go_b, stay_a, stay_b):
    half = go_a.shape[0]
    for keep, got, go, stay in ((keep_a, got_a, go_a, stay_a), (keep_b, got_b, go_b, stay_b)):
        go[...] = total_f32(keep[half:, :], got[half:, :]).astype(BF16)
        stay[...] = total_f32(keep[:half, :], got[:half, :]).astype(BF16)


def tokens_body(n_exp, grad_normed_ref, own_ref, w_ref, grad_ref, out_ref):
    at = 4 * own_ref.shape[1] + n_exp
    gain_one = w_ref[at : at + 16, :].astype(F32)[0:1, :]
    hat, scale = normalize(own_ref[...].astype(F32))
    out_ref[...] = grad_ref[...] + norm_back(hat, scale, gain_one, grad_normed_ref[...])


def spread_body(starts, n_in, pos_ref, *refs):
    mine, far, outs, held = refs[:n_in], refs[n_in : 2 * n_in], refs[2 * n_in : -1], refs[-1]
    at = 0
    for one, two in zip(mine, far):
        held[at : at + one.shape[0], :] = total_f32(one[...], two[...]).astype(BF16)
        at += one.shape[0]
    size = outs[0].shape[0]
    for number, start in enumerate(starts):
        picks = as_bf16(iota((size, held.shape[0]), 0) + start == pos_ref[...])
        outs[number][...] = dot_nn(picks, held[...]).astype(BF16)


def room_of(owned, n_dev):
    return min(owned, -(-(owned // n_dev * 5 // 4) // 16) * 16)


def sent_at(partner):
    return ((partner >> 2) & 1) * 4 + (partner & 1) * 2 + ((partner >> 1) & 1)


def got_at(partner):
    return ((partner >> 1) & 1) * 4 + ((partner >> 2) & 1) * 2 + (partner & 1)


def sent_cell(cell):
    return (cell >> 2) * 4 + (cell & 1) * 2 + ((cell >> 1) & 1)


def plan_body(n_dev, room, me_ref, owner_ref, row_ref, col_ref, most_ref):
    me = me_ref[0]
    owned = owner_ref.shape[1]
    source = owner_ref[...] >> (owned.bit_length() - 1)
    spot = owner_ref[...] & (owned - 1)
    total = n_dev * n_dev
    classes = iota((n_dev, owned), 0)
    member = jnp.concatenate([classes == source[t : t + 1, :] for t in range(n_dev)], axis=0)
    ones = as_bf16(member)
    step = 256
    before = as_bf16(iota((step, step), 0) < iota((step, step), 1))
    count = jnp.zeros((total, 1), F32)
    ranks = []
    for at in range(0, owned, step):
        part = ones[:, at : at + step]
        ranks.append(dot_nn(part, before) + count)
        count = count + jnp.sum(part.astype(F32), axis=1, keepdims=True)
    most_ref[...] = jnp.broadcast_to(jnp.max(count, axis=0, keepdims=True).astype(I32), most_ref.shape)
    line = iota((total, 1), 0)
    to, of = line // n_dev, line % n_dev
    rank = jnp.concatenate(ranks, axis=1)
    turn = ((rank + 0.5) * (1.0 / room)).astype(I32)
    inside = rank.astype(I32) + turn * ((n_dev - 1) * room)
    wanted = member & (to == me)
    arrives = jnp.sum(jnp.where(wanted, inside + got_at(of ^ to) * room, 0), axis=0, keepdims=True)
    returns = jnp.sum(jnp.where(wanted, inside + sent_at(of ^ to) * room, 0), axis=0, keepdims=True)
    leaves = inside + sent_at(of ^ to) * room
    half = owned // LANES
    found = jnp.zeros((2 * half, LANES), F32)
    high, lanes = iota((half, owned), 0), iota((LANES, owned), 0)
    for t in range(n_dev):
        mine = slice(t * n_dev, (t + 1) * n_dev)
        chosen = member[mine] & (of[mine] == me)
        place = jnp.sum(jnp.where(chosen, leaves[mine], 0), axis=0, keepdims=True)
        hit = (spot[t : t + 1, :] // LANES == high) & (source[t : t + 1, :] == me)
        left = jnp.concatenate(
            [jnp.where(hit, place // LANES, 0), jnp.where(hit, place % LANES, 0)], axis=0
        ).astype(F32).astype(BF16)
        found = found + dot_nt(left, as_bf16((spot[t : t + 1, :] % LANES) == lanes))
    found = found[:half] * float(LANES) + found[half:]
    leave_row = jnp.concatenate([found[a : a + 1, :] for a in range(half)], axis=1)
    block = ((leave_row + 0.5) * (1.0 / room)).astype(I32)
    round_no, cell = block // n_dev, block % n_dev
    comes = leave_row.astype(I32) + (round_no * n_dev + got_at(sent_cell(cell)) - block) * room
    rows = jnp.concatenate(
        [leave_row, arrives.astype(F32), returns.astype(F32), comes.astype(F32), jnp.zeros((4, owned), F32)], axis=0
    )
    row_ref[...] = rows.astype(I32)
    col_ref[...] = jnp.transpose(rows).astype(I32)


LEAVES, ARRIVES, RETURNS, COMES = range(4)


def put_rows(line, base_ref, pos_ref, held, outs, tile):
    wanted = pos_ref[line : line + 1, :] - base_ref[0]
    base = 0
    for out in outs:
        for at in range(0, out.shape[0], tile):
            picks = as_bf16(iota((tile, held.shape[0]), 0) + (base + at) == wanted)
            out[at : at + tile, :] = dot_nn(picks, held[...]).astype(BF16)
        base += out.shape[0]


def put_body(line, tile, base_ref, pos_ref, rows_ref, *outs):
    put_rows(line, base_ref, pos_ref, rows_ref, outs, tile)


def sum_put_body(line, tile, cells, n_in, base_ref, pos_ref, *refs):
    mine, theirs, outs, held = refs[:n_in], refs[n_in : 2 * n_in], refs[2 * n_in : -1], refs[-1]
    size = mine[0].shape[0]
    for number in range(n_in):
        held[number * size : (number + 1) * size, :] = total_f32(mine[number][...], theirs[number][...]).astype(BF16)
    wanted = pos_ref[line : line + 1, :] - base_ref[0]
    for cell, out in zip(cells, outs):
        for at in range(0, out.shape[0], tile):
            picks = as_bf16(iota((tile, held.shape[0]), 0) + (cell * out.shape[0] + at) == wanted)
            out[at : at + tile, :] = dot_nn(picks, held[...]).astype(BF16)


def take_body(line, tile, base_ref, pos_ref, *refs):
    pieces, out, held = refs[:-2], refs[-2], refs[-1]
    gather_halves(pieces, held)
    for at in range(0, out.shape[0], tile):
        wanted = pos_ref[at : at + tile, line : line + 1] - base_ref[0]
        picks = as_bf16(iota((tile, held.shape[0]), 1) == wanted)
        out[at : at + tile, :] = dot_nn(picks, held[...]).astype(BF16)


def adam_body(n_in, pos_ref, *refs):
    pieces, (first_ref, second_ref, weight_ref) = refs[:n_in], refs[n_in : n_in + 3]
    grad_ref, first_new, second_new, weight_new, held = refs[n_in + 3 :]

    @pl.when(pl.program_id(0) == 0)
    def _():
        gather_halves(pieces, held)

    picks = as_bf16(iota((grad_ref.shape[0], held.shape[0]), 1) == pos_ref[:, COMES : COMES + 1])
    grad = dot_nn(picks, held[...])
    grad_ref[...] = grad
    made = adam_update(grad, first_ref[...], second_ref[...], weight_ref[...].astype(F32))
    first_new[...], second_new[...], weight_new[...] = made


def mixture_body(result_ref, pos_ref, ids_ref, prob_ref, residual_ref, out_ref):
    toks = residual_ref.shape[0]
    slots = result_ref.shape[0]
    share = prob_ref[...]
    total = residual_ref[...]
    for number in range(2):
        picks = as_bf16(iota((toks, slots), 1) == pos_ref[:, number : number + 1])
        mine = iota(share.shape, 1) == ids_ref[:, number : number + 1]
        gate = jnp.sum(jnp.where(mine, share, 0.0), axis=-1, keepdims=True)
        total = total + gate * dot_nn(picks, result_ref[...])
    out_ref[...] = total.astype(BF16)


SWAP = [(0, 1), (1, 0)]
SWAP_CORE = [(0, 1), (1, 0), (2, 3), (3, 2)]
SWAP_Y = [(0, 2), (2, 0), (1, 3), (3, 1)]


def swap_x(value):
    return lax.ppermute(value, "ctx", SWAP)


def swap_y(value):
    return lax.ppermute(value, "dp", SWAP_Y)


def swap_x_y(value):
    return lax.ppermute(value, ("dp", "ctx"), [(i, i ^ 5) for i in range(8)])


def swap_core(value):
    return lax.ppermute(value, "dp", SWAP_CORE)


def shift_z(value, by):
    count = lax.axis_size("expert")
    return lax.ppermute(value, "expert", [(i, (i + by) % count) for i in range(count)])


def after(values, *others):
    values = list(values)
    return lax.optimization_barrier((*values, *others))[: len(values)]


def total_f32(first, second):
    return first.astype(F32) + second.astype(F32)


def on_chip_experts(
    tokens, cotangent, pad_mask, expert_ids, slot_priority, shared_slots, shared_first, shared_second,
    shared_owner, expert_slots, expert_first, expert_second, expert_owner,
):
    toks, width = tokens.shape[1], tokens.shape[2]
    n_z = lax.axis_size("expert")
    n_exp = EXP_DEV * n_z
    capacity = (10 * toks + 4 * n_exp - 1) // (4 * n_exp)
    slots = n_exp * capacity
    everyone = ("dp", "ctx", "expert")
    dp, mx, mz = lax.axis_index("dp"), lax.axis_index("ctx"), lax.axis_index("expert")
    my, mc = dp // 2, dp % 2

    own_count = shared_slots.shape[0]
    stride = -(-own_count // 8) * 8
    padded = jnp.pad(shared_slots, ((0, stride - own_count), (0, 0)))
    line = [padded] + [shift_z(padded, by) for by in range(1, n_z)]
    part_a = jnp.concatenate(line[: n_z // 2], axis=0)
    part_b = jnp.concatenate(line[n_z // 2 :], axis=0)
    a_y, b_x = swap_y(part_a), swap_x(part_b)
    pair_a, pair_b = jnp.concatenate([part_a, a_y], axis=0), jnp.concatenate([part_b, b_x], axis=0)
    first_near, last_near = [pair_a, pair_b], [swap_x(pair_a), swap_y(pair_b)]
    first_far = [swap_core(piece) for piece in first_near]

    owner_dev, owner_row = shared_owner // own_count, shared_owner % own_count
    o_z, o_x, o_dp = owner_dev % n_z, owner_dev // n_z % 2, owner_dev // (n_z * 2)
    in_c, in_y, in_x = (o_dp % 2) ^ mc, (o_dp // 2) ^ my, o_x ^ mx
    in_z = (mz - o_z + n_z) % n_z
    late = in_z // (n_z // 2)
    cross = jnp.where(late == 0, in_y + 2 * in_x, in_x + 2 * in_y)
    place = (((in_c * 2 + late) * 4 + cross) * (n_z // 2) + in_z % (n_z // 2)) * stride + owner_row
    total_slots = 8 * n_z * stride
    row_count = -(-shared_owner.shape[0] // 16) * 16
    place_col = jnp.pad(place, (0, row_count - place.shape[0]), constant_values=-1)[:, None]
    gain_at = 4 * width + n_exp
    none = jnp.full((15,), -1, I32)
    place_row = jnp.concatenate(
        [place[: 3 * width], place[gain_at : gain_at + 1], none, place[3 * width : gain_at], place[gain_at + 1 :], none]
    )[None, :]

    half_slots = total_slots // 2
    piece = half_slots // 4
    row_tile = row_count // 2 if row_count % 32 == 0 else row_count

    def unpack(spots, pieces, earlier):
        rows_of = lambda columns: pl.BlockSpec((row_tile, columns), lambda i: (i, 0))
        return kernel_call(
            functools.partial(unpack_body, spots, len(earlier)), sds((row_count, width), BF16),
            [pltpu.VMEM((len(pieces) * piece, width), BF16)],
            grid=(row_count // row_tile,),
            in_specs=[rows_of(1)] + [pl.BlockSpec((piece, width), lambda i: (0, 0))] * len(pieces)
            + [rows_of(width)] * len(earlier),
            out_specs=rows_of(width),
            cost=(7 * MICRO, 1e6),
        )(place_col, *pieces, *earlier)

    first_rows = unpack(
        [0, 2 * piece, half_slots, half_slots + 2 * piece], [*first_near, *first_far], []
    )
    last_near = after(last_near, first_rows)
    last_far = [swap_core(piece) for piece in last_near]

    own, other = tokens[0], swap_x(tokens[0])
    ids = expert_ids[0]
    live = pad_mask.astype(F32)
    live_other = swap_x(pad_mask).astype(F32)
    keep_row = jnp.concatenate([live, live_other], axis=1)
    keep_col = live.reshape(toks, 1)
    pos_row, pos_col, cot_sent = kernel_call(
        functools.partial(route_body, n_exp, capacity),
        (sds((8, toks), I32), sds((toks, 8), I32), sds((slots, width), BF16)),
        cost=(4 * MICRO, 1e6),
    )(*after([ids.T], other), slot_priority.astype(F32), live, cotangent[0])

    def exchange(rows):
        return lax.all_to_all(rows, everyone, split_axis=0, concat_axis=0, tiled=True)

    cot_got = exchange(after([cot_sent], a_y, b_x)[0])

    local = my * 2 + mx
    group, n_dev = dp * 2 + mx, 8
    owned = expert_slots.shape[1]
    room = room_of(owned, n_dev)
    owner = jnp.transpose(
        expert_owner[0].reshape(2, 2, 2, 2, FF // 2), (0, 3, 1, 2, 4)
    ).reshape(n_dev, owned)
    held = [pltpu.VMEM((n_dev * room, width), BF16)]
    sent_shapes = [sds((2 * room, width), BF16)] * 4
    smem, vmem = pl.BlockSpec(memory_space=pltpu.SMEM), pl.BlockSpec(memory_space=pltpu.VMEM)
    plan_row, plan_col, most = kernel_call(
        functools.partial(plan_body, n_dev, room),
        (sds((8, owned), I32), sds((owned, 8), I32), sds((8, LANES), I32)), cost=(5 * MICRO, 1e6),
        in_specs=[smem, vmem],
    )(group.astype(I32).reshape(1), *after([owner], part_a, part_b, pos_row, other))
    rounds = (most[0, 0] + room - 1) // room
    def with_base(body, out_shape, scratch, arrays, number=0, cost=QUICK):
        base = jnp.full((1,), number * n_dev * room, I32)
        return kernel_call(
            body, out_shape, scratch, in_specs=[smem] + [vmem] * len(arrays), cost=cost
        )(base, *arrays)

    def over_links(pieces, *others):
        last = after(pieces[3:], *others)[0] if others else pieces[3]
        return [pieces[0], swap_x(pieces[1]), swap_y(pieces[2]), swap_x_y(last)]

    def over_cores(got):
        far = [jnp.concatenate([got[at][room:], got[at + 1][room:]], axis=0) for at in (0, 2)]
        return [*got, swap_core(far[0]), swap_core(far[1])]

    put_leaving = functools.partial(put_body, LEAVES, room)
    take_tile = 256 if owned % 256 == 0 else owned
    take_arrived = functools.partial(take_body, ARRIVES, take_tile)
    leaving = with_base(
        put_leaving, sent_shapes, (), [*after([plan_row], a_y, b_x), expert_slots[0]], 0, (8 * MICRO, 1e6)
    )
    moved = over_links(after(leaving, *last_near))

    weights = unpack(
        [piece, 3 * piece, half_slots + piece, half_slots + 3 * piece], [*last_near, *last_far], [first_rows]
    )

    (qkv, normed, attended, residual, prob, sent, lse_col, lse_row) = kernel_call(
        functools.partial(forward_body, n_exp),
        (
            sds((2 * toks, 3 * width), BF16), sds((toks, width), BF16), sds((toks, width), F32),
            sds((toks, width), F32), sds((toks, n_exp), F32), sds((slots, width), BF16),
            sds((toks, LANES), F32), sds((8, toks), F32),
        ),
        [pltpu.VMEM((toks, width), BF16)],
        cost=(13 * MICRO, 1e6),
    )(*after([own], cot_got), other, keep_row, weights, pos_row)
    got = exchange(sent)
    moved = over_cores(after(moved, sent))
    near_weights = with_base(take_arrived, sds((owned, width), BF16), held, [plan_col, *moved])
    far_weights = [swap_core(near_weights[: FF // 2]), swap_core(near_weights[FF // 2 :])]

    def more_weights(number, totals):
        leaving = with_base(put_leaving, sent_shapes, (), [plan_row, expert_slots[0]], number)
        moved = over_cores(over_links(leaving))
        part = with_base(take_arrived, sds((owned, width), BF16), held, [plan_col, *moved], number)
        there = swap_core(part)
        return totals[0] + part, totals[1] + there[: FF // 2], totals[2] + there[FF // 2 :]

    got, *expert_weights = after([got, near_weights, *far_weights])
    near_weights, *far_weights = lax.fori_loop(1, rounds, more_weights, tuple(expert_weights))

    expert_id = (mz * EXP_DEV + local).astype(I32).reshape(1)
    tile = 256 if slots % 256 == 0 else slots
    router_rows = weights[4 * width : 4 * width + n_exp]
    whole = lambda shape: pl.BlockSpec(shape, lambda i: (0, 0))
    rows_of = lambda columns: pl.BlockSpec((tile, columns), lambda i: (i, 0))
    active, hidden, scaled, result, back, router_grad = kernel_call(
        functools.partial(expert_body, n_exp),
        (
            sds((slots, FF), BF16), sds((slots, FF), BF16), sds((slots, width), BF16),
            sds((slots, width), BF16), sds((slots, width), BF16), sds((n_exp, width), F32),
        ),
        grid=(slots // tile,),
        in_specs=[
            pl.BlockSpec(memory_space=pltpu.SMEM), rows_of(width), rows_of(width),
            whole((FF, width)), whole((FF // 2, width)), whole((FF // 2, width)), whole((n_exp, width)),
        ],
        out_specs=(
            rows_of(FF), rows_of(FF), rows_of(width), rows_of(width), rows_of(width), whole((n_exp, width)),
        ),
        cost=(19 * MICRO, 1e6),
    )(expert_id, got, cot_got, near_weights, *far_weights, router_rows)
    back_got = exchange(back)

    halves = [sds((FF // 2, width), BF16)] * 2 + [sds((FF // 2, width), F32)] * 2
    *theirs, mine_in, mine_out = kernel_call(weight_grad_body, halves, cost=(10 * MICRO, 1e6))(
        hidden, active, got, scaled
    )
    theirs_got, mine = [swap_core(part) for part in theirs], (mine_in, mine_out)
    held_owned = [pltpu.VMEM((owned, width), BF16)]

    def returning(cells, number=0):
        body = functools.partial(sum_put_body, RETURNS, room, cells, 2)
        return with_base(body, [sent_shapes[0]] * len(cells), held_owned, [plan_row, *mine, *theirs_got], number, (4 * MICRO, 1e6))

    moved_x, moved_xy = returning((1, 3))
    moved_0, moved_y = returning((0, 2))
    moved = [moved_0, moved_x, moved_y, moved_xy]
    back_got = after([back_got], *moved)[0]

    grad_residual, out_grad, delta_col, delta_row, gain_two = kernel_call(
        functools.partial(middle_body, n_exp),
        (
            sds((toks, width), F32), sds((toks, width), BF16), sds((toks, LANES), F32),
            sds((8, toks), F32), sds((8, width), F32),
        ),
        cost=(6 * MICRO, 1e6),
    )(back_got, pos_col, residual, cotangent[0], keep_col, attended, weights)
    out_grad_other = swap_x(out_grad)
    sums_other = swap_x(jnp.concatenate([lse_row, delta_row], axis=0))
    query_grad, kv_grad, early = kernel_call(
        functools.partial(inner_body, n_exp),
        (sds((toks, width), BF16), sds((2, toks, width), F32), sds((width + n_exp + 16, width), BF16)),
        cost=(15 * MICRO, 1e6),
    )(qkv, out_grad, lse_col, delta_col, keep_row, attended, grad_residual, router_grad, gain_two)
    moved = over_links(moved, out_grad_other, query_grad, sums_other)
    result_got = exchange(after([result], query_grad)[0])
    *late, grad_normed = kernel_call(
        functools.partial(outer_body, n_exp),
        [sds((rows, width), BF16) for rows in (width, width, width, place_row.shape[1] - 3 * width)]
        + [sds((toks, width), F32)],
        [pltpu.VMEM((toks, 3 * width), BF16)],
        cost=QUICK,
    )(
        qkv, *after([out_grad_other], *moved[1:3]), sums_other, keep_col, query_grad, kv_grad, normed, own, weights, early,
    )
    late_far = [swap_core(part) for part in late]
    quarter = half_slots // 2
    eighth, sixteenth = quarter // 2, quarter // 4
    count = place_row.shape[1]

    def spread(starts, *others):
        return kernel_call(
            functools.partial(spread_body, starts, len(late)), [sds((eighth, width), BF16)] * 2,
            [pltpu.VMEM((count, width), BF16)], cost=QUICK,
        )(*after([place_row], *others), *late, *late_far)

    sends = spread((eighth, quarter + eighth), moved[3])
    got_a, got_b = swap_x(sends[0]), swap_y(sends[1])
    keeps = spread((0, quarter), *sends)
    grad_tokens = kernel_call(
        functools.partial(tokens_body, n_exp), sds((toks, width), F32), cost=QUICK
    )(*after([grad_normed], *sends), own, weights, grad_residual)

    got_a, got_b = after([got_a, got_b], grad_tokens)
    go_a, go_b, sum_a, sum_b = kernel_call(
        step_body, [sds((sixteenth, width), BF16)] * 4, cost=QUICK
    )(keeps[0], got_a, keeps[1], got_b)
    got_a, got_b = swap_y(go_a), swap_x(go_b)
    moved = over_cores(after(moved, go_a))
    sum_a = total_f32(sum_a, got_a).astype(BF16)
    sum_b = total_f32(sum_b, got_b).astype(BF16)
    lines = [sum_a[i * stride : (i + 1) * stride] for i in range(n_z // 2)]
    lines += [sum_b[i * stride : (i + 1) * stride] for i in range(n_z // 2)]
    output = kernel_call(
        mixture_body, sds((toks, width), BF16), cost=QUICK
    )(*after([result_got], *lines), pos_col, ids, prob, residual)
    tile = 256 if owned % 256 == 0 else owned
    rows_of = lambda columns: pl.BlockSpec((tile, columns), lambda i: (i, 0))
    expert_new = kernel_call(
        functools.partial(adam_body, len(moved)), [sds((owned, width), F32)] * 4, held,
        grid=(owned // tile,),
        in_specs=[rows_of(8)] + [pl.BlockSpec(piece.shape, lambda i: (0, 0)) for piece in moved] + [rows_of(width)] * 3,
        out_specs=[rows_of(width)] * 4,
        cost=QUICK,
    )(*after([plan_col], output), *moved, expert_first[0], expert_second[0], expert_slots[0])
    shared_grad = lines[0].astype(F32)
    for by in range(1, n_z):
        came = after([shift_z(lines[by], n_z - by)], expert_new[0])[0]
        shared_grad = shared_grad + came.astype(F32)
    shared_grad = shared_grad[:own_count]


    def more_grads(number, made):
        parts = returning(range(4), number)
        parts = over_cores(over_links(parts))
        take = functools.partial(take_body, COMES, take_tile)
        part = with_base(take, sds((owned, width), BF16), held, [plan_col, *parts], number)
        grad = made[0] + part.astype(F32)
        return (grad, *adam_update(grad, expert_first[0], expert_second[0], expert_slots[0].astype(F32)))

    shared_grad, *expert_new = after([shared_grad, *expert_new], output)
    expert_new = lax.fori_loop(1, rounds, more_grads, tuple(expert_new))
    shared_new = adam_update(shared_grad, shared_first, shared_second, shared_slots.astype(F32))
    return (
        output[None], grad_tokens[None], shared_grad, *shared_new,
        *(value[None] for value in expert_new),
    )


def solution(mesh):
    sizes = mesh.shape
    chip_experts = (sizes["dp"], sizes["ctx"], sizes["expert"]) == (4, 2, 4)
    return jax.shard_map(
        on_chip_experts if chip_experts else on_device,
        mesh=mesh,
        in_specs=(
            P(("dp", "expert"), "ctx", None),
            P(("dp", "expert"), "ctx", None),
            P(("dp", "expert"), "ctx"),
            P(("dp", "expert"), "ctx", None),
            P(("dp", "expert"), "ctx"),
            P(("dp", "ctx", "expert"), None),
            P(("dp", "ctx", "expert"), None),
            P(("dp", "ctx", "expert"), None),
            P(),
            P("expert", ("dp", "ctx"), None),
            P("expert", ("dp", "ctx"), None),
            P("expert", ("dp", "ctx"), None),
            P("expert", None),
        ),
        out_specs=(
            P(("dp", "expert"), "ctx", None),
            P(("dp", "expert"), "ctx", None),
            P(("dp", "ctx", "expert"), None),
            P(("dp", "ctx", "expert"), None),
            P(("dp", "ctx", "expert"), None),
            P(("dp", "ctx", "expert"), None),
            P("expert", ("dp", "ctx"), None),
            P("expert", ("dp", "ctx"), None),
            P("expert", ("dp", "ctx"), None),
            P("expert", ("dp", "ctx"), None),
        ),
        check_vma=False,
    )
```

```python
import functools
import math

import jax
import jax.numpy as jnp
from jax import lax
from jax.experimental import pallas as pl
from jax.experimental.pallas import tpu as pltpu
from jax.sharding import PartitionSpec as P

HEADS = 8
HEAD_DIM = 64
FF = 2048
EXP_DEV = 4


MASKED_SCORE = -1e30
MOMENT_DECAY = 0.5
LEARN_RATE = 0.05
WEIGHT_DECAY = 0.1
EPSILON = 1e-08
NORM_EPSILON = 1e-06


def layer_norm(values, gain_rows):
    center = values - jnp.mean(values, axis=-1, keepdims=True)
    spread = jnp.mean(center * center, axis=-1, keepdims=True)
    return center * lax.rsqrt(spread + NORM_EPSILON) * gain_rows


def routing(chosen, priority, live_rows, expert_count, capacity):
    tok_count = chosen.shape[0]
    token_ids = jnp.arange(tok_count, dtype=jnp.int32)
    ranking = jnp.argsort(priority * tok_count + token_ids)
    labels = jnp.arange(expert_count, dtype=jnp.int32)
    wanted = jnp.any(chosen[:, :, None] == labels[None, None, :], axis=1) & (
        live_rows[:, None] == 1
    )
    wanted = wanted.astype(jnp.int32)
    ranked = wanted[ranking]
    before = jnp.cumsum(ranked, axis=0) - ranked
    position = jnp.zeros_like(before).at[ranking].set(before)
    slot_taken = jnp.take_along_axis(position, chosen, axis=1)
    kept_pair = (slot_taken < capacity) & (live_rows[:, None] == 1)
    target = jnp.where(kept_pair, chosen * capacity + slot_taken, expert_count * capacity)
    owners = jnp.broadcast_to(token_ids[:, None], chosen.shape)
    source = (
        jnp.zeros((expert_count * capacity,), jnp.int32)
        .at[target.reshape(-1)]
        .set(owners.reshape(-1), mode="drop")
    )
    filled = (
        jnp.zeros((expert_count * capacity,), jnp.int32).at[target.reshape(-1)].set(1, mode="drop")
    )
    slot_index = jnp.where(kept_pair, chosen * capacity + slot_taken, 0)
    return (slot_index, kept_pair.astype(jnp.int32), source, filled)


def head_view(values):
    return values.reshape(values.shape[0], values.shape[1], HEADS, HEAD_DIM)


def score_block(queries, key_rows, keep_mask):
    score = jnp.einsum(
        "iqhe,ikhe->ihqk", queries, head_view(key_rows), preferred_element_type=jnp.float32
    ) * HEAD_DIM ** (-0.5)
    return jnp.where(keep_mask[:, None, None, :] > 0, score, MASKED_SCORE)


def stats_step(running, portion, queries):
    row_max, row_sum = running
    key_rows, keep_mask = portion
    score = score_block(queries, key_rows, keep_mask)
    keep_wide = keep_mask.astype(jnp.float32)[:, None, None, :]
    new_max = jnp.maximum(row_max, jnp.max(score, axis=-1))
    row_sum = row_sum * jnp.exp(row_max - new_max) + jnp.sum(
        jnp.exp(score - new_max[..., None]) * keep_wide, axis=-1
    )
    return (new_max, row_sum)


def value_step(running, portion, queries, log_sum):
    key_rows, value_rows, keep_mask = portion
    score = score_block(queries, key_rows, keep_mask)
    keep_wide = keep_mask.astype(jnp.float32)[:, None, None, :]
    attn_prob = (jnp.exp(score - log_sum[..., None]) * keep_wide).astype(jnp.bfloat16)
    return running + jnp.einsum(
        "ihqk,ikhe->iqhe", attn_prob, head_view(value_rows), preferred_element_type=jnp.float32
    )


def grad_step(grad_query, portion, queries, log_sum, grad_out, row_delta):
    key_rows, value_rows, keep_mask = portion
    score = score_block(queries, key_rows, keep_mask)
    keep_wide = keep_mask.astype(jnp.float32)[:, None, None, :]
    attn_prob = jnp.exp(score - log_sum[..., None]) * keep_wide
    prob_low = attn_prob.astype(jnp.bfloat16)
    grad_value = jnp.einsum(
        "ihqk,iqhe->ikhe", prob_low, grad_out, preferred_element_type=jnp.float32
    )
    grad_prob = jnp.einsum(
        "iqhe,ikhe->ihqk", grad_out, head_view(value_rows), preferred_element_type=jnp.float32
    )
    grad_score = (attn_prob * (grad_prob - row_delta[..., None])).astype(jnp.bfloat16)
    score_scale = HEAD_DIM ** (-0.5)
    grad_query = (
        grad_query
        + jnp.einsum(
            "ihqk,ikhe->iqhe", grad_score, head_view(key_rows), preferred_element_type=jnp.float32
        )
        * score_scale
    )
    grad_key = (
        jnp.einsum("ihqk,iqhe->ikhe", grad_score, queries, preferred_element_type=jnp.float32)
        * score_scale
    )
    return (grad_query, jnp.stack([grad_key, grad_value]))


def each_block(step_fn, running, arrays, block_len):
    total_len = arrays[0].shape[1]
    size_rows = math.gcd(total_len, block_len)

    def one_turn(number, current):
        offset = number * size_rows
        portion = tuple(
            (lax.dynamic_slice_in_dim(member, offset, size_rows, 1) for member in arrays)
        )
        return step_fn(current, portion)

    return lax.fori_loop(0, total_len // size_rows, one_turn, running)


def adam_update(gradient, first_old, second_old, weight):
    first_new = MOMENT_DECAY * first_old + (1.0 - MOMENT_DECAY) * gradient
    second_new = MOMENT_DECAY * second_old + (1.0 - MOMENT_DECAY) * gradient * gradient
    weight_new = weight - LEARN_RATE * (
        first_new / (jnp.sqrt(second_new) + EPSILON) + WEIGHT_DECAY * weight
    )
    return (first_new, second_new, weight_new)


def on_device(
    tokens,
    cotangent,
    pad_mask,
    expert_ids,
    slot_priority,
    shared_slots,
    shared_first,
    shared_second,
    shared_owner,
    expert_slots,
    expert_first,
    expert_second,
    expert_owner,
):
    img_count, part_len, features = tokens.shape
    tok_count = img_count * part_len
    expert_count = EXP_DEV * lax.axis_size("expert")
    capacity = (10 * tok_count + 4 * expert_count - 1) // (4 * expert_count)
    all_shared = lax.all_gather(shared_slots, ("dp", "ctx", "expert"), axis=0, tiled=True)
    all_expert = lax.all_gather(expert_slots, ("dp", "ctx"), axis=1, tiled=True)
    pieces = all_shared[shared_owner]
    w_qkv = pieces[: 3 * features]
    w_attn_out = pieces[3 * features : 4 * features]
    w_router = pieces[4 * features : 4 * features + expert_count]
    gain_one = pieces[4 * features + expert_count].astype(jnp.float32)
    gain_two = pieces[4 * features + expert_count + 1].astype(jnp.float32)
    expert_rows = all_expert[0][expert_owner[0]].reshape(EXP_DEV, 2, FF, features)
    w_in = expert_rows[:, 0]
    w_out = expert_rows[:, 1]
    inputs = tokens.reshape(tok_count, features).astype(jnp.float32)
    keep_mask = pad_mask.astype(jnp.bfloat16)
    keep_rows = pad_mask.reshape(tok_count).astype(jnp.float32)
    normed_one, norm_one_back = jax.vjp(layer_norm, inputs, gain_one)
    normed_low = normed_one.astype(jnp.bfloat16)
    qkv_rows = lax.dot_general(
        normed_low, w_qkv, (((1,), (1,)), ((), ())), preferred_element_type=jnp.float32
    ).astype(jnp.bfloat16)
    query_rows = qkv_rows[:, :features].reshape(img_count, part_len, features)
    key_rows = qkv_rows[:, features : 2 * features].reshape(img_count, part_len, features)
    value_rows = qkv_rows[:, 2 * features :].reshape(img_count, part_len, features)
    queries = head_view(query_rows)
    start_max = jnp.full((img_count, HEADS, part_len), MASKED_SCORE, jnp.float32)
    start_sum = jnp.zeros((img_count, HEADS, part_len), jnp.float32)
    start_out = jnp.zeros((img_count, part_len, HEADS, HEAD_DIM), jnp.float32)
    whole_keys, whole_values, whole_keep = (
        lax.all_gather(key_rows, "ctx", axis=1, tiled=True),
        lax.all_gather(value_rows, "ctx", axis=1, tiled=True),
        lax.all_gather(keep_mask, "ctx", axis=1, tiled=True),
    )
    row_max, row_sum = each_block(
        lambda running, portion: stats_step(running, portion, queries),
        (start_max, start_sum),
        (whole_keys, whole_keep),
        part_len,
    )
    log_sum = row_max + jnp.log(row_sum)
    attended = each_block(
        lambda running, portion: value_step(running, portion, queries, log_sum),
        start_out,
        (whole_keys, whole_values, whole_keep),
        part_len,
    )
    attended_low = attended.reshape(tok_count, features).astype(jnp.bfloat16)
    branch = jnp.dot(attended_low, w_attn_out, preferred_element_type=jnp.float32)
    residual = inputs + branch
    normed_two, norm_two_back = jax.vjp(layer_norm, residual, gain_two)
    mixed_low = normed_two.astype(jnp.bfloat16)
    logits = lax.dot_general(
        mixed_low, w_router, (((1,), (1,)), ((), ())), preferred_element_type=jnp.float32
    )
    router_prob = jax.nn.softmax(logits, axis=-1)
    chosen = expert_ids.reshape(tok_count, 2)
    slot_index, kept_pair, source, filled = routing(
        chosen,
        slot_priority.reshape(tok_count),
        pad_mask.reshape(tok_count),
        expert_count,
        capacity,
    )
    filled_low = filled.astype(jnp.bfloat16)
    dispatched = (mixed_low[source] * filled_low[:, None]).reshape(expert_count, capacity, features)
    received = lax.all_to_all(dispatched, "expert", split_axis=0, concat_axis=1, tiled=True)
    hidden = jnp.einsum("ecd,efd->ecf", received, w_in, preferred_element_type=jnp.float32)
    active, gelu_back = jax.vjp(lambda pre_act: jax.nn.gelu(pre_act, approximate=False), hidden)
    active_low = active.astype(jnp.bfloat16)
    result = jnp.einsum(
        "ecf,efd->ecd", active_low, w_out, preferred_element_type=jnp.float32
    ).astype(jnp.bfloat16)
    returned = lax.all_to_all(result, "expert", split_axis=1, concat_axis=0, tiled=True).reshape(
        expert_count * capacity, features
    )
    kept_float = kept_pair.astype(jnp.float32)
    gate_value = jnp.take_along_axis(router_prob, chosen, axis=1) * kept_float
    picked = returned[slot_index].astype(jnp.float32)
    mixture = jnp.sum(gate_value[:, :, None] * picked, axis=1)
    output = (residual + mixture).astype(jnp.bfloat16).reshape(tokens.shape)
    grad_rows = cotangent.reshape(tok_count, features).astype(jnp.float32) * keep_rows[:, None]
    grad_gate = jnp.sum(grad_rows[:, None, :] * picked, axis=-1) * kept_float
    labels = jnp.arange(expert_count, dtype=jnp.int32)
    grad_prob = jnp.sum(
        (chosen[:, :, None] == labels[None, None, :]).astype(jnp.float32) * grad_gate[:, :, None],
        axis=1,
    )
    grad_logits = router_prob * (
        grad_prob - jnp.sum(grad_prob * router_prob, axis=-1, keepdims=True)
    )
    grad_logits_low = grad_logits.astype(jnp.bfloat16)
    slot_expert = jnp.arange(expert_count * capacity, dtype=jnp.int32) // capacity
    slot_gate = jnp.take_along_axis(router_prob[source], slot_expert[:, None], axis=1)[
        :, 0
    ] * filled.astype(jnp.float32)
    grad_result = (
        (grad_rows[source] * slot_gate[:, None])
        .astype(jnp.bfloat16)
        .reshape(expert_count, capacity, features)
    )
    grad_received = lax.all_to_all(grad_result, "expert", split_axis=0, concat_axis=1, tiled=True)
    grad_active = jnp.einsum(
        "ecd,efd->ecf", grad_received, w_out, preferred_element_type=jnp.float32
    )
    grad_hidden = gelu_back(grad_active)[0].astype(jnp.bfloat16)
    grad_w_out = jnp.einsum(
        "ecf,ecd->efd", active_low, grad_received, preferred_element_type=jnp.float32
    )
    grad_w_in = jnp.einsum(
        "ecf,ecd->efd", grad_hidden, received, preferred_element_type=jnp.float32
    )
    grad_sent = jnp.einsum(
        "ecf,efd->ecd", grad_hidden, w_in, preferred_element_type=jnp.float32
    ).astype(jnp.bfloat16)
    grad_back = lax.all_to_all(
        grad_sent, "expert", split_axis=1, concat_axis=0, tiled=True
    ).reshape(expert_count * capacity, features)
    grad_mixed = jnp.sum(grad_back[slot_index].astype(jnp.float32) * kept_float[:, :, None], axis=1)
    grad_mixed = grad_mixed + jnp.dot(grad_logits_low, w_router, preferred_element_type=jnp.float32)
    grad_router = lax.dot_general(
        grad_logits_low, mixed_low, (((0,), (0,)), ((), ())), preferred_element_type=jnp.float32
    )
    grad_residual_part, grad_gain_two = norm_two_back(grad_mixed)
    grad_residual = grad_rows + grad_residual_part
    grad_branch = grad_residual.astype(jnp.bfloat16)
    grad_w_attn_out = lax.dot_general(
        attended_low, grad_branch, (((0,), (0,)), ((), ())), preferred_element_type=jnp.float32
    )
    grad_attended = lax.dot_general(
        grad_branch, w_attn_out, (((1,), (1,)), ((), ())), preferred_element_type=jnp.float32
    ).astype(jnp.bfloat16)
    grad_out = head_view(grad_attended.reshape(img_count, part_len, features))
    row_delta = jnp.transpose(jnp.sum(grad_out.astype(jnp.float32) * attended, axis=-1), (0, 2, 1))
    start_grad = jnp.zeros((img_count, part_len, HEADS, HEAD_DIM), jnp.float32)
    whole_grads = jnp.zeros((2, img_count, whole_keys.shape[1], HEADS, HEAD_DIM), jnp.float32)

    def grad_turn(number, current):
        grad_query, grads_all = current
        offset = number * part_len
        portion = tuple(
            (
                lax.dynamic_slice_in_dim(member, offset, part_len, 1)
                for member in (whole_keys, whole_values, whole_keep)
            )
        )
        grad_query, grad_block = grad_step(
            grad_query, portion, queries, log_sum, grad_out, row_delta
        )
        grads_all = lax.dynamic_update_slice_in_dim(grads_all, grad_block, offset, 2)
        return (grad_query, grads_all)

    grad_query, whole_grads = lax.fori_loop(
        0, whole_keys.shape[1] // part_len, grad_turn, (start_grad, whole_grads)
    )
    grad_pair = lax.psum_scatter(whole_grads, "ctx", scatter_dimension=2, tiled=True)
    grad_qkv = jnp.concatenate(
        [
            grad_query.reshape(tok_count, features),
            grad_pair[0].reshape(tok_count, features),
            grad_pair[1].reshape(tok_count, features),
        ],
        axis=1,
    ).astype(jnp.bfloat16)
    grad_w_qkv = lax.dot_general(
        grad_qkv, normed_low, (((0,), (0,)), ((), ())), preferred_element_type=jnp.float32
    )
    grad_normed = jnp.dot(grad_qkv, w_qkv, preferred_element_type=jnp.float32)
    grad_input_part, grad_gain_one = norm_one_back(grad_normed)
    grad_tokens = (grad_residual + grad_input_part).reshape(tokens.shape)
    shared_pieces = jnp.concatenate(
        [grad_w_qkv, grad_w_attn_out, grad_router, grad_gain_one[None, :], grad_gain_two[None, :]],
        axis=0,
    )
    shared_layout = jnp.zeros(all_shared.shape, jnp.float32).at[shared_owner].set(shared_pieces)
    shared_grad = lax.psum_scatter(
        shared_layout, ("dp", "ctx", "expert"), scatter_dimension=0, tiled=True
    )
    expert_pieces = jnp.stack([grad_w_in, grad_w_out], axis=1).reshape(EXP_DEV * 2 * FF, features)
    expert_layout = (
        jnp.zeros(all_expert.shape, jnp.float32).at[0, expert_owner[0]].set(expert_pieces)
    )
    expert_grad = lax.psum_scatter(expert_layout, ("dp", "ctx"), scatter_dimension=1, tiled=True)
    shared_first_new, shared_second_new, shared_weight_new = adam_update(
        shared_grad, shared_first, shared_second, shared_slots.astype(jnp.float32)
    )
    expert_first_new, expert_second_new, expert_weight_new = adam_update(
        expert_grad, expert_first, expert_second, expert_slots.astype(jnp.float32)
    )
    return (
        output,
        grad_tokens,
        shared_grad,
        shared_first_new,
        shared_second_new,
        shared_weight_new,
        expert_grad,
        expert_first_new,
        expert_second_new,
        expert_weight_new,
    )


F32 = jnp.float32
BF16 = jnp.bfloat16
I32 = jnp.int32
LANES = 128
MASKED = -1e30
VMEM_LIMIT = 60 * 1024 * 1024
MICRO = 1.15e9
QUICK = (1e6, 1e3)
THEIRS = 2


def dot_nn(left, right):
    return lax.dot_general(left, right, (((1,), (0,)), ((), ())), preferred_element_type=F32)


def dot_nt(left, right):
    return lax.dot_general(left, right, (((1,), (1,)), ((), ())), preferred_element_type=F32)


def dot_tn(left, right):
    return lax.dot_general(left, right, (((0,), (0,)), ((), ())), preferred_element_type=F32)


def iota(shape, dim):
    return lax.broadcasted_iota(I32, shape, dim)


def as_bf16(mask):
    return jnp.where(mask, 1.0, 0.0).astype(BF16)


def kernel_call(
    body, out_shape, scratch=(), grid=None, in_specs=None, out_specs=None, cost=None
):
    given = dict(grid=grid, in_specs=in_specs, out_specs=out_specs)
    extra = {name: value for name, value in given.items() if value is not None}
    flops, moved = cost if cost else (1e8, 1e6)
    name = getattr(body, "func", body).__name__
    return pl.pallas_call(
        body,
        name=name,
        out_shape=out_shape,
        scratch_shapes=list(scratch),
        compiler_params=pltpu.CompilerParams(vmem_limit_bytes=VMEM_LIMIT),
        cost_estimate=pl.CostEstimate(flops=int(flops), bytes_accessed=int(moved), transcendentals=0),
        **extra,
    )


def sds(shape, dtype):
    return jax.ShapeDtypeStruct(shape, dtype)


def route_body(n_exp, capacity, ids_ref, prio_ref, live_ref, cot_ref, row_ref, col_ref, sent_ref):
    toks = ids_ref.shape[1]
    half = capacity // 2
    prio_row = prio_ref[...]
    prio_col = jnp.transpose(jnp.broadcast_to(prio_row, (8, toks)))[:, :1]
    earlier = (prio_col < prio_row) | (
        (prio_col == prio_row) & (iota((toks, toks), 0) < iota((toks, toks), 1))
    )
    live = live_ref[...] > 0.0
    labels = iota((n_exp, toks), 0)
    first, second = ids_ref[0:1, :], ids_ref[1:2, :]
    wanted = ((labels == first) | (labels == second)) & live
    taken = dot_nn(as_bf16(wanted), as_bf16(earlier))
    places = []
    for chosen in (first, second):
        slot = jnp.sum(jnp.where(labels == chosen, taken, 0.0), axis=0, keepdims=True).astype(I32)
        kept = live & (slot < capacity)
        shard = chosen >> 2
        local = chosen & 3
        core = (slot >= half).astype(I32)
        target = ((((local >> 1) * 2 + core) * 2 + (local & 1)) * (n_exp // 4)) + shard
        places.append(jnp.where(kept, target * half + slot - core * half, -1))
    row_id = iota((8, toks), 0)
    rows = jnp.where(row_id == 0, places[0], jnp.where(row_id == 1, places[1], -1))
    row_ref[...] = rows
    col_ref[...] = jnp.transpose(rows.astype(F32)).astype(I32)
    slots = sent_ref.shape[0]
    spots = iota((slots, toks), 0)
    picks = as_bf16((spots == places[0]) | (spots == places[1]))
    sent_ref[...] = dot_nn(picks, cot_ref[...]).astype(BF16)


def unpack_body(spots_at, n_earlier, pos_ref, *refs):
    n_pieces = len(spots_at)
    pieces, rest = refs[:n_pieces], refs[n_pieces:]
    out_ref, held = rest[-2], rest[-1]

    @pl.when(pl.program_id(0) == 0)
    def _():
        gather_pieces(pieces, held)

    wanted = pos_ref[...]
    size = pieces[0].shape[0]
    place = jnp.full(wanted.shape, -1, I32)
    for number, at in enumerate(spots_at):
        inside = (wanted >= at) & (wanted < at + size)
        place = jnp.where(inside, wanted - at + number * size, place)
    picks = as_bf16(place == iota((wanted.shape[0], held.shape[0]), 1))
    value = dot_nn(picks, held[...])
    for earlier in rest[:n_earlier]:
        value = value + earlier[...].astype(F32)
    out_ref[...] = value.astype(BF16)


def gather_pieces(pieces, held):
    at = 0
    for piece in pieces:
        held[at : at + piece.shape[0], :] = piece[...]
        at += piece.shape[0]


def gather_halves(pieces, held):
    size = pieces[0].shape[0] // 2
    for number, piece in enumerate(pieces[:4]):
        held[number * size : (number + 1) * size, :] = piece[:size, :]
    at = 4 * size
    for piece in pieces[4:]:
        held[at : at + piece.shape[0], :] = piece[...]
        at += piece.shape[0]


def normalize(values):
    center = values - jnp.mean(values, axis=-1, keepdims=True)
    spread = jnp.mean(center * center, axis=-1, keepdims=True)
    scale = lax.rsqrt(spread + NORM_EPSILON)
    return center * scale, scale


def head_lanes(head, rows):
    return (iota((rows, LANES), 1) // HEAD_DIM) == head


def of_head(values, head):
    return jnp.where(head_lanes(head, values.shape[0]), values, jnp.zeros_like(values))


def by_head(first, second):
    return jnp.where(head_lanes(0, first.shape[0]), first, second)


def forward_body(
    n_exp, own_ref, other_ref, keep_ref, w_ref, pos_ref,
    qkv_ref, normed_ref, attended_ref, residual_ref, prob_ref, sent_ref, lse_col_ref, lse_row_ref,
    mixed_ref,
):
    toks, width = own_ref.shape
    router = 4 * width
    gain_one = w_ref[router + n_exp : router + n_exp + 16, :].astype(F32)
    gain_two = gain_one[1:2, :]
    gain_one = gain_one[0:1, :]
    for part, ref in enumerate((own_ref, other_ref)):
        normed = normalize(ref[...].astype(F32))[0] * gain_one
        low = normed.astype(BF16)
        if part == 0:
            normed_ref[...] = low
        rows = pl.ds(part * toks, toks)
        for third in range(3):
            made = dot_nt(low, w_ref[third * width : (third + 1) * width, :]).astype(BF16)
            if third == 0:
                made = made * jnp.asarray(HEAD_DIM ** (-0.5), BF16)
            qkv_ref[rows, third * width : (third + 1) * width] = made
    bias = jnp.where(keep_ref[...] > 0.0, 0.0, MASKED)
    lane = iota((toks, LANES), 1)
    logs = jnp.zeros((toks, LANES), F32)
    for at in range(0, width, LANES):
        queries = qkv_ref[0:toks, at : at + LANES]
        keys = qkv_ref[:, width + at : width + at + LANES]
        values = qkv_ref[:, 2 * width + at : 2 * width + at + LANES]
        made = []
        for head in range(2):
            score = dot_nt(of_head(queries, head), keys) + bias
            top = jnp.max(score, axis=-1, keepdims=True)
            grown = jnp.exp(score - top)
            total = jnp.sum(grown, axis=-1, keepdims=True)
            made.append(dot_nn(grown.astype(BF16), values) * (1.0 / total))
            logs = jnp.where(lane == 2 * (at // LANES) + head, top + jnp.log(total), logs)
        attended_ref[:, at : at + LANES] = by_head(*made)
    lse_col_ref[...] = logs
    lse_row_ref[...] = jnp.transpose(lse_col_ref[...])[:8, :]
    branch = dot_nn(attended_ref[...].astype(BF16), w_ref[3 * width : 4 * width, :])
    residual = own_ref[...].astype(F32) + branch
    residual_ref[...] = residual
    mixed = (normalize(residual)[0] * gain_two).astype(BF16)
    mixed_ref[...] = mixed
    logits = dot_nt(mixed, w_ref[router : router + n_exp, :])
    prob_ref[...] = jax.nn.softmax(logits, axis=-1)
    slots = sent_ref.shape[0]
    spots = iota((slots, toks), 0)
    picks = as_bf16((spots == pos_ref[0:1, :]) | (spots == pos_ref[1:2, :]))
    sent_ref[...] = dot_nn(picks, mixed).astype(BF16)


def gelu_parts(value):
    below = 0.5 + 0.5 * lax.erf(value * 0.7071067811865476)
    return value * below, below + value * jnp.exp(-0.5 * value * value) * 0.3989422804014327


def expert_body(
    n_exp, expert_ref, got_ref, cot_ref, near_ref, far_in_ref, far_out_ref, router_ref,
    active_ref, hidden_ref, scaled_ref, result_ref, back_ref, router_grad_ref,
):
    @pl.when(pl.program_id(0) == 0)
    def _():
        router_grad_ref[...] = jnp.zeros_like(router_grad_ref)

    expert = expert_ref[0]
    got, cot = got_ref[...], cot_ref[...]
    labels = iota((got.shape[0], n_exp), 1)
    share = jax.nn.softmax(dot_nt(got, router_ref[...]), axis=-1)
    gate = jnp.sum(jnp.where(labels == expert, share, 0.0), axis=-1, keepdims=True)
    scaled = (cot.astype(F32) * gate).astype(BF16)
    scaled_ref[...] = scaled
    half = near_ref.shape[0] // 2
    total = total_back = 0.0
    halves = ((near_ref[:half, :], near_ref[half:, :]), (far_in_ref[...], far_out_ref[...]))
    for number, (w_in, w_out) in enumerate(halves):
        at = slice(number * half, (number + 1) * half)
        active, slope = gelu_parts(dot_nt(got, w_in))
        low = active.astype(BF16)
        active_ref[:, at] = low
        grad = (dot_nt(scaled, w_out) * slope).astype(BF16)
        hidden_ref[:, at] = grad
        total = total + dot_nn(low, w_out)
        total_back = total_back + dot_nn(grad, w_in)
    result = total.astype(BF16)
    result_ref[...] = result
    inner = jnp.sum(result.astype(F32) * cot.astype(F32), axis=-1, keepdims=True)
    grad = share * (jnp.where(labels == expert, inner, 0.0) - gate * inner)
    low = grad.astype(BF16)
    back_ref[...] = (total_back + dot_nn(low, router_ref[...])).astype(BF16)
    router_grad_ref[...] += dot_tn(low, got)


def weight_grad_body(hidden_ref, active_ref, got_ref, scaled_ref, *outs):
    size = outs[0].shape[0]
    for number, out in enumerate(outs):
        left, right = ((hidden_ref, got_ref), (active_ref, scaled_ref))[number % 2]
        at = slice((1 - number // 2) * size, (2 - number // 2) * size)
        out[...] = dot_tn(left[:, at], right[...]).astype(out.dtype)


def norm_back(hat, scale, gain, grad):
    inner = grad * gain
    first = jnp.mean(inner, axis=-1, keepdims=True)
    second = jnp.mean(inner * hat, axis=-1, keepdims=True)
    return (inner - first - hat * second) * scale


def middle_body(
    n_exp, back_ref, pos_ref, residual_ref, cot_ref, keep_ref, attended_ref, w_ref,
    grad_ref, out_grad_ref, delta_col_ref, delta_row_ref, gain_ref,
):
    toks, width = residual_ref.shape
    router = 4 * width
    slots = back_ref.shape[0]
    gain_two = w_ref[router + n_exp : router + n_exp + 16, :].astype(F32)[1:2, :]
    spots = iota((toks, slots), 1)
    picks = as_bf16((spots == pos_ref[:, 0:1]) | (spots == pos_ref[:, 1:2]))
    grad_mixed = dot_nn(picks, back_ref[...])
    hat, scale = normalize(residual_ref[...])
    gain_ref[...] = jnp.broadcast_to(
        jnp.sum(grad_mixed * hat, axis=0, keepdims=True), gain_ref.shape
    )
    grad_rows = cot_ref[...].astype(F32) * keep_ref[...]
    grad = grad_rows + norm_back(hat, scale, gain_two, grad_mixed)
    grad_ref[...] = grad
    low = grad.astype(BF16)
    out_grad = dot_nt(low, w_ref[3 * width : 4 * width, :]).astype(BF16)
    out_grad_ref[...] = out_grad
    product = out_grad.astype(F32) * attended_ref[...]
    delta = jnp.zeros((toks, LANES), F32)
    lane = iota((toks, LANES), 1)
    for head in range(HEADS):
        at = (head // 2) * LANES
        part = jnp.where(head_lanes(head % 2, toks), product[:, at : at + LANES], 0.0)
        delta = jnp.where(lane == head, jnp.sum(part, axis=-1, keepdims=True), delta)
    delta_col_ref[...] = delta
    delta_row_ref[...] = jnp.transpose(delta)[:8, :]


def inner_body(
    n_exp, qkv_ref, out_grad_ref, lse_ref, delta_ref, keep_ref, attended_ref, grad_ref, router_grad_ref, gain_ref,
    query_ref, kv_ref, early_ref,
):
    toks, width = out_grad_ref.shape
    bias = jnp.where(keep_ref[...] > 0.0, 0.0, MASKED)
    for at in range(0, width, LANES):
        queries = qkv_ref[0:toks, at : at + LANES]
        keys = qkv_ref[:, width + at : width + at + LANES]
        values = qkv_ref[:, 2 * width + at : 2 * width + at + LANES]
        out_grad = out_grad_ref[:, at : at + LANES]
        made = []
        for head in range(2):
            line = 2 * (at // LANES) + head
            score = dot_nt(of_head(queries, head), keys) + bias
            prob = jnp.exp(score - lse_ref[:, line : line + 1])
            slope = dot_nt(of_head(out_grad, head), values)
            grad = (prob * (slope - delta_ref[:, line : line + 1])).astype(BF16)
            made.append(
                (dot_nn(grad, keys), dot_tn(grad[:, :toks], queries), dot_tn(prob[:, :toks].astype(BF16), out_grad))
            )
        query_ref[:, at : at + LANES] = (by_head(made[0][0], made[1][0]) * HEAD_DIM ** (-0.5)).astype(BF16)
        kv_ref[0, :, at : at + LANES] = by_head(made[0][1], made[1][1])
        kv_ref[1, :, at : at + LANES] = by_head(made[0][2], made[1][2])
    early_ref[0:width, :] = dot_tn(attended_ref[...].astype(BF16), grad_ref[...].astype(BF16)).astype(BF16)
    early_ref[width : width + n_exp, :] = router_grad_ref[...].astype(BF16)
    row_id = iota((16, width), 0)
    early_ref[width + n_exp : width + n_exp + 16, :] = jnp.where(
        row_id == 0, gain_ref[0:1, :], 0.0
    ).astype(BF16)


def outer_body(
    n_exp, qkv_ref, out_grad_ref, sums_ref, keep_ref, query_ref, kv_ref, normed_ref, own_ref, w_ref, early_ref,
    query_rows_ref, key_rows_ref, value_rows_ref, rest_ref, grad_normed_ref, held,
):
    toks, width = query_ref.shape
    held[:, 0:width] = query_ref[...]
    bias = jnp.where(keep_ref[...] > 0.0, 0.0, MASKED)
    for at in range(0, width, LANES):
        queries = qkv_ref[toks : 2 * toks, at : at + LANES]
        out_grad = out_grad_ref[:, at : at + LANES]
        keys = qkv_ref[0:toks, width + at : width + at + LANES]
        values = qkv_ref[0:toks, 2 * width + at : 2 * width + at + LANES]
        made = []
        for head in range(2):
            line = 2 * (at // LANES) + head
            score = dot_nt(of_head(keys, head), queries) + bias
            prob = jnp.exp(score - sums_ref[line : line + 1, :])
            slope = dot_nt(of_head(values, head), out_grad)
            grad = (prob * (slope - sums_ref[HEADS + line : HEADS + line + 1, :])).astype(BF16)
            made.append((dot_nn(grad, queries), dot_nn(prob.astype(BF16), out_grad)))
        for number in range(2):
            total = kv_ref[number, :, at : at + LANES] + by_head(made[0][number], made[1][number])
            held[:, (number + 1) * width + at : (number + 1) * width + at + LANES] = total.astype(BF16)
    for third, ref in enumerate((query_rows_ref, key_rows_ref, value_rows_ref)):
        ref[...] = dot_tn(held[:, third * width : (third + 1) * width], normed_ref[...]).astype(BF16)
    grad_normed = dot_nn(held[...], w_ref[0 : 3 * width, :])
    grad_normed_ref[...] = grad_normed
    gain_grad = jnp.sum(grad_normed * normalize(own_ref[...].astype(F32))[0], axis=0, keepdims=True)
    rest_ref[0:16, :] = jnp.where(
        iota((16, width), 0) == 0, gain_grad, 0.0
    ).astype(BF16)
    rest_ref[16:, :] = early_ref[...]


def step_body(keep_a, got_a, keep_b, got_b, go_a, go_b, stay_a, stay_b):
    half = go_a.shape[0]
    for keep, got, go, stay in ((keep_a, got_a, go_a, stay_a), (keep_b, got_b, go_b, stay_b)):
        go[...] = total_f32(keep[half:, :], got[half:, :]).astype(BF16)
        stay[...] = total_f32(keep[:half, :], got[:half, :]).astype(BF16)


def tokens_body(n_exp, grad_normed_ref, own_ref, w_ref, grad_ref, out_ref):
    at = 4 * own_ref.shape[1] + n_exp
    gain_one = w_ref[at : at + 16, :].astype(F32)[0:1, :]
    hat, scale = normalize(own_ref[...].astype(F32))
    out_ref[...] = grad_ref[...] + norm_back(hat, scale, gain_one, grad_normed_ref[...])


def spread_body(starts, n_in, pos_ref, *refs):
    mine, far, outs, held = refs[:n_in], refs[n_in : 2 * n_in], refs[2 * n_in : -1], refs[-1]
    at = 0
    for one, two in zip(mine, far):
        held[at : at + one.shape[0], :] = total_f32(one[...], two[...]).astype(BF16)
        at += one.shape[0]
    size = outs[0].shape[0]
    for number, start in enumerate(starts):
        picks = as_bf16(iota((size, held.shape[0]), 0) + start == pos_ref[...])
        outs[number][...] = dot_nn(picks, held[...]).astype(BF16)


def room_of(owned, n_dev):
    return min(owned, -(-(owned // n_dev * 5 // 4) // 16) * 16)


def sent_at(partner):
    return ((partner >> 2) & 1) * 4 + (partner & 1) * 2 + ((partner >> 1) & 1)


def got_at(partner):
    return ((partner >> 1) & 1) * 4 + ((partner >> 2) & 1) * 2 + (partner & 1)


def sent_cell(cell):
    return (cell >> 2) * 4 + (cell & 1) * 2 + ((cell >> 1) & 1)


def plan_body(n_dev, room, me_ref, owner_ref, row_ref, col_ref, most_ref):
    me = me_ref[0]
    owned = owner_ref.shape[1]
    source = owner_ref[...] >> (owned.bit_length() - 1)
    spot = owner_ref[...] & (owned - 1)
    total = n_dev * n_dev
    classes = iota((n_dev, owned), 0)
    member = jnp.concatenate([classes == source[t : t + 1, :] for t in range(n_dev)], axis=0)
    ones = as_bf16(member)
    step = 256
    before = as_bf16(iota((step, step), 0) < iota((step, step), 1))
    count = jnp.zeros((total, 1), F32)
    ranks = []
    for at in range(0, owned, step):
        part = ones[:, at : at + step]
        ranks.append(dot_nn(part, before) + count)
        count = count + jnp.sum(part.astype(F32), axis=1, keepdims=True)
    most_ref[...] = jnp.broadcast_to(jnp.max(count, axis=0, keepdims=True).astype(I32), most_ref.shape)
    line = iota((total, 1), 0)
    to, of = line // n_dev, line % n_dev
    rank = jnp.concatenate(ranks, axis=1)
    turn = ((rank + 0.5) * (1.0 / room)).astype(I32)
    inside = rank.astype(I32) + turn * ((n_dev - 1) * room)
    wanted = member & (to == me)
    arrives = jnp.sum(jnp.where(wanted, inside + got_at(of ^ to) * room, 0), axis=0, keepdims=True)
    returns = jnp.sum(jnp.where(wanted, inside + sent_at(of ^ to) * room, 0), axis=0, keepdims=True)
    leaves = inside + sent_at(of ^ to) * room
    half = owned // LANES
    found = jnp.zeros((2 * half, LANES), F32)
    high, lanes = iota((half, owned), 0), iota((LANES, owned), 0)
    for t in range(n_dev):
        mine = slice(t * n_dev, (t + 1) * n_dev)
        chosen = member[mine] & (of[mine] == me)
        place = jnp.sum(jnp.where(chosen, leaves[mine], 0), axis=0, keepdims=True)
        hit = (spot[t : t + 1, :] // LANES == high) & (source[t : t + 1, :] == me)
        left = jnp.concatenate(
            [jnp.where(hit, place // LANES, 0), jnp.where(hit, place % LANES, 0)], axis=0
        ).astype(F32).astype(BF16)
        found = found + dot_nt(left, as_bf16((spot[t : t + 1, :] % LANES) == lanes))
    found = found[:half] * float(LANES) + found[half:]
    leave_row = jnp.concatenate([found[a : a + 1, :] for a in range(half)], axis=1)
    block = ((leave_row + 0.5) * (1.0 / room)).astype(I32)
    round_no, cell = block // n_dev, block % n_dev
    comes = leave_row.astype(I32) + (round_no * n_dev + got_at(sent_cell(cell)) - block) * room
    rows = jnp.concatenate(
        [leave_row, arrives.astype(F32), returns.astype(F32), comes.astype(F32), jnp.zeros((4, owned), F32)], axis=0
    )
    row_ref[...] = rows.astype(I32)
    col_ref[...] = jnp.transpose(rows).astype(I32)


LEAVES, ARRIVES, RETURNS, COMES = range(4)


def put_rows(line, base_ref, pos_ref, held, outs, tile):
    wanted = pos_ref[line : line + 1, :] - base_ref[0]
    base = 0
    for out in outs:
        for at in range(0, out.shape[0], tile):
            picks = as_bf16(iota((tile, held.shape[0]), 0) + (base + at) == wanted)
            out[at : at + tile, :] = dot_nn(picks, held[...]).astype(BF16)
        base += out.shape[0]


def put_body(line, tile, base_ref, pos_ref, rows_ref, *outs):
    put_rows(line, base_ref, pos_ref, rows_ref, outs, tile)


def sum_put_body(line, tile, cells, n_in, base_ref, pos_ref, *refs):
    mine, theirs, outs, held = refs[:n_in], refs[n_in : 2 * n_in], refs[2 * n_in : -1], refs[-1]
    size = mine[0].shape[0]
    for number in range(n_in):
        held[number * size : (number + 1) * size, :] = total_f32(mine[number][...], theirs[number][...]).astype(BF16)
    wanted = pos_ref[line : line + 1, :] - base_ref[0]
    for cell, out in zip(cells, outs):
        for at in range(0, out.shape[0], tile):
            picks = as_bf16(iota((tile, held.shape[0]), 0) + (cell * out.shape[0] + at) == wanted)
            out[at : at + tile, :] = dot_nn(picks, held[...]).astype(BF16)


def take_body(line, tile, base_ref, pos_ref, *refs):
    pieces, out, held = refs[:-2], refs[-2], refs[-1]
    gather_halves(pieces, held)
    for at in range(0, out.shape[0], tile):
        wanted = pos_ref[at : at + tile, line : line + 1] - base_ref[0]
        picks = as_bf16(iota((tile, held.shape[0]), 1) == wanted)
        out[at : at + tile, :] = dot_nn(picks, held[...]).astype(BF16)


def adam_body(n_in, pos_ref, *refs):
    pieces, (first_ref, second_ref, weight_ref) = refs[:n_in], refs[n_in : n_in + 3]
    grad_ref, first_new, second_new, weight_new, held = refs[n_in + 3 :]

    @pl.when(pl.program_id(0) == 0)
    def _():
        gather_halves(pieces, held)

    picks = as_bf16(iota((grad_ref.shape[0], held.shape[0]), 1) == pos_ref[:, COMES : COMES + 1])
    grad = dot_nn(picks, held[...])
    grad_ref[...] = grad
    made = adam_update(grad, first_ref[...], second_ref[...], weight_ref[...].astype(F32))
    first_new[...], second_new[...], weight_new[...] = made


def mixture_body(result_ref, pos_ref, ids_ref, prob_ref, residual_ref, out_ref):
    toks = residual_ref.shape[0]
    slots = result_ref.shape[0]
    share = prob_ref[...]
    total = residual_ref[...]
    for number in range(2):
        picks = as_bf16(iota((toks, slots), 1) == pos_ref[:, number : number + 1])
        mine = iota(share.shape, 1) == ids_ref[:, number : number + 1]
        gate = jnp.sum(jnp.where(mine, share, 0.0), axis=-1, keepdims=True)
        total = total + gate * dot_nn(picks, result_ref[...])
    out_ref[...] = total.astype(BF16)


SWAP = [(0, 1), (1, 0)]
SWAP_CORE = [(0, 1), (1, 0), (2, 3), (3, 2)]
SWAP_Y = [(0, 2), (2, 0), (1, 3), (3, 1)]


def swap_x(value):
    return lax.ppermute(value, "ctx", SWAP)


def swap_y(value):
    return lax.ppermute(value, "dp", SWAP_Y)


def swap_x_y(value):
    return lax.ppermute(value, ("dp", "ctx"), [(i, i ^ 5) for i in range(8)])


def swap_core(value):
    return lax.ppermute(value, "dp", SWAP_CORE)


def shift_z(value, by):
    count = lax.axis_size("expert")
    return lax.ppermute(value, "expert", [(i, (i + by) % count) for i in range(count)])


def after(values, *others):
    values = list(values)
    return lax.optimization_barrier((*values, *others))[: len(values)]


def total_f32(first, second):
    return first.astype(F32) + second.astype(F32)


def on_chip_experts(
    tokens, cotangent, pad_mask, expert_ids, slot_priority, shared_slots, shared_first, shared_second,
    shared_owner, expert_slots, expert_first, expert_second, expert_owner,
):
    toks, width = tokens.shape[1], tokens.shape[2]
    n_z = lax.axis_size("expert")
    n_exp = EXP_DEV * n_z
    capacity = (10 * toks + 4 * n_exp - 1) // (4 * n_exp)
    slots = n_exp * capacity
    everyone = ("dp", "ctx", "expert")
    dp, mx, mz = lax.axis_index("dp"), lax.axis_index("ctx"), lax.axis_index("expert")
    my, mc = dp // 2, dp % 2

    own_count = shared_slots.shape[0]
    stride = -(-own_count // 8) * 8
    padded = jnp.pad(shared_slots, ((0, stride - own_count), (0, 0)))
    line = [padded] + [shift_z(padded, by) for by in range(1, n_z)]
    part_a = jnp.concatenate(line[: n_z // 2], axis=0)
    part_b = jnp.concatenate(line[n_z // 2 :], axis=0)
    a_y, b_x = swap_y(part_a), swap_x(part_b)
    pair_a, pair_b = jnp.concatenate([part_a, a_y], axis=0), jnp.concatenate([part_b, b_x], axis=0)
    first_near, last_near = [pair_a, pair_b], [swap_x(pair_a), swap_y(pair_b)]
    first_far = [swap_core(piece) for piece in first_near]

    owner_dev, owner_row = shared_owner // own_count, shared_owner % own_count
    o_z, o_x, o_dp = owner_dev % n_z, owner_dev // n_z % 2, owner_dev // (n_z * 2)
    in_c, in_y, in_x = (o_dp % 2) ^ mc, (o_dp // 2) ^ my, o_x ^ mx
    in_z = (mz - o_z + n_z) % n_z
    late = in_z // (n_z // 2)
    cross = jnp.where(late == 0, in_y + 2 * in_x, in_x + 2 * in_y)
    place = (((in_c * 2 + late) * 4 + cross) * (n_z // 2) + in_z % (n_z // 2)) * stride + owner_row
    total_slots = 8 * n_z * stride
    row_count = -(-shared_owner.shape[0] // 16) * 16
    place_col = jnp.pad(place, (0, row_count - place.shape[0]), constant_values=-1)[:, None]
    gain_at = 4 * width + n_exp
    none = jnp.full((15,), -1, I32)
    place_row = jnp.concatenate(
        [place[: 3 * width], place[gain_at : gain_at + 1], none, place[3 * width : gain_at], place[gain_at + 1 :], none]
    )[None, :]

    half_slots = total_slots // 2
    piece = half_slots // 4
    row_tile = row_count // 2 if row_count % 32 == 0 else row_count

    def unpack(spots, pieces, earlier):
        rows_of = lambda columns: pl.BlockSpec((row_tile, columns), lambda i: (i, 0))
        return kernel_call(
            functools.partial(unpack_body, spots, len(earlier)), sds((row_count, width), BF16),
            [pltpu.VMEM((len(pieces) * piece, width), BF16)],
            grid=(row_count // row_tile,),
            in_specs=[rows_of(1)] + [pl.BlockSpec((piece, width), lambda i: (0, 0))] * len(pieces)
            + [rows_of(width)] * len(earlier),
            out_specs=rows_of(width),
            cost=(7 * MICRO, 1e6),
        )(place_col, *pieces, *earlier)

    first_rows = unpack(
        [0, 2 * piece, half_slots, half_slots + 2 * piece], [*first_near, *first_far], []
    )
    last_near = after(last_near, first_rows)
    last_far = [swap_core(piece) for piece in last_near]

    own, other = tokens[0], swap_x(tokens[0])
    ids = expert_ids[0]
    live = pad_mask.astype(F32)
    live_other = swap_x(pad_mask).astype(F32)
    keep_row = jnp.concatenate([live, live_other], axis=1)
    keep_col = live.reshape(toks, 1)
    pos_row, pos_col, cot_sent = kernel_call(
        functools.partial(route_body, n_exp, capacity),
        (sds((8, toks), I32), sds((toks, 8), I32), sds((slots, width), BF16)),
        cost=(4 * MICRO, 1e6),
    )(*after([ids.T], other), slot_priority.astype(F32), live, cotangent[0])

    def exchange(rows):
        return lax.all_to_all(rows, everyone, split_axis=0, concat_axis=0, tiled=True)

    cot_got = exchange(after([cot_sent], a_y, b_x)[0])

    local = my * 2 + mx
    group, n_dev = dp * 2 + mx, 8
    owned = expert_slots.shape[1]
    room = room_of(owned, n_dev)
    owner = jnp.transpose(
        expert_owner[0].reshape(2, 2, 2, 2, FF // 2), (0, 3, 1, 2, 4)
    ).reshape(n_dev, owned)
    held = [pltpu.VMEM((n_dev * room, width), BF16)]
    sent_shapes = [sds((2 * room, width), BF16)] * 4
    smem, vmem = pl.BlockSpec(memory_space=pltpu.SMEM), pl.BlockSpec(memory_space=pltpu.VMEM)
    plan_row, plan_col, most = kernel_call(
        functools.partial(plan_body, n_dev, room),
        (sds((8, owned), I32), sds((owned, 8), I32), sds((8, LANES), I32)), cost=(5 * MICRO, 1e6),
        in_specs=[smem, vmem],
    )(group.astype(I32).reshape(1), *after([owner], part_a, part_b, pos_row, other))
    rounds = (most[0, 0] + room - 1) // room
    def with_base(body, out_shape, scratch, arrays, number=0, cost=QUICK):
        base = jnp.full((1,), number * n_dev * room, I32)
        return kernel_call(
            body, out_shape, scratch, in_specs=[smem] + [vmem] * len(arrays), cost=cost
        )(base, *arrays)

    def over_links(pieces, *others):
        last = after(pieces[3:], *others)[0] if others else pieces[3]
        return [pieces[0], swap_x(pieces[1]), swap_y(pieces[2]), swap_x_y(last)]

    def over_cores(got):
        far = [jnp.concatenate([got[at][room:], got[at + 1][room:]], axis=0) for at in (0, 2)]
        return [*got, swap_core(far[0]), swap_core(far[1])]

    put_leaving = functools.partial(put_body, LEAVES, room)
    take_tile = 256 if owned % 256 == 0 else owned
    take_arrived = functools.partial(take_body, ARRIVES, take_tile)
    leaving = with_base(
        put_leaving, sent_shapes, (), [*after([plan_row], a_y, b_x), expert_slots[0]], 0, (8 * MICRO, 1e6)
    )
    moved = over_links(after(leaving, *last_near))

    weights = unpack(
        [piece, 3 * piece, half_slots + piece, half_slots + 3 * piece], [*last_near, *last_far], [first_rows]
    )

    (qkv, normed, attended, residual, prob, sent, lse_col, lse_row) = kernel_call(
        functools.partial(forward_body, n_exp),
        (
            sds((2 * toks, 3 * width), BF16), sds((toks, width), BF16), sds((toks, width), F32),
            sds((toks, width), F32), sds((toks, n_exp), F32), sds((slots, width), BF16),
            sds((toks, LANES), F32), sds((8, toks), F32),
        ),
        [pltpu.VMEM((toks, width), BF16)],
        cost=(13 * MICRO, 1e6),
    )(*after([own], cot_got), other, keep_row, weights, pos_row)
    got = exchange(sent)
    moved = over_cores(after(moved, sent))
    near_weights = with_base(take_arrived, sds((owned, width), BF16), held, [plan_col, *moved])
    far_weights = [swap_core(near_weights[: FF // 2]), swap_core(near_weights[FF // 2 :])]

    def more_weights(number, totals):
        leaving = with_base(put_leaving, sent_shapes, (), [plan_row, expert_slots[0]], number)
        moved = over_cores(over_links(leaving))
        part = with_base(take_arrived, sds((owned, width), BF16), held, [plan_col, *moved], number)
        there = swap_core(part)
        return totals[0] + part, totals[1] + there[: FF // 2], totals[2] + there[FF // 2 :]

    got, *expert_weights = after([got, near_weights, *far_weights])
    near_weights, *far_weights = lax.fori_loop(1, rounds, more_weights, tuple(expert_weights))

    expert_id = (mz * EXP_DEV + local).astype(I32).reshape(1)
    tile = 256 if slots % 256 == 0 else slots
    router_rows = weights[4 * width : 4 * width + n_exp]
    whole = lambda shape: pl.BlockSpec(shape, lambda i: (0, 0))
    rows_of = lambda columns: pl.BlockSpec((tile, columns), lambda i: (i, 0))
    active, hidden, scaled, result, back, router_grad = kernel_call(
        functools.partial(expert_body, n_exp),
        (
            sds((slots, FF), BF16), sds((slots, FF), BF16), sds((slots, width), BF16),
            sds((slots, width), BF16), sds((slots, width), BF16), sds((n_exp, width), F32),
        ),
        grid=(slots // tile,),
        in_specs=[
            pl.BlockSpec(memory_space=pltpu.SMEM), rows_of(width), rows_of(width),
            whole((FF, width)), whole((FF // 2, width)), whole((FF // 2, width)), whole((n_exp, width)),
        ],
        out_specs=(
            rows_of(FF), rows_of(FF), rows_of(width), rows_of(width), rows_of(width), whole((n_exp, width)),
        ),
        cost=(19 * MICRO, 1e6),
    )(expert_id, got, cot_got, near_weights, *far_weights, router_rows)
    back_got = exchange(back)

    halves = [sds((FF // 2, width), BF16)] * 2 + [sds((FF // 2, width), F32)] * 2
    *theirs, mine_in, mine_out = kernel_call(weight_grad_body, halves, cost=(10 * MICRO, 1e6))(
        hidden, active, got, scaled
    )
    theirs_got, mine = [swap_core(part) for part in theirs], (mine_in, mine_out)
    held_owned = [pltpu.VMEM((owned, width), BF16)]

    def returning(cells, number=0):
        body = functools.partial(sum_put_body, RETURNS, room, cells, 2)
        return with_base(body, [sent_shapes[0]] * len(cells), held_owned, [plan_row, *mine, *theirs_got], number, (4 * MICRO, 1e6))

    moved_x, moved_xy = returning((1, 3))
    moved_0, moved_y = returning((0, 2))
    moved = [moved_0, moved_x, moved_y, moved_xy]
    back_got = after([back_got], *moved)[0]

    grad_residual, out_grad, delta_col, delta_row, gain_two = kernel_call(
        functools.partial(middle_body, n_exp),
        (
            sds((toks, width), F32), sds((toks, width), BF16), sds((toks, LANES), F32),
            sds((8, toks), F32), sds((8, width), F32),
        ),
        cost=(6 * MICRO, 1e6),
    )(back_got, pos_col, residual, cotangent[0], keep_col, attended, weights)
    out_grad_other = swap_x(out_grad)
    sums_other = swap_x(jnp.concatenate([lse_row, delta_row], axis=0))
    query_grad, kv_grad, early = kernel_call(
        functools.partial(inner_body, n_exp),
        (sds((toks, width), BF16), sds((2, toks, width), F32), sds((width + n_exp + 16, width), BF16)),
        cost=(15 * MICRO, 1e6),
    )(qkv, out_grad, lse_col, delta_col, keep_row, attended, grad_residual, router_grad, gain_two)
    moved = over_links(moved, out_grad_other, query_grad, sums_other)
    result_got = exchange(after([result], query_grad)[0])
    *late, grad_normed = kernel_call(
        functools.partial(outer_body, n_exp),
        [sds((rows, width), BF16) for rows in (width, width, width, place_row.shape[1] - 3 * width)]
        + [sds((toks, width), F32)],
        [pltpu.VMEM((toks, 3 * width), BF16)],
        cost=QUICK,
    )(
        qkv, *after([out_grad_other], *moved[1:3]), sums_other, keep_col, query_grad, kv_grad, normed, own, weights, early,
    )
    late_far = [swap_core(part) for part in late]
    quarter = half_slots // 2
    eighth, sixteenth = quarter // 2, quarter // 4
    count = place_row.shape[1]

    def spread(starts, *others):
        return kernel_call(
            functools.partial(spread_body, starts, len(late)), [sds((eighth, width), BF16)] * 2,
            [pltpu.VMEM((count, width), BF16)], cost=QUICK,
        )(*after([place_row], *others), *late, *late_far)

    sends = spread((eighth, quarter + eighth), moved[3])
    got_a, got_b = swap_x(sends[0]), swap_y(sends[1])
    keeps = spread((0, quarter), *sends)
    grad_tokens = kernel_call(
        functools.partial(tokens_body, n_exp), sds((toks, width), F32), cost=QUICK
    )(*after([grad_normed], *sends), own, weights, grad_residual)

    got_a, got_b = after([got_a, got_b], grad_tokens)
    go_a, go_b, sum_a, sum_b = kernel_call(
        step_body, [sds((sixteenth, width), BF16)] * 4, cost=QUICK
    )(keeps[0], got_a, keeps[1], got_b)
    got_a, got_b = swap_y(go_a), swap_x(go_b)
    moved = over_cores(after(moved, go_a))
    sum_a = total_f32(sum_a, got_a).astype(BF16)
    sum_b = total_f32(sum_b, got_b).astype(BF16)
    lines = [sum_a[i * stride : (i + 1) * stride] for i in range(n_z // 2)]
    lines += [sum_b[i * stride : (i + 1) * stride] for i in range(n_z // 2)]
    output = kernel_call(
        mixture_body, sds((toks, width), BF16), cost=QUICK
    )(*after([result_got], *lines), pos_col, ids, prob, residual)
    tile = 512 if owned % 512 == 0 else owned
    rows_of = lambda columns: pl.BlockSpec((tile, columns), lambda i: (i, 0))
    expert_new = kernel_call(
        functools.partial(adam_body, len(moved)), [sds((owned, width), F32)] * 4, held,
        grid=(owned // tile,),
        in_specs=[rows_of(8)] + [pl.BlockSpec(piece.shape, lambda i: (0, 0)) for piece in moved] + [rows_of(width)] * 3,
        out_specs=[rows_of(width)] * 4,
        cost=QUICK,
    )(*after([plan_col], output), *moved, expert_first[0], expert_second[0], expert_slots[0])
    shared_grad = lines[0].astype(F32)
    for by in range(1, n_z):
        came = after([shift_z(lines[by], n_z - by)], expert_new[0])[0]
        shared_grad = shared_grad + came.astype(F32)
    shared_grad = shared_grad[:own_count]


    def more_grads(number, made):
        parts = returning(range(4), number)
        parts = over_cores(over_links(parts))
        take = functools.partial(take_body, COMES, take_tile)
        part = with_base(take, sds((owned, width), BF16), held, [plan_col, *parts], number)
        grad = made[0] + part.astype(F32)
        return (grad, *adam_update(grad, expert_first[0], expert_second[0], expert_slots[0].astype(F32)))

    shared_grad, *expert_new = after([shared_grad, *expert_new], output)
    expert_new = lax.fori_loop(1, rounds, more_grads, tuple(expert_new))
    shared_new = adam_update(shared_grad, shared_first, shared_second, shared_slots.astype(F32))
    return (
        output[None], grad_tokens[None], shared_grad, *shared_new,
        *(value[None] for value in expert_new),
    )


def solution(mesh):
    sizes = mesh.shape
    chip_experts = (sizes["dp"], sizes["ctx"], sizes["expert"]) == (4, 2, 4)
    return jax.shard_map(
        on_chip_experts if chip_experts else on_device,
        mesh=mesh,
        in_specs=(
            P(("dp", "expert"), "ctx", None),
            P(("dp", "expert"), "ctx", None),
            P(("dp", "expert"), "ctx"),
            P(("dp", "expert"), "ctx", None),
            P(("dp", "expert"), "ctx"),
            P(("dp", "ctx", "expert"), None),
            P(("dp", "ctx", "expert"), None),
            P(("dp", "ctx", "expert"), None),
            P(),
            P("expert", ("dp", "ctx"), None),
            P("expert", ("dp", "ctx"), None),
            P("expert", ("dp", "ctx"), None),
            P("expert", None),
        ),
        out_specs=(
            P(("dp", "expert"), "ctx", None),
            P(("dp", "expert"), "ctx", None),
            P(("dp", "ctx", "expert"), None),
            P(("dp", "ctx", "expert"), None),
            P(("dp", "ctx", "expert"), None),
            P(("dp", "ctx", "expert"), None),
            P("expert", ("dp", "ctx"), None),
            P("expert", ("dp", "ctx"), None),
            P("expert", ("dp", "ctx"), None),
            P("expert", ("dp", "ctx"), None),
        ),
        check_vma=False,
    )
```

```python
import functools
import math

import jax
import jax.numpy as jnp
from jax import lax
from jax.experimental import pallas as pl
from jax.experimental.pallas import tpu as pltpu
from jax.sharding import PartitionSpec as P

HEADS = 8
HEAD_DIM = 64
FF = 2048
EXP_DEV = 4


MASKED_SCORE = -1e30
MOMENT_DECAY = 0.5
LEARN_RATE = 0.05
WEIGHT_DECAY = 0.1
EPSILON = 1e-08
NORM_EPSILON = 1e-06


def layer_norm(values, gain_rows):
    center = values - jnp.mean(values, axis=-1, keepdims=True)
    spread = jnp.mean(center * center, axis=-1, keepdims=True)
    return center * lax.rsqrt(spread + NORM_EPSILON) * gain_rows


def routing(chosen, priority, live_rows, expert_count, capacity):
    tok_count = chosen.shape[0]
    token_ids = jnp.arange(tok_count, dtype=jnp.int32)
    ranking = jnp.argsort(priority * tok_count + token_ids)
    labels = jnp.arange(expert_count, dtype=jnp.int32)
    wanted = jnp.any(chosen[:, :, None] == labels[None, None, :], axis=1) & (
        live_rows[:, None] == 1
    )
    wanted = wanted.astype(jnp.int32)
    ranked = wanted[ranking]
    before = jnp.cumsum(ranked, axis=0) - ranked
    position = jnp.zeros_like(before).at[ranking].set(before)
    slot_taken = jnp.take_along_axis(position, chosen, axis=1)
    kept_pair = (slot_taken < capacity) & (live_rows[:, None] == 1)
    target = jnp.where(kept_pair, chosen * capacity + slot_taken, expert_count * capacity)
    owners = jnp.broadcast_to(token_ids[:, None], chosen.shape)
    source = (
        jnp.zeros((expert_count * capacity,), jnp.int32)
        .at[target.reshape(-1)]
        .set(owners.reshape(-1), mode="drop")
    )
    filled = (
        jnp.zeros((expert_count * capacity,), jnp.int32).at[target.reshape(-1)].set(1, mode="drop")
    )
    slot_index = jnp.where(kept_pair, chosen * capacity + slot_taken, 0)
    return (slot_index, kept_pair.astype(jnp.int32), source, filled)


def head_view(values):
    return values.reshape(values.shape[0], values.shape[1], HEADS, HEAD_DIM)


def score_block(queries, key_rows, keep_mask):
    score = jnp.einsum(
        "iqhe,ikhe->ihqk", queries, head_view(key_rows), preferred_element_type=jnp.float32
    ) * HEAD_DIM ** (-0.5)
    return jnp.where(keep_mask[:, None, None, :] > 0, score, MASKED_SCORE)


def stats_step(running, portion, queries):
    row_max, row_sum = running
    key_rows, keep_mask = portion
    score = score_block(queries, key_rows, keep_mask)
    keep_wide = keep_mask.astype(jnp.float32)[:, None, None, :]
    new_max = jnp.maximum(row_max, jnp.max(score, axis=-1))
    row_sum = row_sum * jnp.exp(row_max - new_max) + jnp.sum(
        jnp.exp(score - new_max[..., None]) * keep_wide, axis=-1
    )
    return (new_max, row_sum)


def value_step(running, portion, queries, log_sum):
    key_rows, value_rows, keep_mask = portion
    score = score_block(queries, key_rows, keep_mask)
    keep_wide = keep_mask.astype(jnp.float32)[:, None, None, :]
    attn_prob = (jnp.exp(score - log_sum[..., None]) * keep_wide).astype(jnp.bfloat16)
    return running + jnp.einsum(
        "ihqk,ikhe->iqhe", attn_prob, head_view(value_rows), preferred_element_type=jnp.float32
    )


def grad_step(grad_query, portion, queries, log_sum, grad_out, row_delta):
    key_rows, value_rows, keep_mask = portion
    score = score_block(queries, key_rows, keep_mask)
    keep_wide = keep_mask.astype(jnp.float32)[:, None, None, :]
    attn_prob = jnp.exp(score - log_sum[..., None]) * keep_wide
    prob_low = attn_prob.astype(jnp.bfloat16)
    grad_value = jnp.einsum(
        "ihqk,iqhe->ikhe", prob_low, grad_out, preferred_element_type=jnp.float32
    )
    grad_prob = jnp.einsum(
        "iqhe,ikhe->ihqk", grad_out, head_view(value_rows), preferred_element_type=jnp.float32
    )
    grad_score = (attn_prob * (grad_prob - row_delta[..., None])).astype(jnp.bfloat16)
    score_scale = HEAD_DIM ** (-0.5)
    grad_query = (
        grad_query
        + jnp.einsum(
            "ihqk,ikhe->iqhe", grad_score, head_view(key_rows), preferred_element_type=jnp.float32
        )
        * score_scale
    )
    grad_key = (
        jnp.einsum("ihqk,iqhe->ikhe", grad_score, queries, preferred_element_type=jnp.float32)
        * score_scale
    )
    return (grad_query, jnp.stack([grad_key, grad_value]))


def each_block(step_fn, running, arrays, block_len):
    total_len = arrays[0].shape[1]
    size_rows = math.gcd(total_len, block_len)

    def one_turn(number, current):
        offset = number * size_rows
        portion = tuple(
            (lax.dynamic_slice_in_dim(member, offset, size_rows, 1) for member in arrays)
        )
        return step_fn(current, portion)

    return lax.fori_loop(0, total_len // size_rows, one_turn, running)


def adam_update(gradient, first_old, second_old, weight):
    first_new = MOMENT_DECAY * first_old + (1.0 - MOMENT_DECAY) * gradient
    second_new = MOMENT_DECAY * second_old + (1.0 - MOMENT_DECAY) * gradient * gradient
    weight_new = weight - LEARN_RATE * (
        first_new / (jnp.sqrt(second_new) + EPSILON) + WEIGHT_DECAY * weight
    )
    return (first_new, second_new, weight_new)


def on_device(
    tokens,
    cotangent,
    pad_mask,
    expert_ids,
    slot_priority,
    shared_slots,
    shared_first,
    shared_second,
    shared_owner,
    expert_slots,
    expert_first,
    expert_second,
    expert_owner,
):
    img_count, part_len, features = tokens.shape
    tok_count = img_count * part_len
    expert_count = EXP_DEV * lax.axis_size("expert")
    capacity = (10 * tok_count + 4 * expert_count - 1) // (4 * expert_count)
    all_shared = lax.all_gather(shared_slots, ("dp", "ctx", "expert"), axis=0, tiled=True)
    all_expert = lax.all_gather(expert_slots, ("dp", "ctx"), axis=1, tiled=True)
    pieces = all_shared[shared_owner]
    w_qkv = pieces[: 3 * features]
    w_attn_out = pieces[3 * features : 4 * features]
    w_router = pieces[4 * features : 4 * features + expert_count]
    gain_one = pieces[4 * features + expert_count].astype(jnp.float32)
    gain_two = pieces[4 * features + expert_count + 1].astype(jnp.float32)
    expert_rows = all_expert[0][expert_owner[0]].reshape(EXP_DEV, 2, FF, features)
    w_in = expert_rows[:, 0]
    w_out = expert_rows[:, 1]
    inputs = tokens.reshape(tok_count, features).astype(jnp.float32)
    keep_mask = pad_mask.astype(jnp.bfloat16)
    keep_rows = pad_mask.reshape(tok_count).astype(jnp.float32)
    normed_one, norm_one_back = jax.vjp(layer_norm, inputs, gain_one)
    normed_low = normed_one.astype(jnp.bfloat16)
    qkv_rows = lax.dot_general(
        normed_low, w_qkv, (((1,), (1,)), ((), ())), preferred_element_type=jnp.float32
    ).astype(jnp.bfloat16)
    query_rows = qkv_rows[:, :features].reshape(img_count, part_len, features)
    key_rows = qkv_rows[:, features : 2 * features].reshape(img_count, part_len, features)
    value_rows = qkv_rows[:, 2 * features :].reshape(img_count, part_len, features)
    queries = head_view(query_rows)
    start_max = jnp.full((img_count, HEADS, part_len), MASKED_SCORE, jnp.float32)
    start_sum = jnp.zeros((img_count, HEADS, part_len), jnp.float32)
    start_out = jnp.zeros((img_count, part_len, HEADS, HEAD_DIM), jnp.float32)
    whole_keys, whole_values, whole_keep = (
        lax.all_gather(key_rows, "ctx", axis=1, tiled=True),
        lax.all_gather(value_rows, "ctx", axis=1, tiled=True),
        lax.all_gather(keep_mask, "ctx", axis=1, tiled=True),
    )
    row_max, row_sum = each_block(
        lambda running, portion: stats_step(running, portion, queries),
        (start_max, start_sum),
        (whole_keys, whole_keep),
        part_len,
    )
    log_sum = row_max + jnp.log(row_sum)
    attended = each_block(
        lambda running, portion: value_step(running, portion, queries, log_sum),
        start_out,
        (whole_keys, whole_values, whole_keep),
        part_len,
    )
    attended_low = attended.reshape(tok_count, features).astype(jnp.bfloat16)
    branch = jnp.dot(attended_low, w_attn_out, preferred_element_type=jnp.float32)
    residual = inputs + branch
    normed_two, norm_two_back = jax.vjp(layer_norm, residual, gain_two)
    mixed_low = normed_two.astype(jnp.bfloat16)
    logits = lax.dot_general(
        mixed_low, w_router, (((1,), (1,)), ((), ())), preferred_element_type=jnp.float32
    )
    router_prob = jax.nn.softmax(logits, axis=-1)
    chosen = expert_ids.reshape(tok_count, 2)
    slot_index, kept_pair, source, filled = routing(
        chosen,
        slot_priority.reshape(tok_count),
        pad_mask.reshape(tok_count),
        expert_count,
        capacity,
    )
    filled_low = filled.astype(jnp.bfloat16)
    dispatched = (mixed_low[source] * filled_low[:, None]).reshape(expert_count, capacity, features)
    received = lax.all_to_all(dispatched, "expert", split_axis=0, concat_axis=1, tiled=True)
    hidden = jnp.einsum("ecd,efd->ecf", received, w_in, preferred_element_type=jnp.float32)
    active, gelu_back = jax.vjp(lambda pre_act: jax.nn.gelu(pre_act, approximate=False), hidden)
    active_low = active.astype(jnp.bfloat16)
    result = jnp.einsum(
        "ecf,efd->ecd", active_low, w_out, preferred_element_type=jnp.float32
    ).astype(jnp.bfloat16)
    returned = lax.all_to_all(result, "expert", split_axis=1, concat_axis=0, tiled=True).reshape(
        expert_count * capacity, features
    )
    kept_float = kept_pair.astype(jnp.float32)
    gate_value = jnp.take_along_axis(router_prob, chosen, axis=1) * kept_float
    picked = returned[slot_index].astype(jnp.float32)
    mixture = jnp.sum(gate_value[:, :, None] * picked, axis=1)
    output = (residual + mixture).astype(jnp.bfloat16).reshape(tokens.shape)
    grad_rows = cotangent.reshape(tok_count, features).astype(jnp.float32) * keep_rows[:, None]
    grad_gate = jnp.sum(grad_rows[:, None, :] * picked, axis=-1) * kept_float
    labels = jnp.arange(expert_count, dtype=jnp.int32)
    grad_prob = jnp.sum(
        (chosen[:, :, None] == labels[None, None, :]).astype(jnp.float32) * grad_gate[:, :, None],
        axis=1,
    )
    grad_logits = router_prob * (
        grad_prob - jnp.sum(grad_prob * router_prob, axis=-1, keepdims=True)
    )
    grad_logits_low = grad_logits.astype(jnp.bfloat16)
    slot_expert = jnp.arange(expert_count * capacity, dtype=jnp.int32) // capacity
    slot_gate = jnp.take_along_axis(router_prob[source], slot_expert[:, None], axis=1)[
        :, 0
    ] * filled.astype(jnp.float32)
    grad_result = (
        (grad_rows[source] * slot_gate[:, None])
        .astype(jnp.bfloat16)
        .reshape(expert_count, capacity, features)
    )
    grad_received = lax.all_to_all(grad_result, "expert", split_axis=0, concat_axis=1, tiled=True)
    grad_active = jnp.einsum(
        "ecd,efd->ecf", grad_received, w_out, preferred_element_type=jnp.float32
    )
    grad_hidden = gelu_back(grad_active)[0].astype(jnp.bfloat16)
    grad_w_out = jnp.einsum(
        "ecf,ecd->efd", active_low, grad_received, preferred_element_type=jnp.float32
    )
    grad_w_in = jnp.einsum(
        "ecf,ecd->efd", grad_hidden, received, preferred_element_type=jnp.float32
    )
    grad_sent = jnp.einsum(
        "ecf,efd->ecd", grad_hidden, w_in, preferred_element_type=jnp.float32
    ).astype(jnp.bfloat16)
    grad_back = lax.all_to_all(
        grad_sent, "expert", split_axis=1, concat_axis=0, tiled=True
    ).reshape(expert_count * capacity, features)
    grad_mixed = jnp.sum(grad_back[slot_index].astype(jnp.float32) * kept_float[:, :, None], axis=1)
    grad_mixed = grad_mixed + jnp.dot(grad_logits_low, w_router, preferred_element_type=jnp.float32)
    grad_router = lax.dot_general(
        grad_logits_low, mixed_low, (((0,), (0,)), ((), ())), preferred_element_type=jnp.float32
    )
    grad_residual_part, grad_gain_two = norm_two_back(grad_mixed)
    grad_residual = grad_rows + grad_residual_part
    grad_branch = grad_residual.astype(jnp.bfloat16)
    grad_w_attn_out = lax.dot_general(
        attended_low, grad_branch, (((0,), (0,)), ((), ())), preferred_element_type=jnp.float32
    )
    grad_attended = lax.dot_general(
        grad_branch, w_attn_out, (((1,), (1,)), ((), ())), preferred_element_type=jnp.float32
    ).astype(jnp.bfloat16)
    grad_out = head_view(grad_attended.reshape(img_count, part_len, features))
    row_delta = jnp.transpose(jnp.sum(grad_out.astype(jnp.float32) * attended, axis=-1), (0, 2, 1))
    start_grad = jnp.zeros((img_count, part_len, HEADS, HEAD_DIM), jnp.float32)
    whole_grads = jnp.zeros((2, img_count, whole_keys.shape[1], HEADS, HEAD_DIM), jnp.float32)

    def grad_turn(number, current):
        grad_query, grads_all = current
        offset = number * part_len
        portion = tuple(
            (
                lax.dynamic_slice_in_dim(member, offset, part_len, 1)
                for member in (whole_keys, whole_values, whole_keep)
            )
        )
        grad_query, grad_block = grad_step(
            grad_query, portion, queries, log_sum, grad_out, row_delta
        )
        grads_all = lax.dynamic_update_slice_in_dim(grads_all, grad_block, offset, 2)
        return (grad_query, grads_all)

    grad_query, whole_grads = lax.fori_loop(
        0, whole_keys.shape[1] // part_len, grad_turn, (start_grad, whole_grads)
    )
    grad_pair = lax.psum_scatter(whole_grads, "ctx", scatter_dimension=2, tiled=True)
    grad_qkv = jnp.concatenate(
        [
            grad_query.reshape(tok_count, features),
            grad_pair[0].reshape(tok_count, features),
            grad_pair[1].reshape(tok_count, features),
        ],
        axis=1,
    ).astype(jnp.bfloat16)
    grad_w_qkv = lax.dot_general(
        grad_qkv, normed_low, (((0,), (0,)), ((), ())), preferred_element_type=jnp.float32
    )
    grad_normed = jnp.dot(grad_qkv, w_qkv, preferred_element_type=jnp.float32)
    grad_input_part, grad_gain_one = norm_one_back(grad_normed)
    grad_tokens = (grad_residual + grad_input_part).reshape(tokens.shape)
    shared_pieces = jnp.concatenate(
        [grad_w_qkv, grad_w_attn_out, grad_router, grad_gain_one[None, :], grad_gain_two[None, :]],
        axis=0,
    )
    shared_layout = jnp.zeros(all_shared.shape, jnp.float32).at[shared_owner].set(shared_pieces)
    shared_grad = lax.psum_scatter(
        shared_layout, ("dp", "ctx", "expert"), scatter_dimension=0, tiled=True
    )
    expert_pieces = jnp.stack([grad_w_in, grad_w_out], axis=1).reshape(EXP_DEV * 2 * FF, features)
    expert_layout = (
        jnp.zeros(all_expert.shape, jnp.float32).at[0, expert_owner[0]].set(expert_pieces)
    )
    expert_grad = lax.psum_scatter(expert_layout, ("dp", "ctx"), scatter_dimension=1, tiled=True)
    shared_first_new, shared_second_new, shared_weight_new = adam_update(
        shared_grad, shared_first, shared_second, shared_slots.astype(jnp.float32)
    )
    expert_first_new, expert_second_new, expert_weight_new = adam_update(
        expert_grad, expert_first, expert_second, expert_slots.astype(jnp.float32)
    )
    return (
        output,
        grad_tokens,
        shared_grad,
        shared_first_new,
        shared_second_new,
        shared_weight_new,
        expert_grad,
        expert_first_new,
        expert_second_new,
        expert_weight_new,
    )


F32 = jnp.float32
BF16 = jnp.bfloat16
I32 = jnp.int32
LANES = 128
MASKED = -1e30
VMEM_LIMIT = 60 * 1024 * 1024
MICRO = 1.15e9
QUICK = (1e6, 1e3)
THEIRS = 2


def dot_nn(left, right):
    return lax.dot_general(left, right, (((1,), (0,)), ((), ())), preferred_element_type=F32)


def dot_nt(left, right):
    return lax.dot_general(left, right, (((1,), (1,)), ((), ())), preferred_element_type=F32)


def dot_tn(left, right):
    return lax.dot_general(left, right, (((0,), (0,)), ((), ())), preferred_element_type=F32)


def iota(shape, dim):
    return lax.broadcasted_iota(I32, shape, dim)


def as_bf16(mask):
    return jnp.where(mask, 1.0, 0.0).astype(BF16)


def kernel_call(
    body, out_shape, scratch=(), grid=None, in_specs=None, out_specs=None, cost=None
):
    given = dict(grid=grid, in_specs=in_specs, out_specs=out_specs)
    extra = {name: value for name, value in given.items() if value is not None}
    flops, moved = cost if cost else (1e8, 1e6)
    name = getattr(body, "func", body).__name__
    return pl.pallas_call(
        body,
        name=name,
        out_shape=out_shape,
        scratch_shapes=list(scratch),
        compiler_params=pltpu.CompilerParams(vmem_limit_bytes=VMEM_LIMIT),
        cost_estimate=pl.CostEstimate(flops=int(flops), bytes_accessed=int(moved), transcendentals=0),
        **extra,
    )


def sds(shape, dtype):
    return jax.ShapeDtypeStruct(shape, dtype)


def route_body(n_exp, capacity, ids_ref, prio_ref, live_ref, cot_ref, row_ref, col_ref, sent_ref):
    toks = ids_ref.shape[1]
    half = capacity // 2
    prio_row = prio_ref[...]
    prio_col = jnp.transpose(jnp.broadcast_to(prio_row, (8, toks)))[:, :1]
    earlier = (prio_col < prio_row) | (
        (prio_col == prio_row) & (iota((toks, toks), 0) < iota((toks, toks), 1))
    )
    live = live_ref[...] > 0.0
    labels = iota((n_exp, toks), 0)
    first, second = ids_ref[0:1, :], ids_ref[1:2, :]
    wanted = ((labels == first) | (labels == second)) & live
    taken = dot_nn(as_bf16(wanted), as_bf16(earlier))
    places = []
    for chosen in (first, second):
        slot = jnp.sum(jnp.where(labels == chosen, taken, 0.0), axis=0, keepdims=True).astype(I32)
        kept = live & (slot < capacity)
        shard = chosen >> 2
        local = chosen & 3
        core = (slot >= half).astype(I32)
        target = ((((local >> 1) * 2 + core) * 2 + (local & 1)) * (n_exp // 4)) + shard
        places.append(jnp.where(kept, target * half + slot - core * half, -1))
    row_id = iota((8, toks), 0)
    rows = jnp.where(row_id == 0, places[0], jnp.where(row_id == 1, places[1], -1))
    row_ref[...] = rows
    col_ref[...] = jnp.transpose(rows.astype(F32)).astype(I32)
    slots = sent_ref.shape[0]
    spots = iota((slots, toks), 0)
    picks = as_bf16((spots == places[0]) | (spots == places[1]))
    sent_ref[...] = dot_nn(picks, cot_ref[...]).astype(BF16)


def unpack_body(spots_at, n_earlier, pos_ref, *refs):
    n_pieces = len(spots_at)
    pieces, rest = refs[:n_pieces], refs[n_pieces:]
    out_ref, held = rest[-2], rest[-1]

    @pl.when(pl.program_id(0) == 0)
    def _():
        gather_pieces(pieces, held)

    wanted = pos_ref[...]
    size = pieces[0].shape[0]
    place = jnp.full(wanted.shape, -1, I32)
    for number, at in enumerate(spots_at):
        inside = (wanted >= at) & (wanted < at + size)
        place = jnp.where(inside, wanted - at + number * size, place)
    picks = as_bf16(place == iota((wanted.shape[0], held.shape[0]), 1))
    value = dot_nn(picks, held[...])
    for earlier in rest[:n_earlier]:
        value = value + earlier[...].astype(F32)
    out_ref[...] = value.astype(BF16)


def gather_pieces(pieces, held):
    at = 0
    for piece in pieces:
        held[at : at + piece.shape[0], :] = piece[...]
        at += piece.shape[0]


def gather_halves(pieces, held):
    size = pieces[0].shape[0] // 2
    for number, piece in enumerate(pieces[:4]):
        held[number * size : (number + 1) * size, :] = piece[:size, :]
    at = 4 * size
    for piece in pieces[4:]:
        held[at : at + piece.shape[0], :] = piece[...]
        at += piece.shape[0]


def normalize(values):
    center = values - jnp.mean(values, axis=-1, keepdims=True)
    spread = jnp.mean(center * center, axis=-1, keepdims=True)
    scale = lax.rsqrt(spread + NORM_EPSILON)
    return center * scale, scale


def head_lanes(head, rows):
    return (iota((rows, LANES), 1) // HEAD_DIM) == head


def of_head(values, head):
    return jnp.where(head_lanes(head, values.shape[0]), values, jnp.zeros_like(values))


def by_head(first, second):
    return jnp.where(head_lanes(0, first.shape[0]), first, second)


def forward_body(
    n_exp, own_ref, other_ref, keep_ref, w_ref, pos_ref,
    qkv_ref, normed_ref, attended_ref, residual_ref, prob_ref, sent_ref, lse_col_ref, lse_row_ref,
    mixed_ref,
):
    toks, width = own_ref.shape
    router = 4 * width
    gain_one = w_ref[router + n_exp : router + n_exp + 16, :].astype(F32)
    gain_two = gain_one[1:2, :]
    gain_one = gain_one[0:1, :]
    for part, ref in enumerate((own_ref, other_ref)):
        normed = normalize(ref[...].astype(F32))[0] * gain_one
        low = normed.astype(BF16)
        if part == 0:
            normed_ref[...] = low
        rows = pl.ds(part * toks, toks)
        for third in range(3):
            made = dot_nt(low, w_ref[third * width : (third + 1) * width, :]).astype(BF16)
            if third == 0:
                made = made * jnp.asarray(HEAD_DIM ** (-0.5), BF16)
            qkv_ref[rows, third * width : (third + 1) * width] = made
    bias = jnp.where(keep_ref[...] > 0.0, 0.0, MASKED)
    lane = iota((toks, LANES), 1)
    logs = jnp.zeros((toks, LANES), F32)
    for at in range(0, width, LANES):
        queries = qkv_ref[0:toks, at : at + LANES]
        keys = qkv_ref[:, width + at : width + at + LANES]
        values = qkv_ref[:, 2 * width + at : 2 * width + at + LANES]
        made = []
        for head in range(2):
            score = dot_nt(of_head(queries, head), keys) + bias
            top = jnp.max(score, axis=-1, keepdims=True)
            grown = jnp.exp(score - top)
            total = jnp.sum(grown, axis=-1, keepdims=True)
            made.append(dot_nn(grown.astype(BF16), values) * (1.0 / total))
            logs = jnp.where(lane == 2 * (at // LANES) + head, top + jnp.log(total), logs)
        attended_ref[:, at : at + LANES] = by_head(*made)
    lse_col_ref[...] = logs
    lse_row_ref[...] = jnp.transpose(lse_col_ref[...])[:8, :]
    branch = dot_nn(attended_ref[...].astype(BF16), w_ref[3 * width : 4 * width, :])
    residual = own_ref[...].astype(F32) + branch
    residual_ref[...] = residual
    mixed = (normalize(residual)[0] * gain_two).astype(BF16)
    mixed_ref[...] = mixed
    logits = dot_nt(mixed, w_ref[router : router + n_exp, :])
    prob_ref[...] = jax.nn.softmax(logits, axis=-1)
    slots = sent_ref.shape[0]
    spots = iota((slots, toks), 0)
    picks = as_bf16((spots == pos_ref[0:1, :]) | (spots == pos_ref[1:2, :]))
    sent_ref[...] = dot_nn(picks, mixed).astype(BF16)


def gelu_parts(value):
    below = 0.5 + 0.5 * lax.erf(value * 0.7071067811865476)
    return value * below, below + value * jnp.exp(-0.5 * value * value) * 0.3989422804014327


def expert_body(
    n_exp, expert_ref, got_ref, cot_ref, near_ref, far_in_ref, far_out_ref, router_ref,
    active_ref, hidden_ref, scaled_ref, result_ref, back_ref, router_grad_ref,
):
    @pl.when(pl.program_id(0) == 0)
    def _():
        router_grad_ref[...] = jnp.zeros_like(router_grad_ref)

    expert = expert_ref[0]
    got, cot = got_ref[...], cot_ref[...]
    labels = iota((got.shape[0], n_exp), 1)
    share = jax.nn.softmax(dot_nt(got, router_ref[...]), axis=-1)
    gate = jnp.sum(jnp.where(labels == expert, share, 0.0), axis=-1, keepdims=True)
    scaled = (cot.astype(F32) * gate).astype(BF16)
    scaled_ref[...] = scaled
    half = near_ref.shape[0] // 2
    total = total_back = 0.0
    halves = ((near_ref[:half, :], near_ref[half:, :]), (far_in_ref[...], far_out_ref[...]))
    for number, (w_in, w_out) in enumerate(halves):
        at = slice(number * half, (number + 1) * half)
        active, slope = gelu_parts(dot_nt(got, w_in))
        low = active.astype(BF16)
        active_ref[:, at] = low
        grad = (dot_nt(scaled, w_out) * slope).astype(BF16)
        hidden_ref[:, at] = grad
        total = total + dot_nn(low, w_out)
        total_back = total_back + dot_nn(grad, w_in)
    result = total.astype(BF16)
    result_ref[...] = result
    inner = jnp.sum(result.astype(F32) * cot.astype(F32), axis=-1, keepdims=True)
    grad = share * (jnp.where(labels == expert, inner, 0.0) - gate * inner)
    low = grad.astype(BF16)
    back_ref[...] = (total_back + dot_nn(low, router_ref[...])).astype(BF16)
    router_grad_ref[...] += dot_tn(low, got)


def weight_grad_body(hidden_ref, active_ref, got_ref, scaled_ref, *outs):
    size = outs[0].shape[0]
    for number, out in enumerate(outs):
        left, right = ((hidden_ref, got_ref), (active_ref, scaled_ref))[number % 2]
        at = slice((1 - number // 2) * size, (2 - number // 2) * size)
        out[...] = dot_tn(left[:, at], right[...]).astype(out.dtype)


def norm_back(hat, scale, gain, grad):
    inner = grad * gain
    first = jnp.mean(inner, axis=-1, keepdims=True)
    second = jnp.mean(inner * hat, axis=-1, keepdims=True)
    return (inner - first - hat * second) * scale


def middle_body(
    back_ref, pos_ref, residual_ref, cot_ref, keep_ref, attended_ref, w_ref, gains_ref,
    grad_ref, out_grad_ref, delta_col_ref, delta_row_ref, gain_ref,
):
    toks, width = residual_ref.shape
    slots = back_ref.shape[0]
    gain_two = gains_ref[...].astype(F32)[1:2, :]
    spots = iota((toks, slots), 1)
    picks = as_bf16((spots == pos_ref[:, 0:1]) | (spots == pos_ref[:, 1:2]))
    grad_mixed = dot_nn(picks, back_ref[...])
    hat, scale = normalize(residual_ref[...])
    gain_ref[...] = jnp.broadcast_to(
        jnp.sum(grad_mixed * hat, axis=0, keepdims=True), gain_ref.shape
    )
    grad_rows = cot_ref[...].astype(F32) * keep_ref[...]
    grad = grad_rows + norm_back(hat, scale, gain_two, grad_mixed)
    grad_ref[...] = grad
    low = grad.astype(BF16)
    out_grad = dot_nt(low, w_ref[...]).astype(BF16)
    out_grad_ref[...] = out_grad
    product = out_grad.astype(F32) * attended_ref[...]
    delta = jnp.zeros((toks, LANES), F32)
    lane = iota((toks, LANES), 1)
    for head in range(HEADS):
        at = (head // 2) * LANES
        part = jnp.where(head_lanes(head % 2, toks), product[:, at : at + LANES], 0.0)
        delta = jnp.where(lane == head, jnp.sum(part, axis=-1, keepdims=True), delta)
    delta_col_ref[...] = delta
    delta_row_ref[...] = jnp.transpose(delta)[:8, :]


def inner_body(
    n_exp, qkv_ref, out_grad_ref, lse_ref, delta_ref, keep_ref, attended_ref, grad_ref, router_grad_ref, gain_ref,
    query_ref, kv_ref, early_ref,
):
    toks, width = out_grad_ref.shape
    bias = jnp.where(keep_ref[...] > 0.0, 0.0, MASKED)
    for at in range(0, width, LANES):
        queries = qkv_ref[0:toks, at : at + LANES]
        keys = qkv_ref[:, width + at : width + at + LANES]
        values = qkv_ref[:, 2 * width + at : 2 * width + at + LANES]
        out_grad = out_grad_ref[:, at : at + LANES]
        made = []
        for head in range(2):
            line = 2 * (at // LANES) + head
            score = dot_nt(of_head(queries, head), keys) + bias
            prob = jnp.exp(score - lse_ref[:, line : line + 1])
            slope = dot_nt(of_head(out_grad, head), values)
            grad = (prob * (slope - delta_ref[:, line : line + 1])).astype(BF16)
            made.append(
                (dot_nn(grad, keys), dot_tn(grad[:, :toks], queries), dot_tn(prob[:, :toks].astype(BF16), out_grad))
            )
        query_ref[:, at : at + LANES] = (by_head(made[0][0], made[1][0]) * HEAD_DIM ** (-0.5)).astype(BF16)
        kv_ref[0, :, at : at + LANES] = by_head(made[0][1], made[1][1])
        kv_ref[1, :, at : at + LANES] = by_head(made[0][2], made[1][2])
    early_ref[0:width, :] = dot_tn(attended_ref[...].astype(BF16), grad_ref[...].astype(BF16)).astype(BF16)
    early_ref[width : width + n_exp, :] = router_grad_ref[...].astype(BF16)
    row_id = iota((16, width), 0)
    early_ref[width + n_exp : width + n_exp + 16, :] = jnp.where(
        row_id == 0, gain_ref[0:1, :], 0.0
    ).astype(BF16)


def outer_body(
    n_exp, qkv_ref, out_grad_ref, sums_ref, keep_ref, query_ref, kv_ref, normed_ref, own_ref, w_ref, early_ref,
    query_rows_ref, key_rows_ref, value_rows_ref, rest_ref, grad_normed_ref, held,
):
    toks, width = query_ref.shape
    held[:, 0:width] = query_ref[...]
    bias = jnp.where(keep_ref[...] > 0.0, 0.0, MASKED)
    for at in range(0, width, LANES):
        queries = qkv_ref[toks : 2 * toks, at : at + LANES]
        out_grad = out_grad_ref[:, at : at + LANES]
        keys = qkv_ref[0:toks, width + at : width + at + LANES]
        values = qkv_ref[0:toks, 2 * width + at : 2 * width + at + LANES]
        made = []
        for head in range(2):
            line = 2 * (at // LANES) + head
            score = dot_nt(of_head(keys, head), queries) + bias
            prob = jnp.exp(score - sums_ref[line : line + 1, :])
            slope = dot_nt(of_head(values, head), out_grad)
            grad = (prob * (slope - sums_ref[HEADS + line : HEADS + line + 1, :])).astype(BF16)
            made.append((dot_nn(grad, queries), dot_nn(prob.astype(BF16), out_grad)))
        for number in range(2):
            total = kv_ref[number, :, at : at + LANES] + by_head(made[0][number], made[1][number])
            held[:, (number + 1) * width + at : (number + 1) * width + at + LANES] = total.astype(BF16)
    for third, ref in enumerate((query_rows_ref, key_rows_ref, value_rows_ref)):
        ref[...] = dot_tn(held[:, third * width : (third + 1) * width], normed_ref[...]).astype(BF16)
    grad_normed = dot_nn(held[...], w_ref[0 : 3 * width, :])
    grad_normed_ref[...] = grad_normed
    gain_grad = jnp.sum(grad_normed * normalize(own_ref[...].astype(F32))[0], axis=0, keepdims=True)
    rest_ref[0:16, :] = jnp.where(
        iota((16, width), 0) == 0, gain_grad, 0.0
    ).astype(BF16)
    rest_ref[16:, :] = early_ref[...]


def step_body(keep_a, got_a, keep_b, got_b, go_a, go_b, stay_a, stay_b):
    half = go_a.shape[0]
    for keep, got, go, stay in ((keep_a, got_a, go_a, stay_a), (keep_b, got_b, go_b, stay_b)):
        go[...] = total_f32(keep[half:, :], got[half:, :]).astype(BF16)
        stay[...] = total_f32(keep[:half, :], got[:half, :]).astype(BF16)


def tokens_body(n_exp, grad_normed_ref, own_ref, w_ref, grad_ref, out_ref):
    at = 4 * own_ref.shape[1] + n_exp
    gain_one = w_ref[at : at + 16, :].astype(F32)[0:1, :]
    hat, scale = normalize(own_ref[...].astype(F32))
    out_ref[...] = grad_ref[...] + norm_back(hat, scale, gain_one, grad_normed_ref[...])


def spread_body(starts, n_in, pos_ref, *refs):
    mine, far, outs, held = refs[:n_in], refs[n_in : 2 * n_in], refs[2 * n_in : -1], refs[-1]
    at = 0
    for one, two in zip(mine, far):
        held[at : at + one.shape[0], :] = total_f32(one[...], two[...]).astype(BF16)
        at += one.shape[0]
    size = outs[0].shape[0]
    for number, start in enumerate(starts):
        picks = as_bf16(iota((size, held.shape[0]), 0) + start == pos_ref[...])
        outs[number][...] = dot_nn(picks, held[...]).astype(BF16)


def room_of(owned, n_dev):
    return min(owned, -(-(owned // n_dev * 5 // 4) // 16) * 16)


def sent_at(partner):
    return ((partner >> 2) & 1) * 4 + (partner & 1) * 2 + ((partner >> 1) & 1)


def got_at(partner):
    return ((partner >> 1) & 1) * 4 + ((partner >> 2) & 1) * 2 + (partner & 1)


def sent_cell(cell):
    return (cell >> 2) * 4 + (cell & 1) * 2 + ((cell >> 1) & 1)


def plan_body(n_dev, room, me_ref, owner_ref, row_ref, col_ref, most_ref):
    me = me_ref[0]
    owned = owner_ref.shape[1]
    source = owner_ref[...] >> (owned.bit_length() - 1)
    spot = owner_ref[...] & (owned - 1)
    total = n_dev * n_dev
    classes = iota((n_dev, owned), 0)
    member = jnp.concatenate([classes == source[t : t + 1, :] for t in range(n_dev)], axis=0)
    ones = as_bf16(member)
    step = 256
    before = as_bf16(iota((step, step), 0) < iota((step, step), 1))
    count = jnp.zeros((total, 1), F32)
    ranks = []
    for at in range(0, owned, step):
        part = ones[:, at : at + step]
        ranks.append(dot_nn(part, before) + count)
        count = count + jnp.sum(part.astype(F32), axis=1, keepdims=True)
    most_ref[...] = jnp.broadcast_to(jnp.max(count, axis=0, keepdims=True).astype(I32), most_ref.shape)
    line = iota((total, 1), 0)
    to, of = line // n_dev, line % n_dev
    rank = jnp.concatenate(ranks, axis=1)
    turn = ((rank + 0.5) * (1.0 / room)).astype(I32)
    inside = rank.astype(I32) + turn * ((n_dev - 1) * room)
    wanted = member & (to == me)
    arrives = jnp.sum(jnp.where(wanted, inside + got_at(of ^ to) * room, 0), axis=0, keepdims=True)
    returns = jnp.sum(jnp.where(wanted, inside + sent_at(of ^ to) * room, 0), axis=0, keepdims=True)
    leaves = inside + sent_at(of ^ to) * room
    half = owned // LANES
    found = jnp.zeros((2 * half, LANES), F32)
    high, lanes = iota((half, owned), 0), iota((LANES, owned), 0)
    for t in range(n_dev):
        mine = slice(t * n_dev, (t + 1) * n_dev)
        chosen = member[mine] & (of[mine] == me)
        place = jnp.sum(jnp.where(chosen, leaves[mine], 0), axis=0, keepdims=True)
        hit = (spot[t : t + 1, :] // LANES == high) & (source[t : t + 1, :] == me)
        left = jnp.concatenate(
            [jnp.where(hit, place // LANES, 0), jnp.where(hit, place % LANES, 0)], axis=0
        ).astype(F32).astype(BF16)
        found = found + dot_nt(left, as_bf16((spot[t : t + 1, :] % LANES) == lanes))
    found = found[:half] * float(LANES) + found[half:]
    leave_row = jnp.concatenate([found[a : a + 1, :] for a in range(half)], axis=1)
    block = ((leave_row + 0.5) * (1.0 / room)).astype(I32)
    round_no, cell = block // n_dev, block % n_dev
    comes = leave_row.astype(I32) + (round_no * n_dev + got_at(sent_cell(cell)) - block) * room
    rows = jnp.concatenate(
        [leave_row, arrives.astype(F32), returns.astype(F32), comes.astype(F32), jnp.zeros((4, owned), F32)], axis=0
    )
    row_ref[...] = rows.astype(I32)
    col_ref[...] = jnp.transpose(rows).astype(I32)


LEAVES, ARRIVES, RETURNS, COMES = range(4)


def put_rows(line, base_ref, pos_ref, held, outs, tile):
    wanted = pos_ref[line : line + 1, :] - base_ref[0]
    base = 0
    for out in outs:
        for at in range(0, out.shape[0], tile):
            picks = as_bf16(iota((tile, held.shape[0]), 0) + (base + at) == wanted)
            out[at : at + tile, :] = dot_nn(picks, held[...]).astype(BF16)
        base += out.shape[0]


def put_body(line, tile, base_ref, pos_ref, rows_ref, *outs):
    put_rows(line, base_ref, pos_ref, rows_ref, outs, tile)


def sum_put_body(line, tile, cells, n_in, base_ref, pos_ref, *refs):
    mine, theirs, outs, held = refs[:n_in], refs[n_in : 2 * n_in], refs[2 * n_in : -1], refs[-1]
    size = mine[0].shape[0]
    for number in range(n_in):
        held[number * size : (number + 1) * size, :] = total_f32(mine[number][...], theirs[number][...]).astype(BF16)
    wanted = pos_ref[line : line + 1, :] - base_ref[0]
    for cell, out in zip(cells, outs):
        for at in range(0, out.shape[0], tile):
            picks = as_bf16(iota((tile, held.shape[0]), 0) + (cell * out.shape[0] + at) == wanted)
            out[at : at + tile, :] = dot_nn(picks, held[...]).astype(BF16)


def take_body(line, tile, base_ref, pos_ref, *refs):
    pieces, out, held = refs[:-2], refs[-2], refs[-1]
    gather_halves(pieces, held)
    for at in range(0, out.shape[0], tile):
        wanted = pos_ref[at : at + tile, line : line + 1] - base_ref[0]
        picks = as_bf16(iota((tile, held.shape[0]), 1) == wanted)
        out[at : at + tile, :] = dot_nn(picks, held[...]).astype(BF16)


def adam_body(n_in, pos_ref, *refs):
    pieces, (first_ref, second_ref, weight_ref) = refs[:n_in], refs[n_in : n_in + 3]
    grad_ref, first_new, second_new, weight_new, held = refs[n_in + 3 :]

    @pl.when(pl.program_id(0) == 0)
    def _():
        gather_halves(pieces, held)

    picks = as_bf16(iota((grad_ref.shape[0], held.shape[0]), 1) == pos_ref[:, COMES : COMES + 1])
    grad = dot_nn(picks, held[...])
    grad_ref[...] = grad
    made = adam_update(grad, first_ref[...], second_ref[...], weight_ref[...].astype(F32))
    first_new[...], second_new[...], weight_new[...] = made


def mixture_body(result_ref, pos_ref, ids_ref, prob_ref, residual_ref, out_ref):
    toks = residual_ref.shape[0]
    slots = result_ref.shape[0]
    share = prob_ref[...]
    total = residual_ref[...]
    picks = [as_bf16(iota((toks, slots), 1) == pos_ref[:, number : number + 1]) for number in range(2)]
    picked = dot_nn(jnp.concatenate(picks, axis=0), result_ref[...])
    for number in range(2):
        mine = iota(share.shape, 1) == ids_ref[:, number : number + 1]
        gate = jnp.sum(jnp.where(mine, share, 0.0), axis=-1, keepdims=True)
        total = total + gate * picked[number * toks : (number + 1) * toks, :]
    out_ref[...] = total.astype(BF16)


SWAP = [(0, 1), (1, 0)]
SWAP_CORE = [(0, 1), (1, 0), (2, 3), (3, 2)]
SWAP_Y = [(0, 2), (2, 0), (1, 3), (3, 1)]


def swap_x(value):
    return lax.ppermute(value, "ctx", SWAP)


def swap_y(value):
    return lax.ppermute(value, "dp", SWAP_Y)


def swap_x_y(value):
    return lax.ppermute(value, ("dp", "ctx"), [(i, i ^ 5) for i in range(8)])


def swap_core(value):
    return lax.ppermute(value, "dp", SWAP_CORE)


def shift_z(value, by):
    count = lax.axis_size("expert")
    return lax.ppermute(value, "expert", [(i, (i + by) % count) for i in range(count)])


def after(values, *others):
    values = list(values)
    return lax.optimization_barrier((*values, *others))[: len(values)]


def total_f32(first, second):
    return first.astype(F32) + second.astype(F32)


def on_chip_experts(
    tokens, cotangent, pad_mask, expert_ids, slot_priority, shared_slots, shared_first, shared_second,
    shared_owner, expert_slots, expert_first, expert_second, expert_owner,
):
    toks, width = tokens.shape[1], tokens.shape[2]
    n_z = lax.axis_size("expert")
    n_exp = EXP_DEV * n_z
    capacity = (10 * toks + 4 * n_exp - 1) // (4 * n_exp)
    slots = n_exp * capacity
    everyone = ("dp", "ctx", "expert")
    dp, mx, mz = lax.axis_index("dp"), lax.axis_index("ctx"), lax.axis_index("expert")
    my, mc = dp // 2, dp % 2

    own_count = shared_slots.shape[0]
    stride = -(-own_count // 8) * 8
    padded = jnp.pad(shared_slots, ((0, stride - own_count), (0, 0)))
    line = [padded] + [shift_z(padded, by) for by in range(1, n_z)]
    part_a = jnp.concatenate(line[: n_z // 2], axis=0)
    part_b = jnp.concatenate(line[n_z // 2 :], axis=0)
    a_y, b_x = swap_y(part_a), swap_x(part_b)
    pair_a, pair_b = jnp.concatenate([part_a, a_y], axis=0), jnp.concatenate([part_b, b_x], axis=0)
    first_near, last_near = [pair_a, pair_b], [swap_x(pair_a), swap_y(pair_b)]
    first_far = [swap_core(piece) for piece in first_near]

    owner_dev, owner_row = shared_owner // own_count, shared_owner % own_count
    o_z, o_x, o_dp = owner_dev % n_z, owner_dev // n_z % 2, owner_dev // (n_z * 2)
    in_c, in_y, in_x = (o_dp % 2) ^ mc, (o_dp // 2) ^ my, o_x ^ mx
    in_z = (mz - o_z + n_z) % n_z
    late = in_z // (n_z // 2)
    cross = jnp.where(late == 0, in_y + 2 * in_x, in_x + 2 * in_y)
    place = (((in_c * 2 + late) * 4 + cross) * (n_z // 2) + in_z % (n_z // 2)) * stride + owner_row
    total_slots = 8 * n_z * stride
    row_count = -(-shared_owner.shape[0] // 16) * 16
    place_col = jnp.pad(place, (0, row_count - place.shape[0]), constant_values=-1)[:, None]
    gain_at = 4 * width + n_exp
    none = jnp.full((15,), -1, I32)
    place_row = jnp.concatenate(
        [place[: 3 * width], place[gain_at : gain_at + 1], none, place[3 * width : gain_at], place[gain_at + 1 :], none]
    )[None, :]

    half_slots = total_slots // 2
    piece = half_slots // 4
    row_tile = row_count // 2 if row_count % 32 == 0 else row_count

    def unpack(spots, pieces, earlier):
        rows_of = lambda columns: pl.BlockSpec((row_tile, columns), lambda i: (i, 0))
        return kernel_call(
            functools.partial(unpack_body, spots, len(earlier)), sds((row_count, width), BF16),
            [pltpu.VMEM((len(pieces) * piece, width), BF16)],
            grid=(row_count // row_tile,),
            in_specs=[rows_of(1)] + [pl.BlockSpec((piece, width), lambda i: (0, 0))] * len(pieces)
            + [rows_of(width)] * len(earlier),
            out_specs=rows_of(width),
            cost=(7 * MICRO, 1e6),
        )(place_col, *pieces, *earlier)

    first_rows = unpack(
        [0, 2 * piece, half_slots, half_slots + 2 * piece], [*first_near, *first_far], []
    )
    last_near = after(last_near, first_rows)
    last_far = [swap_core(piece) for piece in last_near]

    own, other = tokens[0], swap_x(tokens[0])
    ids = expert_ids[0]
    live = pad_mask.astype(F32)
    live_other = swap_x(pad_mask).astype(F32)
    keep_row = jnp.concatenate([live, live_other], axis=1)
    keep_col = live.reshape(toks, 1)
    pos_row, pos_col, cot_sent = kernel_call(
        functools.partial(route_body, n_exp, capacity),
        (sds((8, toks), I32), sds((toks, 8), I32), sds((slots, width), BF16)),
        cost=(4 * MICRO, 1e6),
    )(*after([ids.T], other), slot_priority.astype(F32), live, cotangent[0])

    def exchange(rows):
        return lax.all_to_all(rows, everyone, split_axis=0, concat_axis=0, tiled=True)

    cot_got = exchange(after([cot_sent], a_y, b_x)[0])

    local = my * 2 + mx
    group, n_dev = dp * 2 + mx, 8
    owned = expert_slots.shape[1]
    room = room_of(owned, n_dev)
    owner = jnp.transpose(
        expert_owner[0].reshape(2, 2, 2, 2, FF // 2), (0, 3, 1, 2, 4)
    ).reshape(n_dev, owned)
    held = [pltpu.VMEM((n_dev * room, width), BF16)]
    sent_shapes = [sds((2 * room, width), BF16)] * 4
    smem, vmem = pl.BlockSpec(memory_space=pltpu.SMEM), pl.BlockSpec(memory_space=pltpu.VMEM)
    plan_row, plan_col, most = kernel_call(
        functools.partial(plan_body, n_dev, room),
        (sds((8, owned), I32), sds((owned, 8), I32), sds((8, LANES), I32)), cost=(5 * MICRO, 1e6),
        in_specs=[smem, vmem],
    )(group.astype(I32).reshape(1), *after([owner], part_a, part_b, pos_row, other))
    rounds = (most[0, 0] + room - 1) // room
    def with_base(body, out_shape, scratch, arrays, number=0, cost=QUICK):
        base = jnp.full((1,), number * n_dev * room, I32)
        return kernel_call(
            body, out_shape, scratch, in_specs=[smem] + [vmem] * len(arrays), cost=cost
        )(base, *arrays)

    def over_links(pieces, *others):
        last = after(pieces[3:], *others)[0] if others else pieces[3]
        return [pieces[0], swap_x(pieces[1]), swap_y(pieces[2]), swap_x_y(last)]

    def over_cores(got):
        far = [jnp.concatenate([got[at][room:], got[at + 1][room:]], axis=0) for at in (0, 2)]
        return [*got, swap_core(far[0]), swap_core(far[1])]

    put_leaving = functools.partial(put_body, LEAVES, room)
    take_tile = 256 if owned % 256 == 0 else owned
    take_arrived = functools.partial(take_body, ARRIVES, take_tile)
    leaving = with_base(
        put_leaving, sent_shapes, (), [*after([plan_row], a_y, b_x), expert_slots[0]], 0, (8 * MICRO, 1e6)
    )
    moved = over_links(after(leaving, *last_near))

    weights = unpack(
        [piece, 3 * piece, half_slots + piece, half_slots + 3 * piece], [*last_near, *last_far], [first_rows]
    )

    (qkv, normed, attended, residual, prob, sent, lse_col, lse_row) = kernel_call(
        functools.partial(forward_body, n_exp),
        (
            sds((2 * toks, 3 * width), BF16), sds((toks, width), BF16), sds((toks, width), F32),
            sds((toks, width), F32), sds((toks, n_exp), F32), sds((slots, width), BF16),
            sds((toks, LANES), F32), sds((8, toks), F32),
        ),
        [pltpu.VMEM((toks, width), BF16)],
        cost=(13 * MICRO, 1e6),
    )(*after([own], cot_got), other, keep_row, weights, pos_row)
    got = exchange(sent)
    moved = over_cores(after(moved, sent))
    near_weights = with_base(take_arrived, sds((owned, width), BF16), held, [plan_col, *moved])
    far_weights = [swap_core(near_weights[: FF // 2]), swap_core(near_weights[FF // 2 :])]

    def more_weights(number, totals):
        leaving = with_base(put_leaving, sent_shapes, (), [plan_row, expert_slots[0]], number)
        moved = over_cores(over_links(leaving))
        part = with_base(take_arrived, sds((owned, width), BF16), held, [plan_col, *moved], number)
        there = swap_core(part)
        return totals[0] + part, totals[1] + there[: FF // 2], totals[2] + there[FF // 2 :]

    got, *expert_weights = after([got, near_weights, *far_weights])
    near_weights, *far_weights = lax.fori_loop(1, rounds, more_weights, tuple(expert_weights))

    expert_id = (mz * EXP_DEV + local).astype(I32).reshape(1)
    tile = 256 if slots % 256 == 0 else slots
    router_rows = weights[4 * width : 4 * width + n_exp]
    whole = lambda shape: pl.BlockSpec(shape, lambda i: (0, 0))
    rows_of = lambda columns: pl.BlockSpec((tile, columns), lambda i: (i, 0))
    active, hidden, scaled, result, back, router_grad = kernel_call(
        functools.partial(expert_body, n_exp),
        (
            sds((slots, FF), BF16), sds((slots, FF), BF16), sds((slots, width), BF16),
            sds((slots, width), BF16), sds((slots, width), BF16), sds((n_exp, width), F32),
        ),
        grid=(slots // tile,),
        in_specs=[
            pl.BlockSpec(memory_space=pltpu.SMEM), rows_of(width), rows_of(width),
            whole((FF, width)), whole((FF // 2, width)), whole((FF // 2, width)), whole((n_exp, width)),
        ],
        out_specs=(
            rows_of(FF), rows_of(FF), rows_of(width), rows_of(width), rows_of(width), whole((n_exp, width)),
        ),
        cost=(19 * MICRO, 1e6),
    )(expert_id, got, cot_got, near_weights, *far_weights, router_rows)
    back_got = exchange(back)

    halves = [sds((FF // 2, width), BF16)] * 2 + [sds((FF // 2, width), F32)] * 2
    *theirs, mine_in, mine_out = kernel_call(weight_grad_body, halves, cost=(10 * MICRO, 1e6))(
        hidden, active, got, scaled
    )
    theirs_got, mine = [swap_core(part) for part in theirs], (mine_in, mine_out)
    held_owned = [pltpu.VMEM((owned, width), BF16)]

    def returning(cells, number=0):
        body = functools.partial(sum_put_body, RETURNS, room, cells, 2)
        return with_base(body, [sent_shapes[0]] * len(cells), held_owned, [plan_row, *mine, *theirs_got], number, (4 * MICRO, 1e6))

    moved_x, moved_xy = returning((1, 3))
    moved_0, moved_y = returning((0, 2))
    moved = [moved_0, moved_x, moved_y, moved_xy]
    back_got = after([back_got], *moved)[0]

    grad_residual, out_grad, delta_col, delta_row, gain_two = kernel_call(
        middle_body,
        (
            sds((toks, width), F32), sds((toks, width), BF16), sds((toks, LANES), F32),
            sds((8, toks), F32), sds((8, width), F32),
        ),
        cost=(6 * MICRO, 1e6),
        grid=(1,),
        in_specs=[vmem] * 6
        + [pl.BlockSpec((width, width), lambda i: (3, 0)), pl.BlockSpec((16, width), lambda i: (gain_at // 16, 0))],
        out_specs=[vmem] * 5,
    )(back_got, pos_col, residual, cotangent[0], keep_col, attended, weights, weights)
    out_grad_other = swap_x(out_grad)
    sums_other = swap_x(jnp.concatenate([lse_row, delta_row], axis=0))
    query_grad, kv_grad, early = kernel_call(
        functools.partial(inner_body, n_exp),
        (sds((toks, width), BF16), sds((2, toks, width), F32), sds((width + n_exp + 16, width), BF16)),
        cost=(15 * MICRO, 1e6),
    )(qkv, out_grad, lse_col, delta_col, keep_row, attended, grad_residual, router_grad, gain_two)
    moved = over_links(moved, out_grad_other, query_grad, sums_other)
    result_got = exchange(after([result], query_grad)[0])
    *late, grad_normed = kernel_call(
        functools.partial(outer_body, n_exp),
        [sds((rows, width), BF16) for rows in (width, width, width, place_row.shape[1] - 3 * width)]
        + [sds((toks, width), F32)],
        [pltpu.VMEM((toks, 3 * width), BF16)],
        cost=QUICK,
    )(
        qkv, *after([out_grad_other], *moved[1:3]), sums_other, keep_col, query_grad, kv_grad, normed, own, weights, early,
    )
    late_far = [swap_core(part) for part in late]
    quarter = half_slots // 2
    eighth, sixteenth = quarter // 2, quarter // 4
    count = place_row.shape[1]

    def spread(starts, *others):
        return kernel_call(
            functools.partial(spread_body, starts, len(late)), [sds((eighth, width), BF16)] * 2,
            [pltpu.VMEM((count, width), BF16)], cost=QUICK,
        )(*after([place_row], *others), *late, *late_far)

    sends = spread((eighth, quarter + eighth), moved[3])
    got_a, got_b = swap_x(sends[0]), swap_y(sends[1])
    keeps = spread((0, quarter), *sends)
    grad_tokens = kernel_call(
        functools.partial(tokens_body, n_exp), sds((toks, width), F32), cost=QUICK
    )(*after([grad_normed], *sends), own, weights, grad_residual)

    got_a, got_b = after([got_a, got_b], grad_tokens)
    go_a, go_b, sum_a, sum_b = kernel_call(
        step_body, [sds((sixteenth, width), BF16)] * 4, cost=QUICK
    )(keeps[0], got_a, keeps[1], got_b)
    got_a, got_b = swap_y(go_a), swap_x(go_b)
    moved = over_cores(after(moved, go_a))
    sum_a = total_f32(sum_a, got_a).astype(BF16)
    sum_b = total_f32(sum_b, got_b).astype(BF16)
    lines = [sum_a[i * stride : (i + 1) * stride] for i in range(n_z // 2)]
    lines += [sum_b[i * stride : (i + 1) * stride] for i in range(n_z // 2)]
    output = kernel_call(
        mixture_body, sds((toks, width), BF16), cost=QUICK
    )(*after([result_got], *lines), pos_col, ids, prob, residual)
    tile = 512 if owned % 512 == 0 else owned
    rows_of = lambda columns: pl.BlockSpec((tile, columns), lambda i: (i, 0))
    expert_new = kernel_call(
        functools.partial(adam_body, len(moved)), [sds((owned, width), F32)] * 4, held,
        grid=(owned // tile,),
        in_specs=[rows_of(8)] + [pl.BlockSpec(piece.shape, lambda i: (0, 0)) for piece in moved] + [rows_of(width)] * 3,
        out_specs=[rows_of(width)] * 4,
        cost=QUICK,
    )(*after([plan_col], output), *moved, expert_first[0], expert_second[0], expert_slots[0])
    shared_grad = lines[0].astype(F32)
    for by in range(1, n_z):
        came = after([shift_z(lines[by], n_z - by)], expert_new[0])[0]
        shared_grad = shared_grad + came.astype(F32)
    shared_grad = shared_grad[:own_count]


    def more_grads(number, made):
        parts = returning(range(4), number)
        parts = over_cores(over_links(parts))
        take = functools.partial(take_body, COMES, take_tile)
        part = with_base(take, sds((owned, width), BF16), held, [plan_col, *parts], number)
        grad = made[0] + part.astype(F32)
        return (grad, *adam_update(grad, expert_first[0], expert_second[0], expert_slots[0].astype(F32)))

    shared_grad, *expert_new = after([shared_grad, *expert_new], output)
    expert_new = lax.fori_loop(1, rounds, more_grads, tuple(expert_new))
    shared_new = adam_update(shared_grad, shared_first, shared_second, shared_slots.astype(F32))
    return (
        output[None], grad_tokens[None], shared_grad, *shared_new,
        *(value[None] for value in expert_new),
    )


def solution(mesh):
    sizes = mesh.shape
    chip_experts = (sizes["dp"], sizes["ctx"], sizes["expert"]) == (4, 2, 4)
    return jax.shard_map(
        on_chip_experts if chip_experts else on_device,
        mesh=mesh,
        in_specs=(
            P(("dp", "expert"), "ctx", None),
            P(("dp", "expert"), "ctx", None),
            P(("dp", "expert"), "ctx"),
            P(("dp", "expert"), "ctx", None),
            P(("dp", "expert"), "ctx"),
            P(("dp", "ctx", "expert"), None),
            P(("dp", "ctx", "expert"), None),
            P(("dp", "ctx", "expert"), None),
            P(),
            P("expert", ("dp", "ctx"), None),
            P("expert", ("dp", "ctx"), None),
            P("expert", ("dp", "ctx"), None),
            P("expert", None),
        ),
        out_specs=(
            P(("dp", "expert"), "ctx", None),
            P(("dp", "expert"), "ctx", None),
            P(("dp", "ctx", "expert"), None),
            P(("dp", "ctx", "expert"), None),
            P(("dp", "ctx", "expert"), None),
            P(("dp", "ctx", "expert"), None),
            P("expert", ("dp", "ctx"), None),
            P("expert", ("dp", "ctx"), None),
            P("expert", ("dp", "ctx"), None),
            P("expert", ("dp", "ctx"), None),
        ),
        check_vma=False,
    )
```
